256 devices in a mesh: dp: 4 (over z_hi, core), ctx: 16 (over z_lo, y), tp: 4 (over x).
Axes of the slice: x: 4, y: 4, z: 8 (z_hi: 2, z_lo: 4; z = z_hi * 4 + z_lo), core: 2. Of those that a mesh axis runs over, the one named last changes fastest.
Arguments:
- hidden_in: bfloat16 [4, 3584, 8192], P('dp', 'ctx', 'tp'), may hold values from -6 to 6
- queries: bfloat16 [4, 3584, 4096], P('dp', 'ctx', 'tp'), may hold values from -6 to 6
- keys_in: bfloat16 [4, 3584, 512], P('dp', 'ctx', 'tp'), may hold values from -6 to 6
- values_in: bfloat16 [4, 3584, 512], P('dp', 'ctx', 'tp'), may hold values from -6 to 6
- out_grad: bfloat16 [4, 3584, 4096], P('dp', 'ctx', 'tp'), may hold values from -6 to 6
- doc_lengths: int32 [4, 6], P('dp'), may hold values from 1 to 1194, 3584 in all within a row
- pair_perm: int32 [16], replicated, may hold values from 0 to 15, each once
Outputs:
- grad_queries: bfloat16 [4, 3584, 4096], P('dp', 'ctx', 'tp')
- grad_keys: bfloat16 [4, 3584, 512], P('dp', 'ctx', 'tp')
- grad_values: bfloat16 [4, 3584, 512], P('dp', 'ctx', 'tp')
- grad_kv_weight: float32 [1024, 8192], P(('dp', 'ctx'), 'tp')
The draws below stay inside these ranges and needn't reach their ends.
Inputs may be any that keep to these rules, and one draw needn't show every extreme that they name: `doc_lengths`: each row is a permutation of the documents' lengths summing to 3584, the largest exactly 1194. `pair_perm`: a permutation of the indices of ctx.
All inputs are finite; a program needn't handle non-finite values.
Results may differ from the reference program's by a relative error of at most 0.019.
Values may be sent and summed in bfloat16 or wider, within the bound.
No kernel may reach another device: no remote copies, remote signals or barrier semaphores. Data moves between devices by JAX's collectives and lax.ppermute only.
A program may use at most 64 MiB of HBM per device.

```python
import math
import jax
import jax.numpy as jnp
import numpy as np
from jax import lax

D = 8192
QH = 32
KVH = 4
DH = 128
STRETCH = 112
NDOCS = 6
SEQ = 3584
BATCH = 4
N_CTX = 16


def block_levels(stream_key, dims, split, low, high):
    loudness, own = 1.0, jax.random.fold_in(stream_key, 6)
    for position, parts in split:
        draws = jnp.exp(jax.random.uniform(jax.random.fold_in(own, position), (parts,), jnp.float32, low / len(split), high / len(split)))
        loudness = loudness * jnp.repeat(draws, dims[position] // parts).reshape([-1 if axis == position else 1 for axis in range(len(dims))])
    return loudness


def split_up(number_of, total, most, skew):
    portions = [(1 << 20) // math.isqrt(rank ** skew) + 1 for rank in range(2, number_of + 1)]
    rest, holding = total - most - (number_of - 1), [1] * (number_of - 1)
    while rest > 0:
        candidates = [i for i in range(number_of - 1) if holding[i] < most]
        whole, left = sum([portions[i] for i in candidates]), rest
        for i in candidates:
            extra = min(most - holding[i], max(1, left * portions[i] // whole), rest)
            holding[i] = holding[i] + extra
            rest = rest - extra
    return np.array([most] + holding)


def uneven(own_key, number_of, total, limit, skew):
    if number_of == 2:
        one = jax.random.randint(own_key, (), max(1, total - limit), min(limit, total - 1) + 1)
        return jnp.stack([one, total - one])
    lengths = jnp.asarray(split_up(number_of, total, limit, skew), jnp.int32)
    pairs = (number_of - 1) // 2
    donor, receiver = lengths[1:1 + 2 * pairs:2], lengths[2:2 + 2 * pairs:2]
    margin = jnp.minimum(donor - 1, limit - receiver)
    passed = jax.random.randint(jax.random.fold_in(own_key, 1), (pairs,), 0, 1 << 20) % (margin + 1)
    lengths = lengths.at[1:1 + 2 * pairs:2].set(donor - passed).at[2:2 + 2 * pairs:2].set(receiver + passed)
    return lengths[jax.random.permutation(jax.random.fold_in(own_key, 2), number_of)]


def centred(own_key, dims, deviation, most, pieces=(), kind=jnp.bfloat16):
    factor_of = block_levels(own_key, dims, pieces, -0.22, 0.18) if pieces else 1.0
    drawn = jax.random.normal(own_key, dims, jnp.float32) * deviation * factor_of
    return jnp.minimum(jnp.maximum(drawn, -most), most).astype(kind)


def setup_inputs(seed: int = 0) -> dict:
    streams_of = jax.random.split(jax.random.key(seed), 8)
    hidden_in = centred(streams_of[0], (BATCH, SEQ, D), 1.0, 6.0, ((0, 4), (1, 16), (2, 4)))
    queries = centred(streams_of[1], (BATCH, SEQ, QH * DH), 1.0, 6.0, ((0, 4), (1, 16), (2, 4)))
    keys_in = centred(streams_of[2], (BATCH, SEQ, KVH * DH), 1.0, 6.0, ((0, 4), (1, 16), (2, 4)))
    values_in = centred(streams_of[3], (BATCH, SEQ, KVH * DH), 1.0, 6.0, ((0, 4), (1, 16), (2, 4)))
    out_grad = centred(streams_of[4], (BATCH, SEQ, QH * DH), 1.0, 6.0, ((0, 4), (1, 16), (2, 4)))
    doc_lengths = jax.vmap(lambda own: uneven(own, NDOCS, SEQ, SEQ // 3, 2))(jax.random.split(streams_of[5], BATCH)).reshape((BATCH, NDOCS)).astype(jnp.int32)
    pair_perm = jax.random.permutation(streams_of[6], N_CTX).astype(jnp.int32)
    return dict(hidden_in=hidden_in, queries=queries, keys_in=keys_in, values_in=values_in, out_grad=out_grad, doc_lengths=doc_lengths, pair_perm=pair_perm)


def token_positions(row_ids, pair_perm, half_rows, ctx_count):
    ctx_rank = row_ids // (2 * half_rows)
    within = row_ids % (2 * half_rows)
    all_ranks = jnp.arange(ctx_count, dtype=jnp.int32)
    chosen = jnp.sum(jnp.where(ctx_rank[:, None] == all_ranks[None, :], pair_perm[None, :], 0), axis=1).astype(jnp.int32)
    first_pos = chosen * half_rows + within
    second_pos = (2 * ctx_count - 1 - chosen) * half_rows + within - half_rows
    return jnp.where(within < half_rows, first_pos, second_pos).astype(jnp.int32)


def document_of(positions, lengths_row):
    doc_ends = jnp.cumsum(lengths_row).astype(jnp.int32)
    return jnp.sum((positions[:, None] >= doc_ends[None, :]).astype(jnp.int32), axis=1).astype(jnp.int32)


def reference(hidden_in, queries, keys_in, values_in, out_grad, doc_lengths, pair_perm):
    seq_len = 2 * STRETCH * N_CTX
    group_size = QH // KVH
    score_scale = DH ** -0.5
    positions = token_positions(jnp.arange(seq_len, dtype=jnp.int32), pair_perm, STRETCH, N_CTX)
    query_grads = []
    key_grads = []
    value_grads = []
    weight_sum = jnp.zeros((2 * KVH * DH, D), jnp.float32)
    for batch_row in range(BATCH):
        documents = document_of(positions, doc_lengths[batch_row])
        allowed = (positions[None, :] <= positions[:, None]) & (documents[None, :] == documents[:, None])
        query_heads = queries[batch_row].reshape(seq_len, QH, DH).transpose(1, 0, 2)
        key_heads = jnp.repeat(keys_in[batch_row].reshape(seq_len, KVH, DH).transpose(1, 0, 2), group_size, axis=0)
        value_heads = jnp.repeat(values_in[batch_row].reshape(seq_len, KVH, DH).transpose(1, 0, 2), group_size, axis=0)
        grad_heads = out_grad[batch_row].reshape(seq_len, QH, DH).transpose(1, 0, 2)

        def one_head(operands):
            query_one, key_one, value_one, grad_one = operands
            scores = jnp.dot(query_one, key_one.T, preferred_element_type=jnp.float32) * score_scale
            weights = jnp.where(allowed, jnp.exp(scores), 0.0)
            summed = jnp.sum(weights, axis=1)
            numerator = jnp.dot(weights.astype(jnp.bfloat16), value_one, preferred_element_type=jnp.float32)
            attn_out = (numerator / summed[:, None]).astype(jnp.bfloat16)
            log_sum = jnp.log(summed)
            delta_row = jnp.sum(grad_one.astype(jnp.float32) * attn_out.astype(jnp.float32), axis=1)
            probabilities = jnp.where(allowed, jnp.exp(scores - log_sum[:, None]), 0.0)
            grad_value = jnp.dot(probabilities.astype(jnp.bfloat16).T, grad_one, preferred_element_type=jnp.float32)
            grad_probs = jnp.dot(grad_one, value_one.T, preferred_element_type=jnp.float32)
            grad_scores = (probabilities * (grad_probs - delta_row[:, None])).astype(jnp.bfloat16)
            grad_query = jnp.dot(grad_scores, key_one, preferred_element_type=jnp.float32) * score_scale
            grad_key = jnp.dot(grad_scores.T, query_one, preferred_element_type=jnp.float32) * score_scale
            return grad_query, grad_key, grad_value

        grad_query, grad_key, grad_value = lax.map(one_head, (query_heads, key_heads, value_heads, grad_heads))
        query_out = grad_query.transpose(1, 0, 2).reshape(seq_len, QH * DH).astype(jnp.bfloat16)
        key_out = jnp.sum(grad_key.reshape(KVH, group_size, seq_len, DH), axis=1).transpose(1, 0, 2).reshape(seq_len, KVH * DH).astype(jnp.bfloat16)
        value_out = jnp.sum(grad_value.reshape(KVH, group_size, seq_len, DH), axis=1).transpose(1, 0, 2).reshape(seq_len, KVH * DH).astype(jnp.bfloat16)
        stacked = jnp.concatenate([key_out, value_out], axis=1)
        weight_sum = weight_sum + jnp.dot(stacked.T, hidden_in[batch_row], preferred_element_type=jnp.float32)
        query_grads.append(query_out)
        key_grads.append(key_out)
        value_grads.append(value_out)
    return jnp.stack(query_grads), jnp.stack(key_grads), jnp.stack(value_grads), weight_sum
```

```python
import functools

import jax
import jax.numpy as jnp
import numpy as np
from jax import lax
from jax.experimental import pallas as pl
from jax.experimental.pallas import tpu as pltpu
from jax.sharding import Mesh, PartitionSpec as P

DH = 128
HEADS = 8
HALF = 112
ROWS = 2 * HALF
LANES = HEADS * HALF
RANKS = 16
BLOCKS = 2 * RANKS
SEQ = ROWS * RANKS
DOCS = 6
MAX_DOC = 1194
SPAN = 256
STEPS = -(-(MAX_DOC - 1 + HALF) // SPAN)
PAD = SPAN
SCALE = DH**-0.5
LOG2E = 1.4426950408889634
MASKED = -1e30
CARDINAL = ("zh", "co", "zl", "y", "x")
SIZES = (2, 2, 4, 4, 4)
BF = jnp.bfloat16
F32 = jnp.float32


def dot(a, b, ca, cb):
    return lax.dot_general(a, b, (((ca,), (cb,)), ((), ())), preferred_element_type=F32)


def fold(x, op):
    return op(x.reshape(x.shape[0] // 8, 8, x.shape[1]), axis=0)


def attention_kernel(
    len_ref, perm_ref, where_ref, q_ref, do_ref, kv0, kv1, kv2, kv3, dq_ref, dkv_ref,
    kbuf, vbuf, dkacc, dvacc, s_scr, dp_scr, qs, dos,
):
    rank = where_ref[0]
    my_y = where_ref[1]
    kbuf[0:PAD, :] = jnp.zeros((PAD, DH), BF)
    vbuf[0:PAD, :] = jnp.zeros((PAD, DH), BF)
    for shift, ref in enumerate((kv0, kv1, kv2, kv3)):
        src_y = lax.rem(my_y + 4 - shift, 4)
        for zl in range(4):
            pair = perm_ref[zl * 4 + src_y]
            for half, block in enumerate((pair, BLOCKS - 1 - pair)):
                to = pl.ds(pl.multiple_of(PAD + block * HALF, 16), HALF)
                kbuf[to, :] = ref[zl, half * HALF : (half + 1) * HALF, 0:DH]
                vbuf[to, :] = ref[zl, half * HALF : (half + 1) * HALF, DH : 2 * DH]
    dkacc[...] = jnp.zeros_like(dkacc)
    dvacc[...] = jnp.zeros_like(dvacc)

    ends = []
    total = jnp.int32(0)
    for d in range(DOCS - 1):
        total = total + len_ref[d]
        ends.append(total)

    lane = lax.broadcasted_iota(jnp.int32, (1, LANES), 1)
    within = lane
    for h in range(1, HEADS):
        within = jnp.where(lane >= h * HALF, lane - h * HALF, within)

    def one_block(half, carry):
        pair = perm_ref[rank]
        block = jnp.where(half == 0, pair, BLOCKS - 1 - pair)
        row0 = pl.multiple_of(half * HALF, 16)
        for h in range(HEADS):
            qs[h * HALF : (h + 1) * HALF, :] = q_ref[pl.ds(row0, HALF), h * DH : (h + 1) * DH]
            dos[h * HALF : (h + 1) * HALF, :] = do_ref[pl.ds(row0, HALF), h * DH : (h + 1) * DH]
        first = block * HALF
        pos = within + first
        low = jnp.zeros_like(pos)
        low0 = jnp.int32(0)
        for end in ends:
            low = jnp.where(pos >= end, end, low)
            low0 = jnp.where(first >= end, end, low0)
        stop = first + HALF
        count = lax.div(stop - low0 + (SPAN - 1), SPAN)
        start = stop - count * SPAN

        def keys_at(t):
            return pl.ds(pl.multiple_of(PAD + start + t * SPAN, 16), SPAN)

        def kept_at(t):
            return pl.ds(pl.multiple_of(t * SPAN, SPAN), SPAN)

        def score(t, top):
            s = dot(kbuf[keys_at(t), :], qs[...], 1, 1)
            key = lax.broadcasted_iota(jnp.int32, (SPAN, LANES), 0) + (start + t * SPAN)
            s = jnp.where((key >= low) & (key <= pos), s * (SCALE * LOG2E), MASKED)
            s_scr[kept_at(t), :] = s
            return jnp.maximum(top, fold(s, jnp.max))

        top = lax.fori_loop(0, count, score, jnp.full((8, LANES), MASKED, F32))
        top = jnp.max(top, axis=0, keepdims=True)

        def weigh(t, sums):
            mass, moment = sums
            e = jnp.exp2(s_scr[kept_at(t), :] - top)
            dp = dot(vbuf[keys_at(t), :], dos[...], 1, 1)
            s_scr[kept_at(t), :] = e
            dp_scr[kept_at(t), :] = dp
            return mass + fold(e, jnp.sum), moment + fold(e * dp, jnp.sum)

        zero = jnp.zeros((8, LANES), F32)
        mass, moment = lax.fori_loop(0, count, weigh, (zero, zero))
        inverse = 1.0 / jnp.sum(mass, axis=0, keepdims=True)
        delta = jnp.sum(moment, axis=0, keepdims=True) * inverse

        def spread(t, dqt):
            p = s_scr[kept_at(t), :] * inverse
            g = (p * (dp_scr[kept_at(t), :] - delta)).astype(BF)
            at = keys_at(t)
            dvacc[at, :] += dot(p.astype(BF), dos[...], 1, 0)
            dkacc[at, :] += dot(g, qs[...], 1, 0)
            return dqt + dot(kbuf[at, :], g, 0, 0)

        dqt = lax.fori_loop(0, count, spread, jnp.zeros((DH, LANES), F32))
        dq = (dqt * SCALE).T.astype(BF)
        for h in range(HEADS):
            dq_ref[pl.ds(row0, HALF), h * DH : (h + 1) * DH] = dq[h * HALF : (h + 1) * HALF, :]
        return carry

    lax.fori_loop(0, 2, one_block, 0)

    for y in range(4):
        for zl in range(4):
            pair = perm_ref[zl * 4 + y]
            for half, block in enumerate((pair, BLOCKS - 1 - pair)):
                at = pl.ds(pl.multiple_of(PAD + block * HALF, 16), HALF)
                rows = slice(half * HALF, (half + 1) * HALF)
                dkv_ref[y, zl, rows, 0:DH] = (dkacc[at, :] * SCALE).astype(BF)
                dkv_ref[y, zl, rows, DH : 2 * DH] = dvacc[at, :].astype(BF)


def attention(lengths, perm, where, q, do, kvs):
    smem = pl.BlockSpec(memory_space=pltpu.SMEM)
    vmem = pl.BlockSpec(memory_space=pltpu.VMEM)
    return pl.pallas_call(
        attention_kernel,
        out_shape=(
            jax.ShapeDtypeStruct((ROWS, HEADS * DH), BF),
            jax.ShapeDtypeStruct((4, 4, ROWS, 2 * DH), BF),
        ),
        in_specs=[smem] * 3 + [vmem] * 6,
        out_specs=(vmem, vmem),
        scratch_shapes=[
            pltpu.VMEM((PAD + SEQ, DH), BF),
            pltpu.VMEM((PAD + SEQ, DH), BF),
            pltpu.VMEM((PAD + SEQ, DH), F32),
            pltpu.VMEM((PAD + SEQ, DH), F32),
            pltpu.VMEM((STEPS * SPAN, LANES), F32),
            pltpu.VMEM((STEPS * SPAN, LANES), F32),
            pltpu.VMEM((LANES, DH), BF),
            pltpu.VMEM((LANES, DH), BF),
        ],
        compiler_params=pltpu.CompilerParams(vmem_limit_bytes=44 * 2**20),
        cost_estimate=pl.CostEstimate(
            flops=6 * 10**9, bytes_accessed=6 * 10**6, transcendentals=3 * 10**6
        ),
    )(lengths, perm, where, q, do, *kvs)


def ring(shift):
    return [(i, (i + shift) % 4) for i in range(4)]


def total(x):
    return jnp.sum(x.astype(F32), axis=0)


def per_device(hidden_in, queries, keys_in, values_in, out_grad, doc_lengths, pair_perm):
    zl, y = lax.axis_index("zl"), lax.axis_index("y")
    where = jnp.stack([zl * 4 + y, y]).astype(jnp.int32)

    own = jnp.concatenate([keys_in[0], values_in[0]], axis=1)
    column = lax.all_gather(own, "zl", axis=0, tiled=False)
    kvs = [column] + [lax.ppermute(column, "y", ring(j)) for j in (1, 2, 3)]
    dq, dkv = attention(doc_lengths[0], pair_perm, where, queries[0], out_grad[0], kvs)

    part = total(lax.all_to_all(dkv, "y", 0, 0)).astype(BF)
    grads = total(lax.all_to_all(part, "zl", 0, 0)).astype(BF)

    core = lax.axis_index("co")
    swap = [(0, 1), (1, 0)]
    hidden = hidden_in[0].reshape(ROWS, 2, -1)
    mine = lax.dynamic_index_in_dim(hidden, core, 1, False)
    theirs = lax.ppermute(lax.dynamic_index_in_dim(hidden, 1 - core, 1, False), "co", swap)
    features = jnp.concatenate([mine, theirs], axis=0)
    stacked = lax.all_gather(grads, "x", axis=1, tiled=False)
    stacked = stacked.reshape(ROWS, 4, 2, DH).transpose(0, 2, 1, 3).reshape(ROWS, 8 * DH)
    both = jnp.concatenate([stacked, lax.ppermute(stacked, "co", swap)], axis=0)
    w = dot(both, features, 0, 0).astype(BF)
    cols = w.shape[1]
    w = w.reshape(2, 2, 4, 4, 16, cols).transpose(3, 2, 0, 1, 4, 5)
    w = total(lax.all_to_all(w, "y", 0, 0)).astype(BF)
    w = total(lax.all_to_all(w, "zl", 0, 0)).astype(BF)
    w = total(lax.all_to_all(w, "zh", 0, 0))
    keep = lax.dynamic_index_in_dim(w, core, 0, False)
    got = lax.ppermute(lax.dynamic_index_in_dim(w, 1 - core, 0, False), "co", swap)
    pair = jnp.stack([keep, got])
    first = lax.dynamic_index_in_dim(pair, core, 0, False)
    second = lax.dynamic_index_in_dim(pair, 1 - core, 0, False)
    grad_weight = jnp.concatenate([first, second], axis=1)
    return dq[None], grads[None, :, :DH], grads[None, :, DH:], grad_weight


def solution(mesh):
    fine = Mesh(mesh.devices.reshape(SIZES), CARDINAL)
    dp, ctx, tp = ("zh", "co"), ("zl", "y"), "x"
    tokens = P(dp, ctx, tp)
    return jax.shard_map(
        per_device,
        mesh=fine,
        in_specs=(tokens,) * 5 + (P(dp, None), P()),
        out_specs=(tokens,) * 3 + (P(dp + ctx, tp),),
        check_vma=False,
    )
```

```python
import functools

import jax
import jax.numpy as jnp
import numpy as np
from jax import lax
from jax.experimental import pallas as pl
from jax.experimental.pallas import tpu as pltpu
from jax.sharding import Mesh, PartitionSpec as P

DH = 128
HEADS = 8
HALF = 112
ROWS = 2 * HALF
LANES = HEADS * HALF
RANKS = 16
BLOCKS = 2 * RANKS
SEQ = ROWS * RANKS
DOCS = 6
MAX_DOC = 1194
SPAN = 256
STEPS = -(-(MAX_DOC - 1 + HALF) // SPAN)
PAD = SPAN
SCALE = DH**-0.5
LOG2E = 1.4426950408889634
MASKED = -1e30
CARDINAL = ("zh", "co", "zl", "y", "x")
SIZES = (2, 2, 4, 4, 4)
BF = jnp.bfloat16
F32 = jnp.float32


def dot(a, b, ca, cb):
    return lax.dot_general(a, b, (((ca,), (cb,)), ((), ())), preferred_element_type=F32)


def fold(x, op):
    return op(x.reshape(x.shape[0] // 8, 8, x.shape[1]), axis=0)


def attention_kernel(
    facts, q_hbm, do_hbm, kv0, kv1, kv2, kv3, dq_ref, out0, out1, out2, out3,
    q_ref, do_ref, sems, kbuf, vbuf, dkacc, dvacc, s_scr, dp_scr, qs, dos,
):
    loads = [
        pltpu.make_async_copy(q_hbm, q_ref, sems.at[0]),
        pltpu.make_async_copy(do_hbm, do_ref, sems.at[1]),
    ]
    for load in loads:
        load.start()

    def len_of(d):
        return facts[d]

    def pair_of(rank):
        return facts[DOCS + rank]

    my_zl = facts[DOCS + RANKS]
    my_y = facts[DOCS + RANKS + 1]

    def place(pair, half):
        block = pair if half == 0 else BLOCKS - 1 - pair
        return pl.ds(pl.multiple_of(PAD + block * HALF, 16), HALF)

    kbuf[0:PAD, :] = jnp.zeros((PAD, DH), BF)
    vbuf[0:PAD, :] = jnp.zeros((PAD, DH), BF)
    for shift, ref in enumerate((kv0, kv1, kv2, kv3)):
        src_y = lax.rem(my_y + 4 - shift, 4)
        for a in range(4):
            pair = pair_of(lax.rem(my_zl + 4 - a, 4) * 4 + src_y)
            for half in range(2):
                rows = slice(half * HALF, (half + 1) * HALF)
                kbuf[place(pair, half), :] = ref[a, rows, 0:DH]
                vbuf[place(pair, half), :] = ref[a, rows, DH : 2 * DH]
    dkacc[...] = jnp.zeros_like(dkacc)
    dvacc[...] = jnp.zeros_like(dvacc)

    ends = []
    total = jnp.int32(0)
    for d in range(DOCS - 1):
        total = total + len_of(d)
        ends.append(total)

    lane = lax.broadcasted_iota(jnp.int32, (1, LANES), 1)
    within = lane
    for h in range(1, HEADS):
        within = jnp.where(lane >= h * HALF, lane - h * HALF, within)

    for load in loads:
        load.wait()

    def one_block(half, carry):
        pair = pair_of(my_zl * 4 + my_y)
        block = jnp.where(half == 0, pair, BLOCKS - 1 - pair)
        row0 = pl.multiple_of(half * HALF, 16)
        for h in range(HEADS):
            qs[h * HALF : (h + 1) * HALF, :] = q_ref[pl.ds(row0, HALF), h * DH : (h + 1) * DH]
            dos[h * HALF : (h + 1) * HALF, :] = do_ref[pl.ds(row0, HALF), h * DH : (h + 1) * DH]
        first = block * HALF
        pos = within + first
        low = jnp.zeros_like(pos)
        low0 = jnp.int32(0)
        for end in ends:
            low = jnp.where(pos >= end, end, low)
            low0 = jnp.where(first >= end, end, low0)
        stop = first + HALF
        count = lax.div(stop - low0 + (SPAN - 1), SPAN)
        start = stop - count * SPAN

        def keys_at(t):
            return pl.ds(pl.multiple_of(PAD + start + t * SPAN, 16), SPAN)

        def kept_at(t):
            return pl.ds(pl.multiple_of(t * SPAN, SPAN), SPAN)

        def score(t, top):
            s = dot(kbuf[keys_at(t), :], qs[...], 1, 1)
            key = lax.broadcasted_iota(jnp.int32, (SPAN, LANES), 0) + (start + t * SPAN)
            s = jnp.where((key >= low) & (key <= pos), s * (SCALE * LOG2E), MASKED)
            s_scr[kept_at(t), :] = s
            return jnp.maximum(top, fold(s, jnp.max))

        top = lax.fori_loop(0, count, score, jnp.full((8, LANES), MASKED, F32))
        top = jnp.max(top, axis=0, keepdims=True)

        def weigh(t, sums):
            mass, moment = sums
            e = jnp.exp2(s_scr[kept_at(t), :] - top)
            dp = dot(vbuf[keys_at(t), :], dos[...], 1, 1)
            s_scr[kept_at(t), :] = e
            dp_scr[kept_at(t), :] = dp
            return mass + fold(e, jnp.sum), moment + fold(e * dp, jnp.sum)

        zero = jnp.zeros((8, LANES), F32)
        mass, moment = lax.fori_loop(0, count, weigh, (zero, zero))
        inverse = 1.0 / jnp.sum(mass, axis=0, keepdims=True)
        delta = jnp.sum(moment, axis=0, keepdims=True) * inverse

        def spread(t, dqt):
            p = s_scr[kept_at(t), :] * inverse
            g = (p * (dp_scr[kept_at(t), :] - delta)).astype(BF)
            at = keys_at(t)
            dvacc[at, :] += dot(p.astype(BF), dos[...], 1, 0)
            dkacc[at, :] += dot(g, qs[...], 1, 0)
            return dqt + dot(kbuf[at, :], g, 0, 0)

        dqt = lax.fori_loop(0, count, spread, jnp.zeros((DH, LANES), F32))
        dq = (dqt * SCALE).T.astype(BF)
        for h in range(HEADS):
            dq_ref[pl.ds(row0, HALF), h * DH : (h + 1) * DH] = dq[h * HALF : (h + 1) * HALF, :]
        return carry

    lax.fori_loop(0, 2, one_block, 0)

    for shift, ref in enumerate((out0, out1, out2, out3)):
        y = lax.rem(my_y + shift, 4)
        for a in range(4):
            pair = pair_of(lax.rem(my_zl + a, 4) * 4 + y)
            for half in range(2):
                at = place(pair, half)
                rows = slice(half * HALF, (half + 1) * HALF)
                ref[a, rows, 0:DH] = (dkacc[at, :] * SCALE).astype(BF)
                ref[a, rows, DH : 2 * DH] = dvacc[at, :].astype(BF)


def attention(facts, q, do, kvs):
    vmem = pl.BlockSpec(memory_space=pltpu.VMEM)
    hbm = pl.BlockSpec(memory_space=pltpu.HBM)
    return pl.pallas_call(
        attention_kernel,
        out_shape=(jax.ShapeDtypeStruct((ROWS, HEADS * DH), BF),)
        + (jax.ShapeDtypeStruct((4, ROWS, 2 * DH), BF),) * 4,
        in_specs=[pl.BlockSpec(memory_space=pltpu.SMEM), hbm, hbm] + [vmem] * 4,
        out_specs=(vmem,) * 5,
        scratch_shapes=[
            pltpu.VMEM((ROWS, HEADS * DH), BF),
            pltpu.VMEM((ROWS, HEADS * DH), BF),
            pltpu.SemaphoreType.DMA((2,)),
            pltpu.VMEM((PAD + SEQ, DH), BF),
            pltpu.VMEM((PAD + SEQ, DH), BF),
            pltpu.VMEM((PAD + SEQ, DH), F32),
            pltpu.VMEM((PAD + SEQ, DH), F32),
            pltpu.VMEM((STEPS * SPAN, LANES), F32),
            pltpu.VMEM((STEPS * SPAN, LANES), F32),
            pltpu.VMEM((LANES, DH), BF),
            pltpu.VMEM((LANES, DH), BF),
        ],
        compiler_params=pltpu.CompilerParams(vmem_limit_bytes=40 * 2**20),
        cost_estimate=pl.CostEstimate(
            flops=6 * 10**9, bytes_accessed=6 * 10**6, transcendentals=3 * 10**6
        ),
    )(facts, q, do, *kvs)


def ring(shift):
    return [(i, (i + shift) % 4) for i in range(4)]


def add_up(*xs):
    return functools.reduce(lambda a, b: a + b, [x.astype(F32) for x in xs])


def owner(v):
    pairs = []
    for index in np.ndindex(*SIZES):
        zh, co, zl, y, x = index
        target = (zh, x >> 1, (x & 1) * 2 + (zl & 1), (zl >> 1) * 2 + (v ^ co), y)
        pairs.append(tuple(int(np.ravel_multi_index(i, SIZES)) for i in (index, target)))
    return pairs


def hidden_for_weight(hidden, core, y, x):
    width = hidden.shape[1] // 2
    run = width // 4
    mine = lax.dynamic_slice_in_dim(hidden, core * width, width, 1)
    theirs = lax.ppermute(
        lax.dynamic_slice_in_dim(hidden, (1 - core) * width, width, 1), "co", [(0, 1), (1, 0)]
    )
    both = jnp.concatenate([mine, theirs], axis=0)
    runs = []
    for j in range(4):
        chunk = lax.dynamic_slice_in_dim(both, lax.rem(x + j, 4) * run, run, 1)
        runs.append(chunk if j == 0 else lax.ppermute(chunk, "x", ring(j)))
    runs = jnp.stack(runs)
    tokens = []
    for s in range(4):
        block = lax.dynamic_index_in_dim(runs, lax.rem(x - y - s + 8, 4), 0, False)
        tokens.append(block if s == 0 else lax.ppermute(block, "y", ring(s)))
    return lax.all_gather(jnp.concatenate(tokens, axis=0), "x", axis=0, tiled=False)


def per_device(hidden_in, queries, keys_in, values_in, out_grad, doc_lengths, pair_perm):
    zl, y, x = (lax.axis_index(a) for a in ("zl", "y", "x"))
    core = lax.axis_index("co")
    swap = [(0, 1), (1, 0)]
    facts = jnp.concatenate([doc_lengths[0], pair_perm, jnp.stack([zl, y]).astype(jnp.int32)])

    own = jnp.concatenate([keys_in[0], values_in[0]], axis=1)
    column = jnp.stack([own] + [lax.ppermute(own, "zl", ring(a)) for a in (1, 2, 3)])
    kvs = [column] + [lax.ppermute(column, "y", ring(s)) for s in (1, 2, 3)]
    hidden = hidden_for_weight(hidden_in[0], core, y, x)
    dq, *dkv = attention(facts, queries[0], out_grad[0], kvs)

    got = [dkv[0]] + [lax.ppermute(dkv[s], "y", ring(s)) for s in (1, 2, 3)]
    parts = [add_up(*[g[a] for g in got]) for a in range(4)]
    parts = [parts[0]] + [lax.ppermute(parts[a].astype(BF), "zl", ring(a)) for a in (1, 2, 3)]
    grads = add_up(*parts).astype(BF)

    rows = jnp.stack([grads] + [lax.ppermute(grads, "y", ring(s)) for s in (1, 2, 3)])
    rows = jnp.stack([rows, lax.ppermute(rows, "co", swap)], axis=1)
    rows = rows.reshape(8 * ROWS, 2 * DH)
    w = lax.dot_general(rows, hidden, (((0,), (1,)), ((), ())), preferred_element_type=F32)
    w = w.astype(BF).reshape(2, 2, 2, 32, -1).transpose(0, 2, 1, 3, 4).reshape(8, 32, -1)
    w = lax.all_to_all(w, ("zh", "zl"), 0, 0)
    w = jnp.sum(w.astype(F32), axis=0)
    blocks = []
    for v in range(2):
        block = lax.dynamic_slice_in_dim(w, lax.rem(core + v, 2) * 16, 16, 0)
        blocks.append(lax.ppermute(block, CARDINAL, owner(v)))
    even = lax.rem(y, 2) == 0
    left = jnp.where(even, blocks[0], blocks[1])
    right = jnp.where(even, blocks[1], blocks[0])
    grad_weight = jnp.concatenate([left, right], axis=1)
    return dq[None], grads[None, :, :DH], grads[None, :, DH:], grad_weight


def solution(mesh):
    fine = Mesh(mesh.devices.reshape(SIZES), CARDINAL)
    dp, ctx, tp = ("zh", "co"), ("zl", "y"), "x"
    tokens = P(dp, ctx, tp)
    return jax.shard_map(
        per_device,
        mesh=fine,
        in_specs=(tokens,) * 5 + (P(dp, None), P()),
        out_specs=(tokens,) * 3 + (P(dp + ctx, tp),),
        check_vma=False,
    )
```

```python
import functools

import jax
import jax.numpy as jnp
import numpy as np
from jax import lax
from jax.experimental import pallas as pl
from jax.experimental.pallas import tpu as pltpu
from jax.sharding import Mesh, PartitionSpec as P

DH = 128
HEADS = 8
HALF = 112
ROWS = 2 * HALF
LANES = HEADS * HALF
RANKS = 16
BLOCKS = 2 * RANKS
SEQ = ROWS * RANKS
DOCS = 6
MAX_DOC = 1194
SPAN = 256
STEPS = -(-(MAX_DOC - 1 + HALF) // SPAN)
PAD = SPAN
SCALE = DH**-0.5
LOG2E = 1.4426950408889634
MASKED = -1e30
CARDINAL = ("zh", "co", "zl", "y", "x")
SIZES = (2, 2, 4, 4, 4)
BF = jnp.bfloat16
F32 = jnp.float32


def dot(a, b, ca, cb):
    return lax.dot_general(a, b, (((ca,), (cb,)), ((), ())), preferred_element_type=F32)


def fold(x, op):
    return op(x.reshape(x.shape[0] // 8, 8, x.shape[1]), axis=0)


def attention_kernel(
    facts, q_hbm, do_hbm, kv0, kv1, kv2, kv3, dq_ref, out0, out1, out2, out3,
    q_ref, do_ref, sems, kbuf, vbuf, dkacc, dvacc, s_scr, dp_scr, qs, dos,
):
    loads = [
        pltpu.make_async_copy(q_hbm, q_ref, sems.at[0]),
        pltpu.make_async_copy(do_hbm, do_ref, sems.at[1]),
    ]
    for load in loads:
        load.start()

    def len_of(d):
        return facts[d]

    def pair_of(rank):
        return facts[DOCS + rank]

    my_zl = facts[DOCS + RANKS]
    my_y = facts[DOCS + RANKS + 1]

    def place(pair, half):
        block = pair if half == 0 else BLOCKS - 1 - pair
        return pl.ds(pl.multiple_of(PAD + block * HALF, 16), HALF)

    kbuf[0:PAD, :] = jnp.zeros((PAD, DH), BF)
    vbuf[0:PAD, :] = jnp.zeros((PAD, DH), BF)
    for shift, ref in enumerate((kv0, kv1, kv2, kv3)):
        src_y = lax.rem(my_y + 4 - shift, 4)
        for a in range(4):
            pair = pair_of(lax.rem(my_zl + 4 - a, 4) * 4 + src_y)
            for half in range(2):
                rows = slice(half * HALF, (half + 1) * HALF)
                kbuf[place(pair, half), :] = ref[a, rows, 0:DH]
                vbuf[place(pair, half), :] = ref[a, rows, DH : 2 * DH]
    dkacc[...] = jnp.zeros_like(dkacc)
    dvacc[...] = jnp.zeros_like(dvacc)

    ends = []
    total = jnp.int32(0)
    for d in range(DOCS - 1):
        total = total + len_of(d)
        ends.append(total)

    lane = lax.broadcasted_iota(jnp.int32, (1, LANES), 1)
    within = lane
    for h in range(1, HEADS):
        within = jnp.where(lane >= h * HALF, lane - h * HALF, within)

    for load in loads:
        load.wait()

    def one_block(half, carry):
        pair = pair_of(my_zl * 4 + my_y)
        block = jnp.where(half == 0, pair, BLOCKS - 1 - pair)
        row0 = pl.multiple_of(half * HALF, 16)
        for h in range(HEADS):
            qs[h * HALF : (h + 1) * HALF, :] = q_ref[pl.ds(row0, HALF), h * DH : (h + 1) * DH]
            dos[h * HALF : (h + 1) * HALF, :] = do_ref[pl.ds(row0, HALF), h * DH : (h + 1) * DH]
        first = block * HALF
        pos = within + first
        low = jnp.zeros_like(pos)
        low0 = jnp.int32(0)
        for end in ends:
            low = jnp.where(pos >= end, end, low)
            low0 = jnp.where(first >= end, end, low0)
        stop = first + HALF
        count = lax.div(stop - low0 + (SPAN - 1), SPAN)
        start = stop - count * SPAN

        def keys_at(t):
            return pl.ds(pl.multiple_of(PAD + start + t * SPAN, 16), SPAN)

        def kept_at(t):
            return pl.ds(pl.multiple_of(t * SPAN, SPAN), SPAN)

        def score(t, top):
            s = dot(kbuf[keys_at(t), :], qs[...], 1, 1)
            key = lax.broadcasted_iota(jnp.int32, (SPAN, LANES), 0) + (start + t * SPAN)
            s = jnp.where((key >= low) & (key <= pos), s * (SCALE * LOG2E), MASKED)
            s_scr[kept_at(t), :] = s
            return jnp.maximum(top, fold(s, jnp.max))

        top = lax.fori_loop(0, count, score, jnp.full((8, LANES), MASKED, F32))
        top = jnp.max(top, axis=0, keepdims=True)

        def weigh(t, sums):
            mass, moment = sums
            e = jnp.exp2(s_scr[kept_at(t), :] - top)
            dp = dot(vbuf[keys_at(t), :], dos[...], 1, 1)
            s_scr[kept_at(t), :] = e
            dp_scr[kept_at(t), :] = dp
            return mass + fold(e, jnp.sum), moment + fold(e * dp, jnp.sum)

        zero = jnp.zeros((8, LANES), F32)
        mass, moment = lax.fori_loop(0, count, weigh, (zero, zero))
        inverse = 1.0 / jnp.sum(mass, axis=0, keepdims=True)
        delta = jnp.sum(moment, axis=0, keepdims=True) * inverse

        def spread(t, dqt):
            p = s_scr[kept_at(t), :] * inverse
            g = (p * (dp_scr[kept_at(t), :] - delta)).astype(BF)
            at = keys_at(t)
            dvacc[at, :] += dot(p.astype(BF), dos[...], 1, 0)
            dkacc[at, :] += dot(g, qs[...], 1, 0)
            return dqt + dot(kbuf[at, :], g, 0, 0)

        dqt = lax.fori_loop(0, count, spread, jnp.zeros((DH, LANES), F32))
        dq = (dqt * SCALE).T.astype(BF)
        for h in range(HEADS):
            dq_ref[pl.ds(row0, HALF), h * DH : (h + 1) * DH] = dq[h * HALF : (h + 1) * HALF, :]
        return carry

    lax.fori_loop(0, 2, one_block, 0)

    for shift, ref in enumerate((out0, out1, out2, out3)):
        y = lax.rem(my_y + shift, 4)
        for a in range(4):
            pair = pair_of(lax.rem(my_zl + a, 4) * 4 + y)
            for half in range(2):
                at = place(pair, half)
                rows = slice(half * HALF, (half + 1) * HALF)
                ref[a, rows, 0:DH] = (dkacc[at, :] * SCALE).astype(BF)
                ref[a, rows, DH : 2 * DH] = dvacc[at, :].astype(BF)


def attention(facts, q, do, kvs):
    vmem = pl.BlockSpec(memory_space=pltpu.VMEM)
    hbm = pl.BlockSpec(memory_space=pltpu.HBM)
    return pl.pallas_call(
        attention_kernel,
        out_shape=(jax.ShapeDtypeStruct((ROWS, HEADS * DH), BF),)
        + (jax.ShapeDtypeStruct((4, ROWS, 2 * DH), BF),) * 4,
        in_specs=[pl.BlockSpec(memory_space=pltpu.SMEM), hbm, hbm] + [vmem] * 4,
        out_specs=(vmem,) * 5,
        scratch_shapes=[
            pltpu.VMEM((ROWS, HEADS * DH), BF),
            pltpu.VMEM((ROWS, HEADS * DH), BF),
            pltpu.SemaphoreType.DMA((2,)),
            pltpu.VMEM((PAD + SEQ, DH), BF),
            pltpu.VMEM((PAD + SEQ, DH), BF),
            pltpu.VMEM((PAD + SEQ, DH), F32),
            pltpu.VMEM((PAD + SEQ, DH), F32),
            pltpu.VMEM((STEPS * SPAN, LANES), F32),
            pltpu.VMEM((STEPS * SPAN, LANES), F32),
            pltpu.VMEM((LANES, DH), BF),
            pltpu.VMEM((LANES, DH), BF),
        ],
        compiler_params=pltpu.CompilerParams(vmem_limit_bytes=40 * 2**20),
        cost_estimate=pl.CostEstimate(
            flops=6 * 10**9, bytes_accessed=6 * 10**6, transcendentals=3 * 10**6
        ),
    )(facts, q, do, *kvs)


def ring(shift):
    return [(i, (i + shift) % 4) for i in range(4)]


def add_up(*xs):
    return functools.reduce(lambda a, b: a + b, [x.astype(F32) for x in xs])


def owner(v):
    pairs = []
    for index in np.ndindex(*SIZES):
        zh, co, zl, y, x = index
        target = (zh, x >> 1, (x & 1) * 2 + (v ^ co), y, zl)
        pairs.append(tuple(int(np.ravel_multi_index(i, SIZES)) for i in (index, target)))
    return pairs


def product_kernel(facts, hidden, *refs):
    rows, outs, acc = refs[:-5], refs[-5:-1], refs[-1]
    my_y = facts[DOCS + RANKS + 1]
    for run in range(4):
        total = None
        for i, piece in enumerate(rows):
            tokens = hidden[run, i * ROWS * 4 : (i + 1) * ROWS * 4, :]
            part = dot(piece[...].reshape(4 * ROWS, 2 * DH), tokens, 0, 0)
            total = part if total is None else total + part
        acc[...] = total
        for shift, out in enumerate(outs):
            y = lax.rem(my_y + shift, 4)
            for block in range(4):
                at = pl.ds(pl.multiple_of(block * 64 + y * 16, 16), 16)
                out[block, :, run * 256 : (run + 1) * 256] = acc[at, :].astype(BF)


def weight_product(facts, hidden, rows):
    vmem = pl.BlockSpec(memory_space=pltpu.VMEM)
    return pl.pallas_call(
        product_kernel,
        out_shape=(jax.ShapeDtypeStruct((4, 16, 1024), BF),) * 4,
        in_specs=[pl.BlockSpec(memory_space=pltpu.SMEM)] + [vmem] * (1 + len(rows)),
        out_specs=(vmem,) * 4,
        scratch_shapes=[pltpu.VMEM((2 * DH, 256), F32)],
        compiler_params=pltpu.CompilerParams(vmem_limit_bytes=24 * 2**20),
        cost_estimate=pl.CostEstimate(flops=10**9, bytes_accessed=6 * 10**6, transcendentals=0),
    )(facts, hidden, *rows)


def per_device(hidden_in, queries, keys_in, values_in, out_grad, doc_lengths, pair_perm):
    zl, y, x = (lax.axis_index(a) for a in ("zl", "y", "x"))
    zh, core = lax.axis_index("zh"), lax.axis_index("co")
    swap = [(0, 1), (1, 0)]
    facts = jnp.concatenate([doc_lengths[0], pair_perm, jnp.stack([zl, y]).astype(jnp.int32)])

    own = jnp.concatenate([keys_in[0], values_in[0]], axis=1)
    column = [own] + [lax.ppermute(own, "zl", ring(a)) for a in (1, 2, 3)]
    halves = hidden_in[0].reshape(ROWS, 2, 4, -1)
    runs = []
    for j in range(4):
        run = lax.dynamic_index_in_dim(halves, lax.rem(x + j, 4), 2, False)
        run = run.transpose(1, 0, 2)
        runs.append(run if j == 0 else lax.ppermute(run, "x", ring(j)))
    column, runs = lax.optimization_barrier((column, runs))

    column, runs = jnp.stack(column), jnp.stack(runs)
    kvs = [column] + [lax.ppermute(column, "y", ring(s)) for s in (1, 2, 3)]
    tokens = []
    for s in range(4):
        block = lax.dynamic_index_in_dim(runs, lax.rem(x - zl - s + 8, 4), 0, False)
        tokens.append(block if s == 0 else lax.ppermute(block, "zl", ring(s)))
    kvs, tokens = lax.optimization_barrier((kvs, tokens))

    tokens = jnp.stack(tokens)
    mine = lax.dynamic_index_in_dim(tokens, core, 1, False)
    theirs = lax.ppermute(lax.dynamic_index_in_dim(tokens, 1 - core, 1, False), "co", swap)
    hidden = jnp.concatenate([mine.reshape(4 * ROWS, -1), theirs.reshape(4 * ROWS, -1)], axis=0)
    hidden = lax.all_gather(hidden, "x", axis=0, tiled=False)

    dq, *dkv = attention(facts, queries[0], out_grad[0], kvs)

    got = [dkv[0]] + [lax.ppermute(dkv[s], "y", ring(s)) for s in (1, 2, 3)]
    parts = [add_up(*[g[a] for g in got]) for a in range(4)]
    parts = [parts[0]] + [lax.ppermute(parts[a].astype(BF), "zl", ring(a)) for a in (1, 2, 3)]
    grads = add_up(*parts).astype(BF)

    rows = jnp.stack([grads] + [lax.ppermute(grads, "zl", ring(s)) for s in (1, 2, 3)])
    rows = (rows, lax.ppermute(rows, "co", swap))
    shares = weight_product(facts, hidden, rows)
    shares = [shares[0]] + [lax.ppermute(shares[s], "y", ring(s)) for s in (1, 2, 3)]
    share = add_up(*shares).reshape(2, 2, 16, -1)
    kept = lax.dynamic_index_in_dim(share, zh, 0, False)
    sent = lax.dynamic_index_in_dim(share, 1 - zh, 0, False).astype(BF)
    share = kept + lax.ppermute(sent, "zh", swap).astype(F32)
    blocks = []
    for v in range(2):
        block = lax.dynamic_index_in_dim(share, lax.rem(core + v, 2), 0, False)
        blocks.append(lax.ppermute(block, CARDINAL, owner(v)))
    even = lax.rem(zl, 2) == 0
    left = jnp.where(even, blocks[0], blocks[1])
    right = jnp.where(even, blocks[1], blocks[0])
    grad_weight = jnp.concatenate([left, right], axis=1)
    return dq[None], grads[None, :, :DH], grads[None, :, DH:], grad_weight


def solution(mesh):
    fine = Mesh(mesh.devices.reshape(SIZES), CARDINAL)
    dp, ctx, tp = ("zh", "co"), ("zl", "y"), "x"
    tokens = P(dp, ctx, tp)
    return jax.shard_map(
        per_device,
        mesh=fine,
        in_specs=(tokens,) * 5 + (P(dp, None), P()),
        out_specs=(tokens,) * 3 + (P(dp + ctx, tp),),
        check_vma=False,
    )
```

```python
import functools

import jax
import jax.numpy as jnp
import numpy as np
from jax import lax
from jax.experimental import pallas as pl
from jax.experimental.pallas import tpu as pltpu
from jax.sharding import Mesh, PartitionSpec as P

DH = 128
HEADS = 8
HALF = 112
ROWS = 2 * HALF
LANES = HEADS * HALF
RANKS = 16
BLOCKS = 2 * RANKS
SEQ = ROWS * RANKS
DOCS = 6
MAX_DOC = 1194
SPAN = 256
STEPS = -(-(MAX_DOC - 1 + HALF) // SPAN)
PAD = SPAN
SCALE = DH**-0.5
LOG2E = 1.4426950408889634
MASKED = -1e30
CARDINAL = ("zh", "co", "zl", "y", "x")
SIZES = (2, 2, 4, 4, 4)
BF = jnp.bfloat16
F32 = jnp.float32


def dot(a, b, ca, cb):
    return lax.dot_general(a, b, (((ca,), (cb,)), ((), ())), preferred_element_type=F32)


def fold(x, op):
    return op(x.reshape(x.shape[0] // 8, 8, x.shape[1]), axis=0)


def attention_kernel(
    facts, q_hbm, do_hbm, kv0, kv1, kv2, kv3, dq_ref, out0, out1, out2, out3,
    q_ref, do_ref, sems, kbuf, vbuf, dkacc, dvacc, s_scr, dp_scr, qs, dos,
):
    loads = [
        pltpu.make_async_copy(q_hbm, q_ref, sems.at[0]),
        pltpu.make_async_copy(do_hbm, do_ref, sems.at[1]),
    ]
    for load in loads:
        load.start()

    def len_of(d):
        return facts[d]

    def pair_of(rank):
        return facts[DOCS + rank]

    my_zl = facts[DOCS + RANKS]
    my_y = facts[DOCS + RANKS + 1]

    def place(pair, half):
        block = pair if half == 0 else BLOCKS - 1 - pair
        return pl.ds(pl.multiple_of(PAD + block * HALF, 16), HALF)

    kbuf[0:PAD, :] = jnp.zeros((PAD, DH), BF)
    vbuf[0:PAD, :] = jnp.zeros((PAD, DH), BF)
    for shift, ref in enumerate((kv0, kv1, kv2, kv3)):
        src_y = lax.rem(my_y + 4 - shift, 4)
        for a in range(4):
            pair = pair_of(lax.rem(my_zl + 4 - a, 4) * 4 + src_y)
            for half in range(2):
                rows = slice(half * HALF, (half + 1) * HALF)
                kbuf[place(pair, half), :] = ref[a, rows, 0:DH]
                vbuf[place(pair, half), :] = ref[a, rows, DH : 2 * DH]
    dkacc[...] = jnp.zeros_like(dkacc)
    dvacc[...] = jnp.zeros_like(dvacc)

    ends = []
    total = jnp.int32(0)
    for d in range(DOCS - 1):
        total = total + len_of(d)
        ends.append(total)

    lane = lax.broadcasted_iota(jnp.int32, (1, LANES), 1)
    within = lane
    for h in range(1, HEADS):
        within = jnp.where(lane >= h * HALF, lane - h * HALF, within)

    for load in loads:
        load.wait()

    def one_block(half, carry):
        pair = pair_of(my_zl * 4 + my_y)
        block = jnp.where(half == 0, pair, BLOCKS - 1 - pair)
        row0 = pl.multiple_of(half * HALF, 16)
        for h in range(HEADS):
            qs[h * HALF : (h + 1) * HALF, :] = q_ref[pl.ds(row0, HALF), h * DH : (h + 1) * DH]
            dos[h * HALF : (h + 1) * HALF, :] = do_ref[pl.ds(row0, HALF), h * DH : (h + 1) * DH]
        first = block * HALF
        pos = within + first
        low = jnp.zeros_like(pos)
        low0 = jnp.int32(0)
        for end in ends:
            low = jnp.where(pos >= end, end, low)
            low0 = jnp.where(first >= end, end, low0)
        stop = first + HALF
        count = lax.div(stop - low0 + (SPAN - 1), SPAN)
        start = stop - count * SPAN

        def keys_at(t):
            return pl.ds(pl.multiple_of(PAD + start + t * SPAN, 16), SPAN)

        def kept_at(t):
            return pl.ds(pl.multiple_of(t * SPAN, SPAN), SPAN)

        def score(t, top):
            s = dot(kbuf[keys_at(t), :], qs[...], 1, 1)
            key = lax.broadcasted_iota(jnp.int32, (SPAN, LANES), 0) + (start + t * SPAN)
            s = jnp.where((key >= low) & (key <= pos), s * (SCALE * LOG2E), MASKED)
            s_scr[kept_at(t), :] = s
            return jnp.maximum(top, fold(s, jnp.max))

        top = lax.fori_loop(0, count, score, jnp.full((8, LANES), MASKED, F32))
        top = jnp.max(top, axis=0, keepdims=True)

        def weigh(t, sums):
            mass, moment = sums
            e = jnp.exp2(s_scr[kept_at(t), :] - top)
            dp = dot(vbuf[keys_at(t), :], dos[...], 1, 1)
            s_scr[kept_at(t), :] = e
            dp_scr[kept_at(t), :] = dp
            return mass + fold(e, jnp.sum), moment + fold(e * dp, jnp.sum)

        zero = jnp.zeros((8, LANES), F32)
        mass, moment = lax.fori_loop(0, count, weigh, (zero, zero))
        inverse = 1.0 / jnp.sum(mass, axis=0, keepdims=True)
        delta = jnp.sum(moment, axis=0, keepdims=True) * inverse

        def spread(t, dqt):
            p = s_scr[kept_at(t), :] * inverse
            g = (p * (dp_scr[kept_at(t), :] - delta)).astype(BF)
            at = keys_at(t)
            dvacc[at, :] += dot(p.astype(BF), dos[...], 1, 0)
            dkacc[at, :] += dot(g, qs[...], 1, 0)
            return dqt + dot(kbuf[at, :], g, 0, 0)

        dqt = lax.fori_loop(0, count, spread, jnp.zeros((DH, LANES), F32))
        dq = (dqt * SCALE).T.astype(BF)
        for h in range(HEADS):
            dq_ref[pl.ds(row0, HALF), h * DH : (h + 1) * DH] = dq[h * HALF : (h + 1) * HALF, :]
        return carry

    lax.fori_loop(0, 2, one_block, 0)

    for shift, ref in enumerate((out0, out1, out2, out3)):
        y = lax.rem(my_y + shift, 4)
        for a in range(4):
            pair = pair_of(lax.rem(my_zl + a, 4) * 4 + y)
            for half in range(2):
                at = place(pair, half)
                rows = slice(half * HALF, (half + 1) * HALF)
                ref[a, rows, 0:DH] = (dkacc[at, :] * SCALE).astype(BF)
                ref[a, rows, DH : 2 * DH] = dvacc[at, :].astype(BF)


def attention(facts, q, do, kvs):
    vmem = pl.BlockSpec(memory_space=pltpu.VMEM)
    hbm = pl.BlockSpec(memory_space=pltpu.HBM)
    return pl.pallas_call(
        attention_kernel,
        out_shape=(jax.ShapeDtypeStruct((ROWS, HEADS * DH), BF),)
        + (jax.ShapeDtypeStruct((4, ROWS, 2 * DH), BF),) * 4,
        in_specs=[pl.BlockSpec(memory_space=pltpu.SMEM), hbm, hbm] + [vmem] * 4,
        out_specs=(vmem,) * 5,
        scratch_shapes=[
            pltpu.VMEM((ROWS, HEADS * DH), BF),
            pltpu.VMEM((ROWS, HEADS * DH), BF),
            pltpu.SemaphoreType.DMA((2,)),
            pltpu.VMEM((PAD + SEQ, DH), BF),
            pltpu.VMEM((PAD + SEQ, DH), BF),
            pltpu.VMEM((PAD + SEQ, DH), F32),
            pltpu.VMEM((PAD + SEQ, DH), F32),
            pltpu.VMEM((STEPS * SPAN, LANES), F32),
            pltpu.VMEM((STEPS * SPAN, LANES), F32),
            pltpu.VMEM((LANES, DH), BF),
            pltpu.VMEM((LANES, DH), BF),
        ],
        compiler_params=pltpu.CompilerParams(vmem_limit_bytes=40 * 2**20),
        cost_estimate=pl.CostEstimate(
            flops=6 * 10**9, bytes_accessed=6 * 10**6, transcendentals=3 * 10**6
        ),
    )(facts, q, do, *kvs)


def ring(shift):
    return [(i, (i + shift) % 4) for i in range(4)]


def add_up(*xs):
    return functools.reduce(lambda a, b: a + b, [x.astype(F32) for x in xs])


def owner(w, v):
    pairs = []
    for index in np.ndindex(*SIZES):
        zh, co, zl, y, x = index
        target = (w ^ zh, x >> 1, (x & 1) * 2 + (v ^ co), y, zl)
        pairs.append(tuple(int(np.ravel_multi_index(i, SIZES)) for i in (index, target)))
    return pairs


def runs_kernel(where, hidden, *runs):
    half = hidden.shape[1] // 2
    width = half // 4
    for j, run in enumerate(runs):
        q = lax.rem(where[0] + j, 4)
        for h in range(2):
            at = pl.ds(pl.multiple_of(h * half + q * width, width), width)
            run[:, h * width : (h + 1) * width] = hidden[:, at]


def hidden_runs(x, hidden):
    vmem = pl.BlockSpec(memory_space=pltpu.VMEM)
    return pl.pallas_call(
        runs_kernel,
        out_shape=(jax.ShapeDtypeStruct((ROWS, 512), BF),) * 4,
        in_specs=[pl.BlockSpec(memory_space=pltpu.SMEM), vmem],
        out_specs=(vmem,) * 4,
        compiler_params=pltpu.CompilerParams(vmem_limit_bytes=8 * 2**20),
        cost_estimate=pl.CostEstimate(flops=0, bytes_accessed=2 * 10**6, transcendentals=0),
    )(x.reshape(1).astype(jnp.int32), hidden)


def product_kernel(facts, hid0, hid1, hid2, hid3, *refs):
    rows, outs, acc = refs[:-5], refs[-5:-1], refs[-1]
    my_y, my_x = facts[DOCS + RANKS + 1], facts[DOCS + RANKS + 2]
    for j, hidden in enumerate((hid0, hid1, hid2, hid3)):
        run = lax.rem(my_x + 4 - j, 4)
        columns = pl.ds(pl.multiple_of(run * 256, 256), 256)
        total = None
        for i, piece in enumerate(rows):
            tokens = hidden[i * ROWS * 4 : (i + 1) * ROWS * 4, :]
            part = dot(piece[...].reshape(4 * ROWS, 2 * DH), tokens, 0, 0)
            total = part if total is None else total + part
        acc[...] = total
        for shift, out in enumerate(outs):
            y = lax.rem(my_y + shift, 4)
            for block in range(4):
                at = pl.ds(pl.multiple_of(block * 64 + y * 16, 16), 16)
                out[block, :, columns] = acc[at, :].astype(BF)


def weight_product(facts, hidden, rows):
    vmem = pl.BlockSpec(memory_space=pltpu.VMEM)
    return pl.pallas_call(
        product_kernel,
        out_shape=(jax.ShapeDtypeStruct((4, 16, 1024), BF),) * 4,
        in_specs=[pl.BlockSpec(memory_space=pltpu.SMEM)] + [vmem] * (4 + len(rows)),
        out_specs=(vmem,) * 4,
        scratch_shapes=[pltpu.VMEM((2 * DH, 256), F32)],
        compiler_params=pltpu.CompilerParams(vmem_limit_bytes=24 * 2**20),
        cost_estimate=pl.CostEstimate(flops=10**9, bytes_accessed=6 * 10**6, transcendentals=0),
    )(facts, *hidden, *rows)


def after(value, *others):
    return lax.optimization_barrier((value, others))[0]


def per_device(hidden_in, queries, keys_in, values_in, out_grad, doc_lengths, pair_perm):
    zl, y, x = (lax.axis_index(a) for a in ("zl", "y", "x"))
    zh, core = lax.axis_index("zh"), lax.axis_index("co")
    swap = [(0, 1), (1, 0)]
    facts = jnp.concatenate([doc_lengths[0], pair_perm, jnp.stack([zl, y, x]).astype(jnp.int32)])

    def moved(value, axis, shift):
        return lax.ppermute(value, axis, ring(shift))

    own = jnp.concatenate([keys_in[0], values_in[0]], axis=1)
    column = jnp.stack([own] + [moved(own, "zl", a) for a in (1, 2, 3)])
    runs = hidden_runs(x, hidden_in[0])
    runs = [runs[0]] + [moved(runs[j], "x", j) for j in (1, 2, 3)]
    kvs = [column] + [moved(column, "y", s) for s in (1, 2, 3)]

    runs = jnp.stack(after(runs, kvs[1]))
    tokens = []
    for s in range(4):
        block = lax.dynamic_index_in_dim(runs, lax.rem(x - zl - s + 8, 4), 0, False)
        tokens.append(block if s == 0 else moved(block, "zl", s))

    dq, *dkv = attention(facts, queries[0], out_grad[0], kvs)

    dkv, tokens = lax.optimization_barrier((dkv, tokens))
    got = [dkv[0]] + [moved(dkv[s], "y", s) for s in (1, 2, 3)]
    tokens = jnp.stack(tokens)
    mine = lax.dynamic_slice_in_dim(tokens, core * 256, 256, 2)
    theirs = lax.ppermute(lax.dynamic_slice_in_dim(tokens, (1 - core) * 256, 256, 2), "co", swap)
    hidden = jnp.concatenate([mine.reshape(4 * ROWS, -1), theirs.reshape(4 * ROWS, -1)], axis=0)
    hidden = after(hidden, got[1])
    hidden = [hidden] + [moved(hidden, "x", j) for j in (1, 2, 3)]

    parts = [add_up(*[g[a] for g in got]) for a in range(4)]
    parts = [parts[0]] + [moved(parts[a].astype(BF), "zl", a) for a in (1, 2, 3)]
    grads = add_up(*parts).astype(BF)

    rows = jnp.stack([grads] + [moved(grads, "zl", s) for s in (1, 2, 3)])
    rows = (rows, lax.ppermute(rows, "co", swap))
    shares = weight_product(facts, hidden, rows)
    shares = [shares[0]] + [moved(shares[s], "y", s) for s in (1, 2, 3)]
    share = add_up(*shares).astype(BF).reshape(2, 2, 16, -1)
    halves = []
    for v in range(2):
        blocks = []
        for w in range(2):
            block = lax.dynamic_index_in_dim(share, lax.rem(zh + w, 2), 0, False)
            block = lax.dynamic_index_in_dim(block, lax.rem(core + v, 2), 0, False)
            blocks.append(lax.ppermute(block, CARDINAL, owner(w, v)))
        halves.append(add_up(*blocks))
    even = lax.rem(zl, 2) == 0
    left = jnp.where(even, halves[0], halves[1])
    right = jnp.where(even, halves[1], halves[0])
    grad_weight = jnp.concatenate([left, right], axis=1)
    return dq[None], grads[None, :, :DH], grads[None, :, DH:], grad_weight


def solution(mesh):
    fine = Mesh(mesh.devices.reshape(SIZES), CARDINAL)
    dp, ctx, tp = ("zh", "co"), ("zl", "y"), "x"
    tokens = P(dp, ctx, tp)
    return jax.shard_map(
        per_device,
        mesh=fine,
        in_specs=(tokens,) * 5 + (P(dp, None), P()),
        out_specs=(tokens,) * 3 + (P(dp + ctx, tp),),
        check_vma=False,
    )
```

```python
import functools

import jax
import jax.numpy as jnp
import numpy as np
from jax import lax
from jax.experimental import pallas as pl
from jax.experimental.pallas import tpu as pltpu
from jax.sharding import Mesh, PartitionSpec as P

DH = 128
HEADS = 8
HALF = 112
ROWS = 2 * HALF
LANES = HEADS * HALF
RANKS = 16
BLOCKS = 2 * RANKS
SEQ = ROWS * RANKS
RUN = 512
DOCS = 6
MAX_DOC = 1194
SPAN = 256
STEPS = -(-(MAX_DOC - 1 + HALF) // SPAN)
PAD = SPAN
SCALE = DH**-0.5
LOG2E = 1.4426950408889634
MASKED = -1e30
CARDINAL = ("zh", "co", "zl", "y", "x")
SIZES = (2, 2, 4, 4, 4)
BF = jnp.bfloat16
F32 = jnp.float32


def dot(a, b, ca, cb):
    return lax.dot_general(a, b, (((ca,), (cb,)), ((), ())), preferred_element_type=F32)


def fold(x, op):
    return op(x.reshape(x.shape[0] // 8, 8, x.shape[1]), axis=0)


def attention_kernel(
    facts, q_hbm, do_hbm, kv0, kv1, kv2, kv3, dq_ref, out0, out1, out2, out3,
    q_ref, do_ref, sems, kbuf, vbuf, dkacc, dvacc, s_scr, dp_scr, qs, dos,
):
    loads = [
        pltpu.make_async_copy(q_hbm, q_ref, sems.at[0]),
        pltpu.make_async_copy(do_hbm, do_ref, sems.at[1]),
    ]
    for load in loads:
        load.start()

    def len_of(d):
        return facts[d]

    def pair_of(rank):
        return facts[DOCS + rank]

    my_zl = facts[DOCS + RANKS]
    my_y = facts[DOCS + RANKS + 1]

    def place(pair, half):
        block = pair if half == 0 else BLOCKS - 1 - pair
        return pl.ds(pl.multiple_of(PAD + block * HALF, 16), HALF)

    kbuf[0:PAD, :] = jnp.zeros((PAD, DH), BF)
    vbuf[0:PAD, :] = jnp.zeros((PAD, DH), BF)
    for shift, ref in enumerate((kv0, kv1, kv2, kv3)):
        src_y = lax.rem(my_y + 4 - shift, 4)
        for a in range(4):
            pair = pair_of(lax.rem(my_zl + 4 - a, 4) * 4 + src_y)
            for half in range(2):
                rows = slice(half * HALF, (half + 1) * HALF)
                kbuf[place(pair, half), :] = ref[a, rows, 0:DH]
                vbuf[place(pair, half), :] = ref[a, rows, DH : 2 * DH]
    dkacc[...] = jnp.zeros_like(dkacc)
    dvacc[...] = jnp.zeros_like(dvacc)

    ends = []
    total = jnp.int32(0)
    for d in range(DOCS - 1):
        total = total + len_of(d)
        ends.append(total)

    lane = lax.broadcasted_iota(jnp.int32, (1, LANES), 1)
    within = lane
    for h in range(1, HEADS):
        within = jnp.where(lane >= h * HALF, lane - h * HALF, within)

    for load in loads:
        load.wait()

    def one_block(half, carry):
        pair = pair_of(my_zl * 4 + my_y)
        block = jnp.where(half == 0, pair, BLOCKS - 1 - pair)
        row0 = pl.multiple_of(half * HALF, 16)
        for h in range(HEADS):
            qs[h * HALF : (h + 1) * HALF, :] = q_ref[pl.ds(row0, HALF), h * DH : (h + 1) * DH]
            dos[h * HALF : (h + 1) * HALF, :] = do_ref[pl.ds(row0, HALF), h * DH : (h + 1) * DH]
        first = block * HALF
        pos = within + first
        low = jnp.zeros_like(pos)
        low0 = jnp.int32(0)
        for end in ends:
            low = jnp.where(pos >= end, end, low)
            low0 = jnp.where(first >= end, end, low0)
        stop = first + HALF
        count = lax.div(stop - low0 + (SPAN - 1), SPAN)
        start = stop - count * SPAN

        def keys_at(t):
            return pl.ds(pl.multiple_of(PAD + start + t * SPAN, 16), SPAN)

        def kept_at(t):
            return pl.ds(pl.multiple_of(t * SPAN, SPAN), SPAN)

        def score(t, top):
            s = dot(kbuf[keys_at(t), :], qs[...], 1, 1)
            key = lax.broadcasted_iota(jnp.int32, (SPAN, LANES), 0) + (start + t * SPAN)
            s = jnp.where((key >= low) & (key <= pos), s * (SCALE * LOG2E), MASKED)
            s_scr[kept_at(t), :] = s
            return jnp.maximum(top, fold(s, jnp.max))

        top = lax.fori_loop(0, count, score, jnp.full((8, LANES), MASKED, F32))
        top = jnp.max(top, axis=0, keepdims=True)

        def weigh(t, sums):
            mass, moment = sums
            e = jnp.exp2(s_scr[kept_at(t), :] - top)
            dp = dot(vbuf[keys_at(t), :], dos[...], 1, 1)
            s_scr[kept_at(t), :] = e
            dp_scr[kept_at(t), :] = dp
            return mass + fold(e, jnp.sum), moment + fold(e * dp, jnp.sum)

        zero = jnp.zeros((8, LANES), F32)
        mass, moment = lax.fori_loop(0, count, weigh, (zero, zero))
        inverse = 1.0 / jnp.sum(mass, axis=0, keepdims=True)
        delta = jnp.sum(moment, axis=0, keepdims=True) * inverse

        def spread(t, dqt):
            p = s_scr[kept_at(t), :] * inverse
            g = (p * (dp_scr[kept_at(t), :] - delta)).astype(BF)
            at = keys_at(t)
            dvacc[at, :] += dot(p.astype(BF), dos[...], 1, 0)
            dkacc[at, :] += dot(g, qs[...], 1, 0)
            return dqt + dot(kbuf[at, :], g, 0, 0)

        dqt = lax.fori_loop(0, count, spread, jnp.zeros((DH, LANES), F32))
        dq = (dqt * SCALE).T.astype(BF)
        for h in range(HEADS):
            dq_ref[pl.ds(row0, HALF), h * DH : (h + 1) * DH] = dq[h * HALF : (h + 1) * HALF, :]
        return carry

    lax.fori_loop(0, 2, one_block, 0)

    for shift, ref in enumerate((out0, out1, out2, out3)):
        y = lax.rem(my_y + shift, 4)
        for a in range(4):
            pair = pair_of(lax.rem(my_zl + a, 4) * 4 + y)
            for half in range(2):
                at = place(pair, half)
                rows = slice(half * HALF, (half + 1) * HALF)
                ref[a, rows, 0:DH] = (dkacc[at, :] * SCALE).astype(BF)
                ref[a, rows, DH : 2 * DH] = dvacc[at, :].astype(BF)


def attention(facts, q, do, kvs):
    vmem = pl.BlockSpec(memory_space=pltpu.VMEM)
    hbm = pl.BlockSpec(memory_space=pltpu.HBM)
    return pl.pallas_call(
        attention_kernel,
        out_shape=(jax.ShapeDtypeStruct((ROWS, HEADS * DH), BF),)
        + (jax.ShapeDtypeStruct((4, ROWS, 2 * DH), BF),) * 4,
        in_specs=[pl.BlockSpec(memory_space=pltpu.SMEM), hbm, hbm] + [vmem] * 4,
        out_specs=(vmem,) * 5,
        scratch_shapes=[
            pltpu.VMEM((ROWS, HEADS * DH), BF),
            pltpu.VMEM((ROWS, HEADS * DH), BF),
            pltpu.SemaphoreType.DMA((2,)),
            pltpu.VMEM((PAD + SEQ, DH), BF),
            pltpu.VMEM((PAD + SEQ, DH), BF),
            pltpu.VMEM((PAD + SEQ, DH), F32),
            pltpu.VMEM((PAD + SEQ, DH), F32),
            pltpu.VMEM((STEPS * SPAN, LANES), F32),
            pltpu.VMEM((STEPS * SPAN, LANES), F32),
            pltpu.VMEM((LANES, DH), BF),
            pltpu.VMEM((LANES, DH), BF),
        ],
        compiler_params=pltpu.CompilerParams(vmem_limit_bytes=40 * 2**20),
        cost_estimate=pl.CostEstimate(
            flops=6 * 10**9, bytes_accessed=6 * 10**6, transcendentals=3 * 10**6
        ),
    )(facts, q, do, *kvs)


def ring(shift):
    return [(i, (i + shift) % 4) for i in range(4)]


def add_up(*xs):
    return functools.reduce(lambda a, b: a + b, [x.astype(F32) for x in xs])


def owner(w, v):
    pairs = []
    for index in np.ndindex(*SIZES):
        zh, co, zl, y, x = index
        target = (w ^ zh, x >> 1, (x & 1) * 2 + (v ^ co), y, zl)
        pairs.append(tuple(int(np.ravel_multi_index(i, SIZES)) for i in (index, target)))
    return pairs


def first_kernel(where, keys, values, hidden, own, *runs):
    own[:, 0:DH] = keys[...]
    own[:, DH : 2 * DH] = values[...]
    for j, run in enumerate(runs):
        q = lax.rem(where[0] + j, 4)
        run[...] = hidden[:, pl.ds(pl.multiple_of(q * RUN, RUN), RUN)]


def first_messages(x, keys, values, hidden):
    vmem = pl.BlockSpec(memory_space=pltpu.VMEM)
    return pl.pallas_call(
        first_kernel,
        out_shape=(jax.ShapeDtypeStruct((ROWS, 2 * DH), BF),)
        + (jax.ShapeDtypeStruct((ROWS, RUN), BF),) * 4,
        in_specs=[pl.BlockSpec(memory_space=pltpu.SMEM)] + [vmem] * 3,
        out_specs=(vmem,) * 5,
        compiler_params=pltpu.CompilerParams(vmem_limit_bytes=8 * 2**20),
        cost_estimate=pl.CostEstimate(flops=0, bytes_accessed=2 * 10**6, transcendentals=0),
    )(x.reshape(1).astype(jnp.int32), keys, values, hidden)


def product_kernel(facts, hid0, hid1, hid2, hid3, rows, kept, sent, acc):
    my_y, my_x, core = (facts[DOCS + RANKS + i] for i in (1, 2, 3))
    for j, hidden in enumerate((hid0, hid1, hid2, hid3)):
        run = lax.rem(my_x + 4 - j, 4)
        half, place = run // 2, lax.rem(run, 2)
        columns = pl.ds(pl.multiple_of(place * RUN, RUN), RUN)
        acc[...] = dot(rows[...].reshape(4 * ROWS, 2 * DH), hidden[...], 0, 0)

        def store(out):
            for shift in range(4):
                y = lax.rem(my_y + shift, 4)
                for block in range(4):
                    at = pl.ds(pl.multiple_of(block * 64 + y * 16, 16), 16)
                    out[shift, block, :, columns] = acc[at, :].astype(BF)

        @pl.when(half == core)
        def _():
            store(kept)

        @pl.when(half != core)
        def _():
            store(sent)


def weight_product(facts, hidden, rows):
    vmem = pl.BlockSpec(memory_space=pltpu.VMEM)
    return pl.pallas_call(
        product_kernel,
        out_shape=(jax.ShapeDtypeStruct((4, 4, 16, 2 * RUN), BF),) * 2,
        in_specs=[pl.BlockSpec(memory_space=pltpu.SMEM)] + [vmem] * 5,
        out_specs=(vmem,) * 2,
        scratch_shapes=[pltpu.VMEM((2 * DH, RUN), F32)],
        compiler_params=pltpu.CompilerParams(vmem_limit_bytes=24 * 2**20),
        cost_estimate=pl.CostEstimate(flops=10**9, bytes_accessed=6 * 10**6, transcendentals=0),
    )(facts, *hidden, rows)


def after(value, *others):
    return lax.optimization_barrier((value, others))[0]


def per_device(hidden_in, queries, keys_in, values_in, out_grad, doc_lengths, pair_perm):
    zl, y, x = (lax.axis_index(a) for a in ("zl", "y", "x"))
    zh, core = lax.axis_index("zh"), lax.axis_index("co")
    swap = [(0, 1), (1, 0)]
    facts = jnp.concatenate([doc_lengths[0], pair_perm, jnp.stack([zl, y, x, core]).astype(jnp.int32)])

    def moved(value, axis, shift):
        return lax.ppermute(value, axis, ring(shift))

    own, *runs = first_messages(x, keys_in[0], values_in[0], hidden_in[0])
    column = jnp.stack([own] + [moved(own, "zl", a) for a in (1, 2, 3)])
    runs = [runs[0]] + [moved(runs[j], "x", j) for j in (1, 2, 3)]
    column, runs = lax.optimization_barrier((column, runs))
    kvs = [column] + [moved(column, "y", s) for s in (1, 2, 3)]

    runs = jnp.stack(after(runs, kvs[1]))
    tokens = []
    for s in range(4):
        block = lax.dynamic_index_in_dim(runs, lax.rem(x - zl - s + 8, 4), 0, False)
        tokens.append(block if s == 0 else moved(block, "zl", s))

    dq, *dkv = attention(facts, queries[0], out_grad[0], kvs)

    got = [dkv[0]] + [moved(dkv[s], "y", s) for s in (1, 2, 3)]
    hidden = jnp.stack(after(tokens, dkv)).reshape(4 * ROWS, RUN)
    hidden = [hidden] + [moved(hidden, "x", j) for j in (1, 2, 3)]

    parts = [add_up(*[g[a] for g in got]) for a in range(4)]
    parts = [parts[0]] + [moved(parts[a].astype(BF), "zl", a) for a in (1, 2, 3)]
    grads = add_up(*parts).astype(BF)

    rows = jnp.stack([grads] + [moved(grads, "zl", s) for s in (1, 2, 3)])
    kept, sent = weight_product(facts, hidden, rows)
    sent = lax.ppermute(sent, "co", swap)
    shares = [add_up(kept[s], sent[s]).astype(BF) for s in range(4)]
    shares = [shares[0]] + [moved(shares[s], "y", s) for s in (1, 2, 3)]
    share = add_up(*shares).astype(BF).reshape(2, 2, 16, -1)
    halves = []
    for v in range(2):
        blocks = []
        for w in range(2):
            block = lax.dynamic_index_in_dim(share, lax.rem(zh + w, 2), 0, False)
            block = lax.dynamic_index_in_dim(block, lax.rem(core + v, 2), 0, False)
            blocks.append(lax.ppermute(block, CARDINAL, owner(w, v)))
        halves.append(add_up(*blocks))
    even = lax.rem(zl, 2) == 0
    left = jnp.where(even, halves[0], halves[1])
    right = jnp.where(even, halves[1], halves[0])
    grad_weight = jnp.concatenate([left, right], axis=1)
    return dq[None], grads[None, :, :DH], grads[None, :, DH:], grad_weight


def solution(mesh):
    fine = Mesh(mesh.devices.reshape(SIZES), CARDINAL)
    dp, ctx, tp = ("zh", "co"), ("zl", "y"), "x"
    tokens = P(dp, ctx, tp)
    return jax.shard_map(
        per_device,
        mesh=fine,
        in_specs=(tokens,) * 5 + (P(dp, None), P()),
        out_specs=(tokens,) * 3 + (P(dp + ctx, tp),),
        check_vma=False,
    )
```

```python
import functools

import jax
import jax.numpy as jnp
import numpy as np
from jax import lax
from jax.experimental import pallas as pl
from jax.experimental.pallas import tpu as pltpu
from jax.sharding import Mesh, PartitionSpec as P

DH = 128
HEADS = 8
HALF = 112
ROWS = 2 * HALF
LANES = HEADS * HALF
RANKS = 16
BLOCKS = 2 * RANKS
SEQ = ROWS * RANKS
DOCS = 6
MAX_DOC = 1194
SPAN = 256
STEPS = -(-(MAX_DOC - 1 + HALF) // SPAN)
PAD = SPAN
SCALE = DH**-0.5
LOG2E = 1.4426950408889634
MASKED = -1e30
CARDINAL = ("zh", "co", "zl", "y", "x")
SIZES = (2, 2, 4, 4, 4)
BF = jnp.bfloat16
F32 = jnp.float32


def dot(a, b, ca, cb):
    return lax.dot_general(a, b, (((ca,), (cb,)), ((), ())), preferred_element_type=F32)


def fold(x, op):
    return op(x.reshape(x.shape[0] // 8, 8, x.shape[1]), axis=0)


class Place:
    def __init__(self, facts):
        self.facts = facts
        self.zl, self.y = facts[DOCS + RANKS], facts[DOCS + RANKS + 1]

    def pair(self, rank):
        return self.facts[DOCS + rank]

    def rows(self, zl, y, half):
        pair = self.pair(zl * 4 + y)
        block = pair if half == 0 else BLOCKS - 1 - pair
        return pl.ds(pl.multiple_of(PAD + block * HALF, 16), HALF)

    def gather(self, refs, buf):
        buf[0:PAD, :] = jnp.zeros((PAD, DH), BF)
        for s, ref in enumerate(refs):
            for a in range(4):
                zl, y = lax.rem(self.zl + 4 - a, 4), lax.rem(self.y + 4 - s, 4)
                for half in range(2):
                    rows = slice(half * HALF, (half + 1) * HALF)
                    buf[self.rows(zl, y, half), :] = ref[a, rows, :]

    def scatter(self, acc, refs, scale):
        for s, ref in enumerate(refs):
            for a in range(4):
                zl, y = lax.rem(self.zl + a, 4), lax.rem(self.y + s, 4)
                for half in range(2):
                    rows = slice(half * HALF, (half + 1) * HALF)
                    ref[a, rows, :] = (acc[self.rows(zl, y, half), :] * scale).astype(BF)


class Window:
    def __init__(self, place, half):
        pair = place.pair(place.zl * 4 + place.y)
        block = jnp.where(half == 0, pair, BLOCKS - 1 - pair)
        lane = lax.broadcasted_iota(jnp.int32, (1, LANES), 1)
        within = lane
        for h in range(1, HEADS):
            within = jnp.where(lane >= h * HALF, lane - h * HALF, within)
        first = block * HALF
        self.pos = within + first
        self.low = jnp.zeros_like(self.pos)
        low0 = jnp.int32(0)
        end = jnp.int32(0)
        for d in range(DOCS - 1):
            end = end + place.facts[d]
            self.low = jnp.where(self.pos >= end, end, self.low)
            low0 = jnp.where(first >= end, end, low0)
        stop = first + HALF
        self.count = lax.div(stop - low0 + (SPAN - 1), SPAN)
        self.start = stop - self.count * SPAN

    def keys(self, t):
        return pl.ds(pl.multiple_of(PAD + self.start + t * SPAN, 16), SPAN)

    def kept(self, t):
        return pl.ds(pl.multiple_of(t * SPAN, SPAN), SPAN)

    def scores(self, t, kbuf, qs):
        s = dot(kbuf[self.keys(t), :], qs[...], 1, 1) * (SCALE * LOG2E)
        key = lax.broadcasted_iota(jnp.int32, (SPAN, LANES), 0) + (self.start + t * SPAN)
        return jnp.where((key >= self.low) & (key <= self.pos), s, MASKED)


def heads_apart(ref, half, stack):
    row0 = pl.multiple_of(half * HALF, 16)
    for h in range(HEADS):
        stack[h * HALF : (h + 1) * HALF, :] = ref[pl.ds(row0, HALF), h * DH : (h + 1) * DH]


def forward_kernel(
    facts, q_ref, do_ref, k0, k1, k2, k3, stats, out0, out1, out2, out3,
    kbuf, dvacc, s_scr, qs, dos,
):
    place = Place(facts)
    place.gather((k0, k1, k2, k3), kbuf)
    dvacc[...] = jnp.zeros_like(dvacc)

    def one_block(half, carry):
        heads_apart(q_ref, half, qs)
        heads_apart(do_ref, half, dos)
        window = Window(place, half)

        def score(t, top):
            s = window.scores(t, kbuf, qs)
            s_scr[window.kept(t), :] = s
            return jnp.maximum(top, fold(s, jnp.max))

        top = lax.fori_loop(0, window.count, score, jnp.full((8, LANES), MASKED, F32))
        top = jnp.max(top, axis=0, keepdims=True)

        def weigh(t, mass):
            e = jnp.exp2(s_scr[window.kept(t), :] - top)
            s_scr[window.kept(t), :] = e
            return mass + fold(e, jnp.sum)

        mass = lax.fori_loop(0, window.count, weigh, jnp.zeros((8, LANES), F32))
        inverse = 1.0 / jnp.sum(mass, axis=0, keepdims=True)

        def spread(t, carry):
            p = (s_scr[window.kept(t), :] * inverse).astype(BF)
            dvacc[window.keys(t), :] += dot(p, dos[...], 1, 0)
            return carry

        lax.fori_loop(0, window.count, spread, 0)
        stats[2 * half] = top
        stats[2 * half + 1] = inverse
        return carry

    lax.fori_loop(0, 2, one_block, 0)
    place.scatter(dvacc, (out0, out1, out2, out3), 1.0)


def backward_kernel(
    facts, q_ref, do_ref, k0, k1, k2, k3, v0, v1, v2, v3, stats,
    dq_ref, out0, out1, out2, out3,
    kbuf, vbuf, dkacc, p_scr, dp_scr, qs, dos,
):
    place = Place(facts)
    place.gather((k0, k1, k2, k3), kbuf)
    place.gather((v0, v1, v2, v3), vbuf)
    dkacc[...] = jnp.zeros_like(dkacc)

    def one_block(half, carry):
        heads_apart(q_ref, half, qs)
        heads_apart(do_ref, half, dos)
        window = Window(place, half)
        top, inverse = stats[2 * half], stats[2 * half + 1]

        def weigh(t, moment):
            p = jnp.exp2(window.scores(t, kbuf, qs) - top) * inverse
            dp = dot(vbuf[window.keys(t), :], dos[...], 1, 1)
            p_scr[window.kept(t), :] = p
            dp_scr[window.kept(t), :] = dp
            return moment + fold(p * dp, jnp.sum)

        moment = lax.fori_loop(0, window.count, weigh, jnp.zeros((8, LANES), F32))
        delta = jnp.sum(moment, axis=0, keepdims=True)

        def spread(t, dqt):
            g = (p_scr[window.kept(t), :] * (dp_scr[window.kept(t), :] - delta)).astype(BF)
            at = window.keys(t)
            dkacc[at, :] += dot(g, qs[...], 1, 0)
            return dqt + dot(kbuf[at, :], g, 0, 0)

        dqt = lax.fori_loop(0, window.count, spread, jnp.zeros((DH, LANES), F32))
        dq = (dqt * SCALE).T.astype(BF)
        row0 = pl.multiple_of(half * HALF, 16)
        for h in range(HEADS):
            dq_ref[pl.ds(row0, HALF), h * DH : (h + 1) * DH] = dq[h * HALF : (h + 1) * HALF, :]
        return carry

    lax.fori_loop(0, 2, one_block, 0)
    place.scatter(dkacc, (out0, out1, out2, out3), SCALE)


SHARES = (jax.ShapeDtypeStruct((4, ROWS, DH), BF),) * 4


def forward(facts, q, do, ks):
    vmem = pl.BlockSpec(memory_space=pltpu.VMEM)
    return pl.pallas_call(
        forward_kernel,
        out_shape=(jax.ShapeDtypeStruct((4, 1, LANES), F32),) + SHARES,
        in_specs=[pl.BlockSpec(memory_space=pltpu.SMEM)] + [vmem] * 6,
        out_specs=(vmem,) * 5,
        scratch_shapes=[
            pltpu.VMEM((PAD + SEQ, DH), BF),
            pltpu.VMEM((PAD + SEQ, DH), F32),
            pltpu.VMEM((STEPS * SPAN, LANES), F32),
            pltpu.VMEM((LANES, DH), BF),
            pltpu.VMEM((LANES, DH), BF),
        ],
        compiler_params=pltpu.CompilerParams(vmem_limit_bytes=32 * 2**20),
        cost_estimate=pl.CostEstimate(
            flops=3 * 10**9, bytes_accessed=4 * 10**6, transcendentals=2 * 10**6
        ),
    )(facts, q, do, *ks)


def backward(facts, q, do, ks, vs, stats):
    vmem = pl.BlockSpec(memory_space=pltpu.VMEM)
    return pl.pallas_call(
        backward_kernel,
        out_shape=(jax.ShapeDtypeStruct((ROWS, HEADS * DH), BF),) + SHARES,
        in_specs=[pl.BlockSpec(memory_space=pltpu.SMEM)] + [vmem] * 11,
        out_specs=(vmem,) * 5,
        scratch_shapes=[
            pltpu.VMEM((PAD + SEQ, DH), BF),
            pltpu.VMEM((PAD + SEQ, DH), BF),
            pltpu.VMEM((PAD + SEQ, DH), F32),
            pltpu.VMEM((STEPS * SPAN, LANES), F32),
            pltpu.VMEM((STEPS * SPAN, LANES), F32),
            pltpu.VMEM((LANES, DH), BF),
            pltpu.VMEM((LANES, DH), BF),
        ],
        compiler_params=pltpu.CompilerParams(vmem_limit_bytes=32 * 2**20),
        cost_estimate=pl.CostEstimate(
            flops=5 * 10**9, bytes_accessed=5 * 10**6, transcendentals=2 * 10**6
        ),
    )(facts, q, do, *ks, *vs, stats)


def ring(shift):
    return [(i, (i + shift) % 4) for i in range(4)]


def add_up(*xs):
    return functools.reduce(lambda a, b: a + b, [x.astype(F32) for x in xs])


def copy_kernel(*refs):
    for source, target in zip(refs[: len(refs) // 2], refs[len(refs) // 2 :]):
        target[...] = source[...]


def near(*arrays):
    vmem = pl.BlockSpec(memory_space=pltpu.VMEM)
    return pl.pallas_call(
        copy_kernel,
        out_shape=tuple(jax.ShapeDtypeStruct(a.shape, a.dtype) for a in arrays),
        in_specs=[vmem] * len(arrays),
        out_specs=(vmem,) * len(arrays),
        compiler_params=pltpu.CompilerParams(vmem_limit_bytes=16 * 2**20),
    )(*arrays)


def columns_kernel(c0, c1, c2, c3, keys, values):
    for a, ref in enumerate((c0, c1, c2, c3)):
        keys[a] = ref[:, 0:DH]
        values[a] = ref[:, DH : 2 * DH]


def columns_of(pieces):
    vmem = pl.BlockSpec(memory_space=pltpu.VMEM)
    return pl.pallas_call(
        columns_kernel,
        out_shape=SHARES[:2],
        in_specs=[vmem] * 4,
        out_specs=(vmem,) * 2,
        compiler_params=pltpu.CompilerParams(vmem_limit_bytes=16 * 2**20),
    )(*pieces)


def product_kernel(facts, mine, theirs, own, other, row1, row2, row3, out0, out1, out2, out3, acc):
    my_zl, my_y, my_x, core = (facts[DOCS + RANKS + i] for i in range(4))
    for j, row in enumerate(((own, other), row1, row2, row3)):
        group = lax.rem(my_x + 4 - j, 4)

        @pl.when(group // 2 == core)
        def _():
            if j == 0:
                first, second = own[...], other[...]
            else:
                first, second = row[0:ROWS, :], row[ROWS : 2 * ROWS, :]
            for c in range(4):
                columns = slice(c * 512, (c + 1) * 512)
                acc[...] = dot(first, mine[:, columns], 0, 0) + dot(second, theirs[:, columns], 0, 0)
                for s, out in enumerate((out0, out1, out2, out3)):
                    y = lax.rem(my_y + s, 4)
                    for low in range(2):
                        at = pl.ds(pl.multiple_of(low * 64 + y * 16, 16), 16)
                        a = lax.rem(lax.rem(group, 2) * 2 + low + 4 - my_zl, 4)
                        out[a, :, columns] = acc[at, :].astype(BF)


def weight_product(facts, *operands):
    vmem = pl.BlockSpec(memory_space=pltpu.VMEM)
    return pl.pallas_call(
        product_kernel,
        out_shape=(jax.ShapeDtypeStruct((4, 16, 2048), BF),) * 4,
        in_specs=[pl.BlockSpec(memory_space=pltpu.SMEM)] + [vmem] * 7,
        out_specs=(vmem,) * 4,
        scratch_shapes=[pltpu.VMEM((DH, 512), F32)],
        compiler_params=pltpu.CompilerParams(vmem_limit_bytes=24 * 2**20),
        cost_estimate=pl.CostEstimate(flops=10**9, bytes_accessed=4 * 10**6, transcendentals=0),
    )(facts, *operands)


def after(value, *others):
    return lax.optimization_barrier((value, others))[0]


def per_device(hidden_in, queries, keys_in, values_in, out_grad, doc_lengths, pair_perm):
    zl, y, x = (lax.axis_index(a) for a in ("zl", "y", "x"))
    zh, core = lax.axis_index("zh"), lax.axis_index("co")
    swap = [(0, 1), (1, 0)]
    facts = jnp.concatenate([doc_lengths[0], pair_perm, jnp.stack([zl, y, x, core]).astype(jnp.int32)])

    def moved(value, axis, shift):
        return lax.ppermute(value, axis, ring(shift))

    own = jnp.concatenate([keys_in[0], values_in[0]], axis=1)
    pieces = [own] + [moved(own, "zl", a) for a in (1, 2, 3)]
    rows_in = near(queries[0], out_grad[0])
    hidden = hidden_in[0]
    hidden = (hidden, lax.ppermute(hidden, "co", swap))
    pieces, rows_in, hidden = lax.optimization_barrier((pieces, rows_in, hidden))
    ks, vs = columns_of(pieces)
    ks = [ks] + [moved(ks, "y", s) for s in (1, 2, 3)]
    vs = after(vs, ks[1])
    vs = [vs] + [moved(vs, "y", s) for s in (1, 2, 3)]

    def received(shares):
        return [shares[0]] + [moved(shares[s], "y", s) for s in (1, 2, 3)]

    def summed(got):
        parts = [add_up(*[g[a] for g in got]) for a in range(4)]
        return add_up(parts[0], *[moved(parts[a].astype(BF), "zl", a) for a in (1, 2, 3)])

    cross = [
        (x0 + 4 * c, x0 + 4 * (1 - c)) for c in range(2) for x0 in range(4) if x0 // 2 == 1 - c
    ]

    def along(j):
        return [
            (x0 + 4 * c, (x0 + j) % 4 + 4 * c) for c in range(2) for x0 in range(4) if x0 // 2 == c
        ]

    def product(grads):
        other = lax.ppermute(grads, ("co", "x"), cross)
        both = jnp.concatenate([grads, other], axis=0)
        rows = [lax.ppermute(both, ("co", "x"), along(j)) for j in (1, 2, 3)]
        return weight_product(facts, *hidden, grads, other, *rows)

    stats, *dvs = forward(facts, *rows_in, ks)
    dvs = received(dvs)
    dq, *dks = backward(facts, *rows_in, ks, vs, stats)
    dks = received(after(dks, dvs))
    value_grads = summed(dvs).astype(BF)
    key_grads = summed(dks).astype(BF)
    value_weight = summed(received(product(value_grads)))
    key_weight = summed(received(product(key_grads)))
    kept = jnp.where(zh == 0, key_weight, value_weight)
    sent = jnp.where(zh == 0, value_weight, key_weight).astype(BF)
    grad_weight = kept + lax.ppermute(sent, "zh", swap).astype(F32)
    return dq[None], key_grads[None], value_grads[None], grad_weight


def solution(mesh):
    fine = Mesh(mesh.devices.reshape(SIZES), CARDINAL)
    dp, ctx, tp = ("zh", "co"), ("zl", "y"), "x"
    tokens = P(dp, ctx, tp)
    return jax.shard_map(
        per_device,
        mesh=fine,
        in_specs=(tokens,) * 5 + (P(dp, None), P()),
        out_specs=(tokens,) * 3 + (P(dp + ctx, tp),),
        check_vma=False,
    )
```

```python
import functools

import jax
import jax.numpy as jnp
import numpy as np
from jax import lax
from jax.experimental import pallas as pl
from jax.experimental.pallas import tpu as pltpu
from jax.sharding import Mesh, PartitionSpec as P

DH = 128
HEADS = 8
HALF = 112
ROWS = 2 * HALF
LANES = HEADS * HALF
RANKS = 16
BLOCKS = 2 * RANKS
SEQ = ROWS * RANKS
DOCS = 6
MAX_DOC = 1194
SPAN = 256
STEPS = -(-(MAX_DOC - 1 + HALF) // SPAN)
PAD = SPAN
SCALE = DH**-0.5
LOG2E = 1.4426950408889634
MASKED = -1e30
CARDINAL = ("zh", "co", "zl", "y", "x")
SIZES = (2, 2, 4, 4, 4)
BF = jnp.bfloat16
F32 = jnp.float32


def dot(a, b, ca, cb):
    return lax.dot_general(a, b, (((ca,), (cb,)), ((), ())), preferred_element_type=F32)


def fold(x, op):
    return op(x.reshape(x.shape[0] // 8, 8, x.shape[1]), axis=0)


class Place:
    def __init__(self, facts):
        self.facts = facts
        self.zl, self.y = facts[DOCS + RANKS], facts[DOCS + RANKS + 1]

    def pair(self, rank):
        return self.facts[DOCS + rank]

    def rows(self, zl, y, half):
        pair = self.pair(zl * 4 + y)
        block = pair if half == 0 else BLOCKS - 1 - pair
        return pl.ds(pl.multiple_of(PAD + block * HALF, 16), HALF)

    def gather(self, refs, buf):
        buf[0:PAD, :] = jnp.zeros((PAD, DH), BF)
        for s, ref in enumerate(refs):
            for a in range(4):
                zl, y = lax.rem(self.zl + 4 - a, 4), lax.rem(self.y + 4 - s, 4)
                for half in range(2):
                    rows = slice(half * HALF, (half + 1) * HALF)
                    buf[self.rows(zl, y, half), :] = ref[a, rows, :]

    def scatter(self, acc, refs, scale):
        for s, ref in enumerate(refs):
            for a in range(4):
                zl, y = lax.rem(self.zl + a, 4), lax.rem(self.y + s, 4)
                for half in range(2):
                    rows = slice(half * HALF, (half + 1) * HALF)
                    ref[a, rows, :] = (acc[self.rows(zl, y, half), :] * scale).astype(BF)


class Window:
    def __init__(self, place, half):
        pair = place.pair(place.zl * 4 + place.y)
        block = jnp.where(half == 0, pair, BLOCKS - 1 - pair)
        lane = lax.broadcasted_iota(jnp.int32, (1, LANES), 1)
        within = lane
        for h in range(1, HEADS):
            within = jnp.where(lane >= h * HALF, lane - h * HALF, within)
        first = block * HALF
        self.pos = within + first
        self.low = jnp.zeros_like(self.pos)
        low0 = jnp.int32(0)
        end = jnp.int32(0)
        for d in range(DOCS - 1):
            end = end + place.facts[d]
            self.low = jnp.where(self.pos >= end, end, self.low)
            low0 = jnp.where(first >= end, end, low0)
        stop = first + HALF
        self.count = lax.div(stop - low0 + (SPAN - 1), SPAN)
        self.start = stop - self.count * SPAN

    def keys(self, t):
        return pl.ds(pl.multiple_of(PAD + self.start + t * SPAN, 16), SPAN)

    def kept(self, t):
        return pl.ds(pl.multiple_of(t * SPAN, SPAN), SPAN)

    def scores(self, t, kbuf, qs):
        s = dot(kbuf[self.keys(t), :], qs[...], 1, 1) * (SCALE * LOG2E)
        key = lax.broadcasted_iota(jnp.int32, (SPAN, LANES), 0) + (self.start + t * SPAN)
        return jnp.where((key >= self.low) & (key <= self.pos), s, MASKED)


def heads_apart(ref, half, stack):
    row0 = pl.multiple_of(half * HALF, 16)
    for h in range(HEADS):
        stack[h * HALF : (h + 1) * HALF, :] = ref[pl.ds(row0, HALF), h * DH : (h + 1) * DH]


def forward_kernel(
    facts, q_ref, do_ref, k0, k1, k2, k3, stats, out0, out1, out2, out3,
    kbuf, dvacc, s_scr, qs, dos,
):
    place = Place(facts)
    place.gather((k0, k1, k2, k3), kbuf)
    dvacc[...] = jnp.zeros_like(dvacc)

    def one_block(half, carry):
        heads_apart(q_ref, half, qs)
        heads_apart(do_ref, half, dos)
        window = Window(place, half)

        def score(t, top):
            s = window.scores(t, kbuf, qs)
            s_scr[window.kept(t), :] = s
            return jnp.maximum(top, fold(s, jnp.max))

        top = lax.fori_loop(0, window.count, score, jnp.full((8, LANES), MASKED, F32))
        top = jnp.max(top, axis=0, keepdims=True)

        def weigh(t, mass):
            e = jnp.exp2(s_scr[window.kept(t), :] - top)
            s_scr[window.kept(t), :] = e
            return mass + fold(e, jnp.sum)

        mass = lax.fori_loop(0, window.count, weigh, jnp.zeros((8, LANES), F32))
        inverse = 1.0 / jnp.sum(mass, axis=0, keepdims=True)

        def spread(t, carry):
            p = (s_scr[window.kept(t), :] * inverse).astype(BF)
            dvacc[window.keys(t), :] += dot(p, dos[...], 1, 0)
            return carry

        lax.fori_loop(0, window.count, spread, 0)
        stats[2 * half] = top
        stats[2 * half + 1] = inverse
        return carry

    lax.fori_loop(0, 2, one_block, 0)
    place.scatter(dvacc, (out0, out1, out2, out3), 1.0)


def backward_kernel(
    facts, q_ref, do_ref, k0, k1, k2, k3, v0, v1, v2, v3, stats,
    dq_ref, out0, out1, out2, out3,
    kbuf, vbuf, dkacc, p_scr, dp_scr, qs, dos,
):
    place = Place(facts)
    place.gather((k0, k1, k2, k3), kbuf)
    place.gather((v0, v1, v2, v3), vbuf)
    dkacc[...] = jnp.zeros_like(dkacc)

    def one_block(half, carry):
        heads_apart(q_ref, half, qs)
        heads_apart(do_ref, half, dos)
        window = Window(place, half)
        top, inverse = stats[2 * half], stats[2 * half + 1]

        def weigh(t, moment):
            p = jnp.exp2(window.scores(t, kbuf, qs) - top) * inverse
            dp = dot(vbuf[window.keys(t), :], dos[...], 1, 1)
            p_scr[window.kept(t), :] = p
            dp_scr[window.kept(t), :] = dp
            return moment + fold(p * dp, jnp.sum)

        moment = lax.fori_loop(0, window.count, weigh, jnp.zeros((8, LANES), F32))
        delta = jnp.sum(moment, axis=0, keepdims=True)

        def spread(t, dqt):
            g = (p_scr[window.kept(t), :] * (dp_scr[window.kept(t), :] - delta)).astype(BF)
            at = window.keys(t)
            dkacc[at, :] += dot(g, qs[...], 1, 0)
            return dqt + dot(kbuf[at, :], g, 0, 0)

        dqt = lax.fori_loop(0, window.count, spread, jnp.zeros((DH, LANES), F32))
        dq = (dqt * SCALE).T.astype(BF)
        row0 = pl.multiple_of(half * HALF, 16)
        for h in range(HEADS):
            dq_ref[pl.ds(row0, HALF), h * DH : (h + 1) * DH] = dq[h * HALF : (h + 1) * HALF, :]
        return carry

    lax.fori_loop(0, 2, one_block, 0)
    place.scatter(dkacc, (out0, out1, out2, out3), SCALE)


SHARES = (jax.ShapeDtypeStruct((4, ROWS, DH), BF),) * 4


def forward(facts, q, do, ks):
    vmem = pl.BlockSpec(memory_space=pltpu.VMEM)
    return pl.pallas_call(
        forward_kernel,
        out_shape=(jax.ShapeDtypeStruct((4, 1, LANES), F32),) + SHARES,
        in_specs=[pl.BlockSpec(memory_space=pltpu.SMEM)] + [vmem] * 6,
        out_specs=(vmem,) * 5,
        scratch_shapes=[
            pltpu.VMEM((PAD + SEQ, DH), BF),
            pltpu.VMEM((PAD + SEQ, DH), F32),
            pltpu.VMEM((STEPS * SPAN, LANES), F32),
            pltpu.VMEM((LANES, DH), BF),
            pltpu.VMEM((LANES, DH), BF),
        ],
        compiler_params=pltpu.CompilerParams(vmem_limit_bytes=32 * 2**20),
        cost_estimate=pl.CostEstimate(
            flops=3 * 10**9, bytes_accessed=4 * 10**6, transcendentals=2 * 10**6
        ),
    )(facts, q, do, *ks)


def backward(facts, q, do, ks, vs, stats):
    vmem = pl.BlockSpec(memory_space=pltpu.VMEM)
    return pl.pallas_call(
        backward_kernel,
        out_shape=(jax.ShapeDtypeStruct((ROWS, HEADS * DH), BF),) + SHARES,
        in_specs=[pl.BlockSpec(memory_space=pltpu.SMEM)] + [vmem] * 11,
        out_specs=(vmem,) * 5,
        scratch_shapes=[
            pltpu.VMEM((PAD + SEQ, DH), BF),
            pltpu.VMEM((PAD + SEQ, DH), BF),
            pltpu.VMEM((PAD + SEQ, DH), F32),
            pltpu.VMEM((STEPS * SPAN, LANES), F32),
            pltpu.VMEM((STEPS * SPAN, LANES), F32),
            pltpu.VMEM((LANES, DH), BF),
            pltpu.VMEM((LANES, DH), BF),
        ],
        compiler_params=pltpu.CompilerParams(vmem_limit_bytes=32 * 2**20),
        cost_estimate=pl.CostEstimate(
            flops=5 * 10**9, bytes_accessed=5 * 10**6, transcendentals=2 * 10**6
        ),
    )(facts, q, do, *ks, *vs, stats)


def ring(shift):
    return [(i, (i + shift) % 4) for i in range(4)]


def add_up(*xs):
    return functools.reduce(lambda a, b: a + b, [x.astype(F32) for x in xs])


def copy_kernel(*refs):
    for source, target in zip(refs[: len(refs) // 2], refs[len(refs) // 2 :]):
        target[...] = source[...]


def near(*arrays):
    vmem = pl.BlockSpec(memory_space=pltpu.VMEM)
    return pl.pallas_call(
        copy_kernel,
        out_shape=tuple(jax.ShapeDtypeStruct(a.shape, a.dtype) for a in arrays),
        in_specs=[vmem] * len(arrays),
        out_specs=(vmem,) * len(arrays),
        compiler_params=pltpu.CompilerParams(vmem_limit_bytes=16 * 2**20),
    )(*arrays)


def columns_kernel(c0, c1, c2, c3, keys, values):
    for a, ref in enumerate((c0, c1, c2, c3)):
        keys[a] = ref[:, 0:DH]
        values[a] = ref[:, DH : 2 * DH]


def columns_of(pieces):
    vmem = pl.BlockSpec(memory_space=pltpu.VMEM)
    return pl.pallas_call(
        columns_kernel,
        out_shape=SHARES[:2],
        in_specs=[vmem] * 4,
        out_specs=(vmem,) * 2,
        compiler_params=pltpu.CompilerParams(vmem_limit_bytes=16 * 2**20),
    )(*pieces)


def finish_kernel(facts, *refs):
    key_parts, value_parts, (key_out, value_out, mine, sent) = refs[:4], refs[4:8], refs[8:]

    def rounded(parts):
        return functools.reduce(lambda a, b: a + b, [p[...].astype(F32) for p in parts]).astype(BF)

    key, value = rounded(key_parts), rounded(value_parts)
    key_out[...] = key
    value_out[...] = value
    key, value = key.astype(F32), value.astype(F32)
    left = lax.broadcasted_iota(jnp.int32, key.shape, 1) < DH // 2
    low = jnp.where(left, key, pltpu.roll(value, DH // 2, 1)).astype(BF)
    high = jnp.where(left, pltpu.roll(key, DH // 2, 1), value).astype(BF)
    even = lax.rem(facts[DOCS + RANKS], 2) == 0

    @pl.when(even)
    def _():
        mine[...] = low
        sent[...] = high

    @pl.when(jnp.logical_not(even))
    def _():
        mine[...] = high
        sent[...] = low


def finish(facts, key_parts, value_parts):
    vmem = pl.BlockSpec(memory_space=pltpu.VMEM)
    return pl.pallas_call(
        finish_kernel,
        out_shape=(jax.ShapeDtypeStruct((ROWS, DH), BF),) * 4,
        in_specs=[pl.BlockSpec(memory_space=pltpu.SMEM)] + [vmem] * 8,
        out_specs=(vmem,) * 4,
        compiler_params=pltpu.CompilerParams(vmem_limit_bytes=8 * 2**20),
    )(facts, *key_parts, *value_parts)


def product_kernel(
    facts, hid0, hid1, hid2, hid3, row0, row1, row2, row3, out0, out1, out2, out3, acc
):
    my_zl, my_y, my_x, core, zh = (facts[DOCS + RANKS + i] for i in range(5))
    for j, row in enumerate((row0, row1, row2, row3)):
        group = lax.rem(my_x + 4 - j, 4)

        @pl.when(group // 2 == core)
        def _():
            for c in range(4):
                columns = slice(c * 512, (c + 1) * 512)
                total = None
                for i, hidden in enumerate((hid0, hid1, hid2, hid3)):
                    part = dot(row[i * ROWS : (i + 1) * ROWS, :], hidden[:, columns], 0, 0)
                    total = part if total is None else total + part
                acc[...] = total
                side = lax.rem(lax.rem(group, 2) + my_zl // 2, 2)
                for s, out in enumerate((out0, out1, out2, out3)):
                    y = lax.rem(my_y + s, 4)
                    for kind in range(2):
                        at = pl.ds(pl.multiple_of(kind * 64 + y * 16, 16), 16)
                        out[lax.rem(kind + zh, 2), side, :, columns] = acc[at, :].astype(BF)


def weight_product(facts, *operands):
    vmem = pl.BlockSpec(memory_space=pltpu.VMEM)
    return pl.pallas_call(
        product_kernel,
        out_shape=(jax.ShapeDtypeStruct((2, 2, 16, 2048), BF),) * 4,
        in_specs=[pl.BlockSpec(memory_space=pltpu.SMEM)] + [vmem] * 8,
        out_specs=(vmem,) * 4,
        scratch_shapes=[pltpu.VMEM((DH, 512), F32)],
        compiler_params=pltpu.CompilerParams(vmem_limit_bytes=24 * 2**20),
        cost_estimate=pl.CostEstimate(flops=10**9, bytes_accessed=4 * 10**6, transcendentals=0),
    )(facts, *operands)


def after(value, *others):
    return lax.optimization_barrier((value, others))[0]


def per_device(hidden_in, queries, keys_in, values_in, out_grad, doc_lengths, pair_perm):
    zl, y, x = (lax.axis_index(a) for a in ("zl", "y", "x"))
    zh, core = lax.axis_index("zh"), lax.axis_index("co")
    swap = [(0, 1), (1, 0)]
    facts = jnp.concatenate([doc_lengths[0], pair_perm, jnp.stack([zl, y, x, core, zh]).astype(jnp.int32)])

    def moved(value, axis, shift):
        return lax.ppermute(value, axis, ring(shift))

    own = jnp.concatenate([keys_in[0], values_in[0]], axis=1)
    pieces = [own] + [moved(own, "zl", a) for a in (1, 2, 3)]
    rows_in = near(queries[0], out_grad[0])
    hidden = hidden_in[0]
    hidden = (hidden, lax.ppermute(hidden, "co", swap))
    pieces, rows_in, hidden = lax.optimization_barrier((pieces, rows_in, hidden))
    ks, vs = columns_of(pieces)
    ks = [ks] + [moved(ks, "y", s) for s in (1, 2, 3)]
    vs = after(vs, ks[1])
    vs = [vs] + [moved(vs, "y", s) for s in (1, 2, 3)]

    def received(shares):
        return [shares[0]] + [moved(shares[s], "y", s) for s in (1, 2, 3)]

    def over_zl(got):
        parts = [add_up(*[g[a] for g in got]) for a in range(4)]
        return [parts[0]] + [moved(parts[a].astype(BF), "zl", a) for a in (1, 2, 3)]

    stats, *dvs = forward(facts, *rows_in, ks)
    dvs = received(dvs)
    neighbour = [(0, 1), (1, 0), (2, 3), (3, 2)]
    beside = lax.ppermute(after(hidden[0], stats), "zl", neighbour)
    dq, *dks = backward(facts, *rows_in, ks, vs, stats)
    dks = received(after(dks, dvs))
    key_grads, value_grads, mine, sent = finish(facts, over_zl(dks), over_zl(dvs))

    beside = after(beside, *dks)
    hidden = (hidden[0], beside, hidden[1], lax.ppermute(beside, "co", swap))
    rows = jnp.stack([mine, lax.ppermute(sent, "zl", neighbour)])
    cross = [
        (x0 + 4 * c, x0 + 4 * (1 - c)) for c in range(2) for x0 in range(4) if x0 // 2 == 1 - c
    ]
    rows = jnp.stack([rows, lax.ppermute(rows, ("co", "x"), cross)]).reshape(4 * ROWS, DH)

    def along(j):
        return [
            (x0 + 4 * c, (x0 + j) % 4 + 4 * c) for c in range(2) for x0 in range(4) if x0 // 2 == c
        ]

    rows = [rows] + [lax.ppermute(rows, ("co", "x"), along(j)) for j in (1, 2, 3)]
    shares = received(weight_product(facts, *hidden, *rows))
    total = add_up(*shares)
    other_zl = [(0, 2), (2, 0), (1, 3), (3, 1)]
    both = [(a + 4 * c, b + 4 * (1 - c)) for a, b in other_zl for c in range(2)]
    grad_weight = add_up(
        total[0, 0],
        lax.ppermute(total[0, 1].astype(BF), "zl", other_zl),
        lax.ppermute(total[1, 0].astype(BF), "zh", swap),
        lax.ppermute(total[1, 1].astype(BF), ("zh", "zl"), both),
    )
    return dq[None], key_grads[None], value_grads[None], grad_weight


def solution(mesh):
    fine = Mesh(mesh.devices.reshape(SIZES), CARDINAL)
    dp, ctx, tp = ("zh", "co"), ("zl", "y"), "x"
    tokens = P(dp, ctx, tp)
    return jax.shard_map(
        per_device,
        mesh=fine,
        in_specs=(tokens,) * 5 + (P(dp, None), P()),
        out_specs=(tokens,) * 3 + (P(dp + ctx, tp),),
        check_vma=False,
    )
```

```python
import functools

import jax
import jax.numpy as jnp
import numpy as np
from jax import lax
from jax.experimental import pallas as pl
from jax.experimental.pallas import tpu as pltpu
from jax.sharding import Mesh, PartitionSpec as P

DH = 128
HEADS = 8
HALF = 112
ROWS = 2 * HALF
LANES = HEADS * HALF
RANKS = 16
BLOCKS = 2 * RANKS
SEQ = ROWS * RANKS
DOCS = 6
MAX_DOC = 1194
SPAN = 256
STEPS = -(-(MAX_DOC - 1 + HALF) // SPAN)
PAD = SPAN
SCALE = DH**-0.5
LOG2E = 1.4426950408889634
MASKED = -1e30
CARDINAL = ("zh", "co", "zl", "y", "x")
SIZES = (2, 2, 4, 4, 4)
BF = jnp.bfloat16
F32 = jnp.float32


def dot(a, b, ca, cb):
    return lax.dot_general(a, b, (((ca,), (cb,)), ((), ())), preferred_element_type=F32)


def fold(x, op):
    return op(x.reshape(x.shape[0] // 8, 8, x.shape[1]), axis=0)


class Place:
    def __init__(self, facts):
        self.facts = facts
        self.zl, self.y = facts[DOCS + RANKS], facts[DOCS + RANKS + 1]

    def pair(self, rank):
        return self.facts[DOCS + rank]

    def rows(self, zl, y, half):
        pair = self.pair(zl * 4 + y)
        block = pair if half == 0 else BLOCKS - 1 - pair
        return pl.ds(pl.multiple_of(PAD + block * HALF, 16), HALF)

    def gather(self, refs, buf, by_zl=False):
        buf[0:PAD, :] = jnp.zeros((PAD, DH), BF)
        for i, ref in enumerate(refs):
            for j in range(4):
                a, s = (i, j) if by_zl else (j, i)
                zl, y = lax.rem(self.zl + 4 - a, 4), lax.rem(self.y + 4 - s, 4)
                for half in range(2):
                    rows = slice(half * HALF, (half + 1) * HALF)
                    buf[self.rows(zl, y, half), :] = ref[j, rows, :]

    def scatter(self, acc, refs, scale):
        for s, ref in enumerate(refs):
            for a in range(4):
                zl, y = lax.rem(self.zl + a, 4), lax.rem(self.y + s, 4)
                for half in range(2):
                    rows = slice(half * HALF, (half + 1) * HALF)
                    ref[a, rows, :] = (acc[self.rows(zl, y, half), :] * scale).astype(BF)


class Window:
    def __init__(self, place, half):
        pair = place.pair(place.zl * 4 + place.y)
        block = jnp.where(half == 0, pair, BLOCKS - 1 - pair)
        lane = lax.broadcasted_iota(jnp.int32, (1, LANES), 1)
        within = lane
        for h in range(1, HEADS):
            within = jnp.where(lane >= h * HALF, lane - h * HALF, within)
        first = block * HALF
        self.pos = within + first
        self.low = jnp.zeros_like(self.pos)
        low0 = jnp.int32(0)
        end = jnp.int32(0)
        for d in range(DOCS - 1):
            end = end + place.facts[d]
            self.low = jnp.where(self.pos >= end, end, self.low)
            low0 = jnp.where(first >= end, end, low0)
        stop = first + HALF
        self.count = lax.div(stop - low0 + (SPAN - 1), SPAN)
        self.start = stop - self.count * SPAN

    def keys(self, t):
        return pl.ds(pl.multiple_of(PAD + self.start + t * SPAN, 16), SPAN)

    def kept(self, t):
        return pl.ds(pl.multiple_of(t * SPAN, SPAN), SPAN)

    def scores(self, t, kbuf, qs):
        s = dot(kbuf[self.keys(t), :], qs[...], 1, 1) * (SCALE * LOG2E)
        key = lax.broadcasted_iota(jnp.int32, (SPAN, LANES), 0) + (self.start + t * SPAN)
        return jnp.where((key >= self.low) & (key <= self.pos), s, MASKED)


def heads_apart(ref, half, stack):
    row0 = pl.multiple_of(half * HALF, 16)
    for h in range(HEADS):
        stack[h * HALF : (h + 1) * HALF, :] = ref[pl.ds(row0, HALF), h * DH : (h + 1) * DH]


def forward_kernel(
    facts, q_ref, do_ref, k0, k1, k2, k3, stats, out0, out1, out2, out3,
    kbuf, dvacc, s_scr, qs, dos,
):
    place = Place(facts)
    place.gather((k0, k1, k2, k3), kbuf, by_zl=True)
    dvacc[...] = jnp.zeros_like(dvacc)

    def one_block(half, carry):
        heads_apart(q_ref, half, qs)
        heads_apart(do_ref, half, dos)
        window = Window(place, half)

        def score(t, mass):
            s = window.scores(t, kbuf, qs)
            s_scr[window.kept(t), :] = s
            return mass + fold(jnp.exp2(s), jnp.sum)

        mass = lax.fori_loop(0, window.count, score, jnp.zeros((8, LANES), F32))
        log_sum = jnp.log2(jnp.sum(mass, axis=0, keepdims=True))

        def spread(t, carry):
            p = jnp.exp2(s_scr[window.kept(t), :] - log_sum).astype(BF)
            dvacc[window.keys(t), :] += dot(p, dos[...], 1, 0)
            return carry

        lax.fori_loop(0, window.count, spread, 0)
        stats[half] = log_sum
        return carry

    lax.fori_loop(0, 2, one_block, 0)
    place.scatter(dvacc, (out0, out1, out2, out3), 1.0)


def backward_kernel(
    facts, q_ref, do_ref, k0, k1, k2, k3, v0, v1, v2, v3, stats,
    dq_ref, out0, out1, out2, out3,
    kbuf, vbuf, dkacc, p_scr, dp_scr, qs, dos,
):
    place = Place(facts)
    place.gather((k0, k1, k2, k3), kbuf, by_zl=True)
    place.gather((v0, v1, v2, v3), vbuf)
    dkacc[...] = jnp.zeros_like(dkacc)

    def one_block(half, carry):
        heads_apart(q_ref, half, qs)
        heads_apart(do_ref, half, dos)
        window = Window(place, half)
        log_sum = stats[half]

        def weigh(t, moment):
            p = jnp.exp2(window.scores(t, kbuf, qs) - log_sum)
            dp = dot(vbuf[window.keys(t), :], dos[...], 1, 1)
            p_scr[window.kept(t), :] = p
            dp_scr[window.kept(t), :] = dp
            return moment + fold(p * dp, jnp.sum)

        moment = lax.fori_loop(0, window.count, weigh, jnp.zeros((8, LANES), F32))
        delta = jnp.sum(moment, axis=0, keepdims=True)

        def spread(t, dqt):
            g = (p_scr[window.kept(t), :] * (dp_scr[window.kept(t), :] - delta)).astype(BF)
            at = window.keys(t)
            dkacc[at, :] += dot(g, qs[...], 1, 0)
            return dqt + dot(kbuf[at, :], g, 0, 0)

        dqt = lax.fori_loop(0, window.count, spread, jnp.zeros((DH, LANES), F32))
        dq = (dqt * SCALE).T.astype(BF)
        row0 = pl.multiple_of(half * HALF, 16)
        for h in range(HEADS):
            dq_ref[pl.ds(row0, HALF), h * DH : (h + 1) * DH] = dq[h * HALF : (h + 1) * HALF, :]
        return carry

    lax.fori_loop(0, 2, one_block, 0)
    place.scatter(dkacc, (out0, out1, out2, out3), SCALE)


SHARES = (jax.ShapeDtypeStruct((4, ROWS, DH), BF),) * 4


def forward(facts, q, do, ks):
    vmem = pl.BlockSpec(memory_space=pltpu.VMEM)
    return pl.pallas_call(
        forward_kernel,
        out_shape=(jax.ShapeDtypeStruct((2, 1, LANES), F32),) + SHARES,
        in_specs=[pl.BlockSpec(memory_space=pltpu.SMEM)] + [vmem] * 6,
        out_specs=(vmem,) * 5,
        scratch_shapes=[
            pltpu.VMEM((PAD + SEQ, DH), BF),
            pltpu.VMEM((PAD + SEQ, DH), F32),
            pltpu.VMEM((STEPS * SPAN, LANES), F32),
            pltpu.VMEM((LANES, DH), BF),
            pltpu.VMEM((LANES, DH), BF),
        ],
        compiler_params=pltpu.CompilerParams(vmem_limit_bytes=32 * 2**20),
        cost_estimate=pl.CostEstimate(flops=3 * 10**9, bytes_accessed=4 * 10**6, transcendentals=2 * 10**6),
    )(facts, q, do, *ks)


def backward(facts, q, do, ks, vs, stats):
    vmem = pl.BlockSpec(memory_space=pltpu.VMEM)
    return pl.pallas_call(
        backward_kernel,
        out_shape=(jax.ShapeDtypeStruct((ROWS, HEADS * DH), BF),) + SHARES,
        in_specs=[pl.BlockSpec(memory_space=pltpu.SMEM)] + [vmem] * 11,
        out_specs=(vmem,) * 5,
        scratch_shapes=[
            pltpu.VMEM((PAD + SEQ, DH), BF),
            pltpu.VMEM((PAD + SEQ, DH), BF),
            pltpu.VMEM((PAD + SEQ, DH), F32),
            pltpu.VMEM((STEPS * SPAN, LANES), F32),
            pltpu.VMEM((STEPS * SPAN, LANES), F32),
            pltpu.VMEM((LANES, DH), BF),
            pltpu.VMEM((LANES, DH), BF),
        ],
        compiler_params=pltpu.CompilerParams(vmem_limit_bytes=32 * 2**20),
        cost_estimate=pl.CostEstimate(
            flops=5 * 10**9, bytes_accessed=5 * 10**6, transcendentals=2 * 10**6
        ),
    )(facts, q, do, *ks, *vs, stats)


def ring(shift):
    return [(i, (i + shift) % 4) for i in range(4)]


def add_up(*xs):
    return functools.reduce(lambda a, b: a + b, [x.astype(F32) for x in xs])


def copy_kernel(*refs):
    for source, target in zip(refs[: len(refs) // 2], refs[len(refs) // 2 :]):
        target[...] = source[...]


def near(*arrays):
    vmem = pl.BlockSpec(memory_space=pltpu.VMEM)
    return pl.pallas_call(
        copy_kernel,
        out_shape=tuple(jax.ShapeDtypeStruct(a.shape, a.dtype) for a in arrays),
        in_specs=[vmem] * len(arrays),
        out_specs=(vmem,) * len(arrays),
        compiler_params=pltpu.CompilerParams(vmem_limit_bytes=16 * 2**20),
    )(*arrays)


def stack_kernel(*refs):
    for i, ref in enumerate(refs[:-2]):
        refs[-2 + i // 4][i % 4] = ref[...]


def stacked(ks, vs):
    vmem = pl.BlockSpec(memory_space=pltpu.VMEM)
    return pl.pallas_call(
        stack_kernel,
        out_shape=SHARES[:2],
        in_specs=[vmem] * 8,
        out_specs=(vmem,) * 2,
        compiler_params=pltpu.CompilerParams(vmem_limit_bytes=16 * 2**20),
    )(*ks, *vs)


def finish_kernel(facts, *refs):
    key_parts, value_parts, (key_out, value_out, mine, sent) = refs[:4], refs[4:8], refs[8:]

    def rounded(parts):
        return functools.reduce(lambda a, b: a + b, [p[...].astype(F32) for p in parts]).astype(BF)

    key, value = rounded(key_parts), rounded(value_parts)
    key_out[...] = key
    value_out[...] = value
    key, value = key.astype(F32), value.astype(F32)
    left = lax.broadcasted_iota(jnp.int32, key.shape, 1) < DH // 2
    low = jnp.where(left, key, pltpu.roll(value, DH // 2, 1)).astype(BF)
    high = jnp.where(left, pltpu.roll(key, DH // 2, 1), value).astype(BF)
    even = lax.rem(facts[DOCS + RANKS], 2) == 0

    @pl.when(even)
    def _():
        mine[...] = low
        sent[...] = high

    @pl.when(jnp.logical_not(even))
    def _():
        mine[...] = high
        sent[...] = low


def finish(facts, key_parts, value_parts):
    vmem = pl.BlockSpec(memory_space=pltpu.VMEM)
    return pl.pallas_call(
        finish_kernel,
        out_shape=(jax.ShapeDtypeStruct((ROWS, DH), BF),) * 4,
        in_specs=[pl.BlockSpec(memory_space=pltpu.SMEM)] + [vmem] * 8,
        out_specs=(vmem,) * 4,
        compiler_params=pltpu.CompilerParams(vmem_limit_bytes=8 * 2**20),
    )(facts, *key_parts, *value_parts)


def product_kernel(
    facts, hid0, hid1, hid2, hid3, row0, row1, row2, row3, out0, out1, out2, out3, acc
):
    my_zl, my_y, my_x, core, zh = (facts[DOCS + RANKS + i] for i in range(5))
    for j, row in enumerate((row0, row1, row2, row3)):
        group = lax.rem(my_x + 4 - j, 4)

        @pl.when(group // 2 == core)
        def _():
            for c in range(4):
                columns = slice(c * 512, (c + 1) * 512)
                total = None
                for i, hidden in enumerate((hid0, hid1, hid2, hid3)):
                    part = dot(row[i * ROWS : (i + 1) * ROWS, :], hidden[:, columns], 0, 0)
                    total = part if total is None else total + part
                acc[...] = total
                side = lax.rem(lax.rem(group, 2) + my_zl // 2, 2)
                for s, out in enumerate((out0, out1, out2, out3)):
                    y = lax.rem(my_y + s, 4)
                    for kind in range(2):
                        at = pl.ds(pl.multiple_of(kind * 64 + y * 16, 16), 16)
                        out[lax.rem(kind + zh, 2), side, :, columns] = acc[at, :].astype(BF)


def weight_product(facts, *operands):
    vmem = pl.BlockSpec(memory_space=pltpu.VMEM)
    return pl.pallas_call(
        product_kernel,
        out_shape=(jax.ShapeDtypeStruct((2, 2, 16, 2048), BF),) * 4,
        in_specs=[pl.BlockSpec(memory_space=pltpu.SMEM)] + [vmem] * 8,
        out_specs=(vmem,) * 4,
        scratch_shapes=[pltpu.VMEM((DH, 512), F32)],
        compiler_params=pltpu.CompilerParams(vmem_limit_bytes=24 * 2**20),
        cost_estimate=pl.CostEstimate(flops=10**9, bytes_accessed=4 * 10**6, transcendentals=0),
    )(facts, *operands)


def after(value, *others):
    return lax.optimization_barrier((value, others))[0]


def per_device(hidden_in, queries, keys_in, values_in, out_grad, doc_lengths, pair_perm):
    zl, y, x = (lax.axis_index(a) for a in ("zl", "y", "x"))
    zh, core = lax.axis_index("zh"), lax.axis_index("co")
    swap = [(0, 1), (1, 0)]
    facts = jnp.concatenate([doc_lengths[0], pair_perm, jnp.stack([zl, y, x, core, zh]).astype(jnp.int32)])

    def moved(value, axis, shift):
        return lax.ppermute(value, axis, ring(shift))

    key, value = keys_in[0], values_in[0]
    ks = [key] + [moved(key, "y", s) for s in (1, 2, 3)]
    vs = [value] + [moved(value, "zl", a) for a in (1, 2, 3)]
    rows_in = near(queries[0], out_grad[0])
    ks, vs, rows_in = lax.optimization_barrier((ks, vs, rows_in))
    ks, vs = stacked(ks, vs)
    ks = [ks] + [moved(ks, "zl", a) for a in (1, 2, 3)]
    vs = [vs] + [moved(vs, "y", s) for s in (1, 2, 3)]
    ks, vs = lax.optimization_barrier((ks, vs))

    def received(shares):
        return [shares[0]] + [moved(shares[s], "y", s) for s in (1, 2, 3)]

    def over_zl(got):
        parts = [add_up(*[g[a] for g in got]) for a in range(4)]
        return [parts[0]] + [moved(parts[a].astype(BF), "zl", a) for a in (1, 2, 3)]

    stats, *dvs = forward(facts, *rows_in, ks)
    dvs = received(dvs)
    neighbour = [(0, 1), (1, 0), (2, 3), (3, 2)]
    hidden = hidden_in[0]
    beside = lax.ppermute(after(hidden, stats), "zl", neighbour)
    dq, *dks = backward(facts, *rows_in, ks, vs, stats)
    dks = received(after(dks, *dvs, beside))
    value_parts = over_zl(dvs)
    dks, hidden, beside = after((dks, hidden, beside), *value_parts)
    key_grads, value_grads, mine, sent = finish(facts, over_zl(dks), value_parts)

    hidden = (hidden, beside) + tuple(lax.ppermute(h, "co", swap) for h in (hidden, beside))
    def to_worker(other_core, other_zl):
        index = [(c, z, x0) for c in range(2) for z in range(4) for x0 in range(4)]
        pairs = [
            (i, ((c ^ other_core) * 4 + (z ^ other_zl)) * 4 + x0)
            for i, (c, z, x0) in enumerate(index)
            if x0 // 2 == c ^ other_core
        ]
        return lax.ppermute(sent if other_zl else mine, ("co", "zl", "x"), pairs)

    rows = jnp.stack([mine, to_worker(0, 1), to_worker(1, 0), to_worker(1, 1)])
    rows = rows.reshape(4 * ROWS, DH)

    def along(j):
        return [
            (x0 + 4 * c, (x0 + j) % 4 + 4 * c) for c in range(2) for x0 in range(4) if x0 // 2 == c
        ]

    rows = [rows] + [lax.ppermute(rows, ("co", "x"), along(j)) for j in (1, 2, 3)]
    shares = received(weight_product(facts, *hidden, *rows))
    total = add_up(*shares)
    other_zl = [(0, 2), (2, 0), (1, 3), (3, 1)]
    both = [(a + 4 * c, b + 4 * (1 - c)) for a, b in other_zl for c in range(2)]
    grad_weight = add_up(
        total[0, 0],
        lax.ppermute(total[0, 1].astype(BF), "zl", other_zl),
        lax.ppermute(total[1, 0].astype(BF), "zh", swap),
        lax.ppermute(total[1, 1].astype(BF), ("zh", "zl"), both),
    )
    return dq[None], key_grads[None], value_grads[None], grad_weight


def solution(mesh):
    fine = Mesh(mesh.devices.reshape(SIZES), CARDINAL)
    dp, ctx, tp = ("zh", "co"), ("zl", "y"), "x"
    tokens = P(dp, ctx, tp)
    return jax.shard_map(
        per_device,
        mesh=fine,
        in_specs=(tokens,) * 5 + (P(dp, None), P()),
        out_specs=(tokens,) * 3 + (P(dp + ctx, tp),),
        check_vma=False,
    )
```

```python
import functools

import jax
import jax.numpy as jnp
import numpy as np
from jax import lax
from jax.experimental import pallas as pl
from jax.experimental.pallas import tpu as pltpu
from jax.sharding import Mesh, PartitionSpec as P

DH = 128
HEADS = 8
HALF = 112
ROWS = 2 * HALF
LANES = HEADS * HALF
RANKS = 16
BLOCKS = 2 * RANKS
SEQ = ROWS * RANKS
DOCS = 6
MAX_DOC = 1194
SPAN = 2 * HALF
STEPS = -(-(MAX_DOC - 1 + HALF) // SPAN)
PAD = SPAN
SCALE = DH**-0.5
LOG2E = 1.4426950408889634
MASKED = -1e30
CARDINAL = ("zh", "co", "zl", "y", "x")
SIZES = (2, 2, 4, 4, 4)
BF = jnp.bfloat16
F32 = jnp.float32


def dot(a, b, ca, cb):
    return lax.dot_general(a, b, (((ca,), (cb,)), ((), ())), preferred_element_type=F32)


def fold(x, op):
    return op(x.reshape(x.shape[0] // 8, 8, x.shape[1]), axis=0)


class Place:
    def __init__(self, facts):
        self.facts = facts
        self.zl, self.y = facts[DOCS + RANKS], facts[DOCS + RANKS + 1]

    def pair(self, rank):
        return self.facts[DOCS + rank]

    def rows(self, zl, y, half):
        pair = self.pair(zl * 4 + y)
        block = pair if half == 0 else BLOCKS - 1 - pair
        return pl.ds(pl.multiple_of(PAD + block * HALF, 16), HALF)

    def gather(self, refs, buf):
        buf[0:PAD, :] = jnp.zeros((PAD, DH), BF)
        for s, ref in enumerate(refs):
            for a in range(4):
                zl, y = lax.rem(self.zl + 4 - a, 4), lax.rem(self.y + 4 - s, 4)
                for half in range(2):
                    rows = slice(half * HALF, (half + 1) * HALF)
                    buf[self.rows(zl, y, half), :] = ref[a, rows, :]

    def scatter(self, acc, refs, scale):
        for s, ref in enumerate(refs):
            for a in range(4):
                zl, y = lax.rem(self.zl + a, 4), lax.rem(self.y + s, 4)
                for half in range(2):
                    rows = slice(half * HALF, (half + 1) * HALF)
                    ref[a, rows, :] = (acc[self.rows(zl, y, half), :] * scale).astype(BF)


class Window:
    def __init__(self, place, half):
        pair = place.pair(place.zl * 4 + place.y)
        block = jnp.where(half == 0, pair, BLOCKS - 1 - pair)
        lane = lax.broadcasted_iota(jnp.int32, (1, LANES), 1)
        within = lane
        for h in range(1, HEADS):
            within = jnp.where(lane >= h * HALF, lane - h * HALF, within)
        first = block * HALF
        self.first = first
        self.pos = within + first
        self.low = jnp.zeros_like(self.pos)
        low0 = jnp.int32(0)
        self.last_low = jnp.int32(0)
        end = jnp.int32(0)
        for d in range(DOCS - 1):
            end = end + place.facts[d]
            self.low = jnp.where(self.pos >= end, end, self.low)
            low0 = jnp.where(first >= end, end, low0)
            self.last_low = jnp.where(first + HALF - 1 >= end, end, self.last_low)
        stop = first + HALF
        self.count = lax.div(stop - low0 + (SPAN - 1), SPAN)
        self.start = stop - self.count * SPAN

    def keys(self, t):
        return pl.ds(pl.multiple_of(PAD + self.start + t * SPAN, 16), SPAN)

    def kept(self, t):
        return pl.ds(pl.multiple_of(t * SPAN, SPAN), SPAN)

    def scores(self, t, kbuf, qs):
        return dot(kbuf[self.keys(t), :], qs[...], 1, 1) * (SCALE * LOG2E)

    def masked(self, t, s):
        key = lax.broadcasted_iota(jnp.int32, (SPAN, LANES), 0) + (self.start + t * SPAN)
        return jnp.where((key >= self.low) & (key <= self.pos), s, MASKED)

    def all_allowed(self, t):
        first_key = self.start + t * SPAN
        return (first_key >= self.last_low) & (first_key + SPAN <= self.first + 1)


def heads_apart(ref, half, stack):
    row0 = pl.multiple_of(half * HALF, 16)
    for h in range(HEADS):
        stack[h * HALF : (h + 1) * HALF, :] = ref[pl.ds(row0, HALF), h * DH : (h + 1) * DH]


def forward_kernel(
    facts, q_ref, do_ref, k0, k1, k2, k3, stats, out0, out1, out2, out3,
    kbuf, dvacc, s_scr, qs, dos,
):
    place = Place(facts)
    place.gather((k0, k1, k2, k3), kbuf)
    dvacc[...] = jnp.zeros_like(dvacc)

    def one_block(half, carry):
        heads_apart(q_ref, half, qs)
        heads_apart(do_ref, half, dos)
        window = Window(place, half)

        def score(t, mass):
            def some(masked):
                s = window.scores(t, kbuf, qs)
                s = window.masked(t, s) if masked else s
                s_scr[window.kept(t), :] = s
                return mass + fold(jnp.exp2(s), jnp.sum)

            return lax.cond(window.all_allowed(t), lambda: some(False), lambda: some(True))

        mass = lax.fori_loop(0, window.count, score, jnp.zeros((8, LANES), F32))
        log_sum = jnp.log2(jnp.sum(mass, axis=0, keepdims=True))

        def spread(t, carry):
            p = jnp.exp2(s_scr[window.kept(t), :] - log_sum).astype(BF)
            dvacc[window.keys(t), :] += dot(p, dos[...], 1, 0)
            return carry

        lax.fori_loop(0, window.count, spread, 0)
        stats[half] = log_sum
        return carry

    lax.fori_loop(0, 2, one_block, 0)
    place.scatter(dvacc, (out0, out1, out2, out3), 1.0)


def backward_kernel(
    facts, q_ref, do_ref, k0, k1, k2, k3, v0, v1, v2, v3, stats,
    dq_ref, out0, out1, out2, out3,
    kbuf, vbuf, dkacc, p_scr, dp_scr, qs, dos,
):
    place = Place(facts)
    place.gather((k0, k1, k2, k3), kbuf)
    place.gather((v0, v1, v2, v3), vbuf)
    dkacc[...] = jnp.zeros_like(dkacc)

    def one_block(half, carry):
        heads_apart(q_ref, half, qs)
        heads_apart(do_ref, half, dos)
        window = Window(place, half)
        log_sum = stats[half]

        def weigh(t, moment):
            def some(masked):
                s = window.scores(t, kbuf, qs)
                s = window.masked(t, s) if masked else s
                p = jnp.exp2(s - log_sum)
                dp = dot(vbuf[window.keys(t), :], dos[...], 1, 1)
                p_scr[window.kept(t), :] = p
                dp_scr[window.kept(t), :] = dp
                return moment + fold(p * dp, jnp.sum)

            return lax.cond(window.all_allowed(t), lambda: some(False), lambda: some(True))

        moment = lax.fori_loop(0, window.count, weigh, jnp.zeros((8, LANES), F32))
        delta = jnp.sum(moment, axis=0, keepdims=True)

        def spread(t, dqt):
            g = (p_scr[window.kept(t), :] * (dp_scr[window.kept(t), :] - delta)).astype(BF)
            at = window.keys(t)
            dkacc[at, :] += dot(g, qs[...], 1, 0)
            return dqt + dot(kbuf[at, :], g, 0, 0)

        dqt = lax.fori_loop(0, window.count, spread, jnp.zeros((DH, LANES), F32))
        dq = (dqt * SCALE).T.astype(BF)
        row0 = pl.multiple_of(half * HALF, 16)
        for h in range(HEADS):
            dq_ref[pl.ds(row0, HALF), h * DH : (h + 1) * DH] = dq[h * HALF : (h + 1) * HALF, :]
        return carry

    lax.fori_loop(0, 2, one_block, 0)
    place.scatter(dkacc, (out0, out1, out2, out3), SCALE)


SHARES = (jax.ShapeDtypeStruct((4, ROWS, DH), BF),) * 4


def forward(facts, q, do, ks):
    vmem = pl.BlockSpec(memory_space=pltpu.VMEM)
    return pl.pallas_call(
        forward_kernel,
        out_shape=(jax.ShapeDtypeStruct((2, 1, LANES), F32),) + SHARES,
        in_specs=[pl.BlockSpec(memory_space=pltpu.SMEM)] + [vmem] * 6,
        out_specs=(vmem,) * 5,
        scratch_shapes=[
            pltpu.VMEM((PAD + SEQ, DH), BF),
            pltpu.VMEM((PAD + SEQ, DH), F32),
            pltpu.VMEM((STEPS * SPAN, LANES), F32),
            pltpu.VMEM((LANES, DH), BF),
            pltpu.VMEM((LANES, DH), BF),
        ],
        compiler_params=pltpu.CompilerParams(vmem_limit_bytes=32 * 2**20),
        cost_estimate=pl.CostEstimate(flops=3 * 10**9, bytes_accessed=4 * 10**6, transcendentals=2 * 10**6),
    )(facts, q, do, *ks)


def backward(facts, q, do, ks, vs, stats):
    vmem = pl.BlockSpec(memory_space=pltpu.VMEM)
    return pl.pallas_call(
        backward_kernel,
        out_shape=(jax.ShapeDtypeStruct((ROWS, HEADS * DH), BF),) + SHARES,
        in_specs=[pl.BlockSpec(memory_space=pltpu.SMEM)] + [vmem] * 11,
        out_specs=(vmem,) * 5,
        scratch_shapes=[
            pltpu.VMEM((PAD + SEQ, DH), BF),
            pltpu.VMEM((PAD + SEQ, DH), BF),
            pltpu.VMEM((PAD + SEQ, DH), F32),
            pltpu.VMEM((STEPS * SPAN, LANES), F32),
            pltpu.VMEM((STEPS * SPAN, LANES), F32),
            pltpu.VMEM((LANES, DH), BF),
            pltpu.VMEM((LANES, DH), BF),
        ],
        compiler_params=pltpu.CompilerParams(vmem_limit_bytes=32 * 2**20),
        cost_estimate=pl.CostEstimate(
            flops=5 * 10**9, bytes_accessed=5 * 10**6, transcendentals=2 * 10**6
        ),
    )(facts, q, do, *ks, *vs, stats)


def ring(shift):
    return [(i, (i + shift) % 4) for i in range(4)]


def add_up(*xs):
    return functools.reduce(lambda a, b: a + b, [x.astype(F32) for x in xs])


def copy_kernel(*refs):
    for source, target in zip(refs[: len(refs) // 2], refs[len(refs) // 2 :]):
        target[...] = source[...]


def near(*arrays):
    vmem = pl.BlockSpec(memory_space=pltpu.VMEM)
    return pl.pallas_call(
        copy_kernel,
        out_shape=tuple(jax.ShapeDtypeStruct(a.shape, a.dtype) for a in arrays),
        in_specs=[vmem] * len(arrays),
        out_specs=(vmem,) * len(arrays),
        compiler_params=pltpu.CompilerParams(vmem_limit_bytes=16 * 2**20),
    )(*arrays)


def columns_kernel(c0, c1, c2, c3, keys, values):
    for a, ref in enumerate((c0, c1, c2, c3)):
        keys[a] = ref[:, 0:DH]
        values[a] = ref[:, DH : 2 * DH]


def columns_of(pieces):
    vmem = pl.BlockSpec(memory_space=pltpu.VMEM)
    return pl.pallas_call(
        columns_kernel,
        out_shape=SHARES[:2],
        in_specs=[vmem] * 4,
        out_specs=(vmem,) * 2,
        compiler_params=pltpu.CompilerParams(vmem_limit_bytes=16 * 2**20),
    )(*pieces)


def finish_kernel(facts, *refs):
    key_parts, value_parts, (key_out, value_out, mine, sent) = refs[:4], refs[4:8], refs[8:]

    def rounded(parts):
        return functools.reduce(lambda a, b: a + b, [p[...].astype(F32) for p in parts]).astype(BF)

    key, value = rounded(key_parts), rounded(value_parts)
    key_out[...] = key
    value_out[...] = value
    key, value = key.astype(F32), value.astype(F32)
    left = lax.broadcasted_iota(jnp.int32, key.shape, 1) < DH // 2
    low = jnp.where(left, key, pltpu.roll(value, DH // 2, 1)).astype(BF)
    high = jnp.where(left, pltpu.roll(key, DH // 2, 1), value).astype(BF)
    even = lax.rem(facts[DOCS + RANKS], 2) == 0

    @pl.when(even)
    def _():
        mine[...] = low
        sent[...] = high

    @pl.when(jnp.logical_not(even))
    def _():
        mine[...] = high
        sent[...] = low


def finish(facts, key_parts, value_parts):
    vmem = pl.BlockSpec(memory_space=pltpu.VMEM)
    return pl.pallas_call(
        finish_kernel,
        out_shape=(jax.ShapeDtypeStruct((ROWS, DH), BF),) * 4,
        in_specs=[pl.BlockSpec(memory_space=pltpu.SMEM)] + [vmem] * 8,
        out_specs=(vmem,) * 4,
        compiler_params=pltpu.CompilerParams(vmem_limit_bytes=8 * 2**20),
    )(facts, *key_parts, *value_parts)


def product_kernel(
    facts, hid0, hid1, hid2, hid3, row0, row1, row2, row3, out0, out1, out2, out3, acc
):
    my_zl, my_y, my_x, core, zh = (facts[DOCS + RANKS + i] for i in range(5))
    for j, row in enumerate((row0, row1, row2, row3)):
        group = lax.rem(my_x + 4 - j, 4)

        @pl.when(group // 2 == core)
        def _():
            for c in range(4):
                columns = slice(c * 512, (c + 1) * 512)
                total = None
                for i, hidden in enumerate((hid0, hid1, hid2, hid3)):
                    part = dot(row[i * ROWS : (i + 1) * ROWS, :], hidden[:, columns], 0, 0)
                    total = part if total is None else total + part
                acc[...] = total
                side = lax.rem(lax.rem(group, 2) + my_zl // 2, 2)
                for s, out in enumerate((out0, out1, out2, out3)):
                    y = lax.rem(my_y + s, 4)
                    for kind in range(2):
                        at = pl.ds(pl.multiple_of(kind * 64 + y * 16, 16), 16)
                        out[lax.rem(kind + zh, 2), side, :, columns] = acc[at, :].astype(BF)


def weight_product(facts, *operands):
    vmem = pl.BlockSpec(memory_space=pltpu.VMEM)
    return pl.pallas_call(
        product_kernel,
        out_shape=(jax.ShapeDtypeStruct((2, 2, 16, 2048), BF),) * 4,
        in_specs=[pl.BlockSpec(memory_space=pltpu.SMEM)] + [vmem] * 8,
        out_specs=(vmem,) * 4,
        scratch_shapes=[pltpu.VMEM((DH, 512), F32)],
        compiler_params=pltpu.CompilerParams(vmem_limit_bytes=24 * 2**20),
        cost_estimate=pl.CostEstimate(flops=10**9, bytes_accessed=4 * 10**6, transcendentals=0),
    )(facts, *operands)


def after(value, *others):
    return lax.optimization_barrier((value, others))[0]


def per_device(hidden_in, queries, keys_in, values_in, out_grad, doc_lengths, pair_perm):
    zl, y, x = (lax.axis_index(a) for a in ("zl", "y", "x"))
    zh, core = lax.axis_index("zh"), lax.axis_index("co")
    swap = [(0, 1), (1, 0)]
    neighbour = [(0, 1), (1, 0), (2, 3), (3, 2)]
    facts = jnp.concatenate([doc_lengths[0], pair_perm, jnp.stack([zl, y, x, core, zh]).astype(jnp.int32)])

    def moved(value, axis, shift):
        return lax.ppermute(value, axis, ring(shift))

    own = jnp.concatenate([keys_in[0], values_in[0]], axis=1)
    pieces = [own] + [moved(own, "zl", a) for a in (1, 2, 3)]
    rows_in = near(queries[0], out_grad[0])
    hidden = hidden_in[0]
    hidden = (hidden, lax.ppermute(hidden, "co", swap))
    pieces, rows_in, hidden = lax.optimization_barrier((pieces, rows_in, hidden))
    ks, vs = columns_of(pieces)
    ks = [ks] + [moved(ks, "y", s) for s in (1, 2, 3)]
    vs = after(vs, ks[1])
    beside = lax.ppermute(after(hidden[0], ks[1]), "zl", neighbour)
    vs = [vs] + [moved(vs, "y", s) if s != 2 else vs for s in (1, 2, 3)]

    def received(shares):
        return [shares[0]] + [moved(shares[s], "y", s) for s in (1, 2, 3)]

    def over_zl(got):
        parts = [add_up(*[g[a] for g in got]) for a in range(4)]
        return [parts[0]] + [moved(parts[a].astype(BF), "zl", a) for a in (1, 2, 3)]

    stats, *dvs = forward(facts, *rows_in, ks)
    dvs = received(dvs)
    vs[2] = moved(after(vs[0], stats), "y", 2)
    dq, *dks = backward(facts, *rows_in, ks, vs, stats)
    dks = received(after(dks, dvs))
    key_grads, value_grads, mine, sent = finish(facts, over_zl(dks), over_zl(dvs))

    beside = after(beside, *dks)
    hidden = (hidden[0], beside, hidden[1], lax.ppermute(beside, "co", swap))
    rows = jnp.stack([mine, lax.ppermute(sent, "zl", neighbour)])
    cross = [
        (x0 + 4 * c, x0 + 4 * (1 - c)) for c in range(2) for x0 in range(4) if x0 // 2 == 1 - c
    ]
    rows = jnp.stack([rows, lax.ppermute(rows, ("co", "x"), cross)]).reshape(4 * ROWS, DH)

    def along(j):
        return [
            (x0 + 4 * c, (x0 + j) % 4 + 4 * c) for c in range(2) for x0 in range(4) if x0 // 2 == c
        ]

    rows = [rows] + [lax.ppermute(rows, ("co", "x"), along(j)) for j in (1, 2, 3)]
    shares = received(weight_product(facts, *hidden, *rows))
    total = add_up(*shares)
    other_zl = [(0, 2), (2, 0), (1, 3), (3, 1)]
    both = [(a + 4 * c, b + 4 * (1 - c)) for a, b in other_zl for c in range(2)]
    grad_weight = add_up(
        total[0, 0],
        lax.ppermute(total[0, 1].astype(BF), "zl", other_zl),
        lax.ppermute(total[1, 0].astype(BF), "zh", swap),
        lax.ppermute(total[1, 1].astype(BF), ("zh", "zl"), both),
    )
    return dq[None], key_grads[None], value_grads[None], grad_weight


def solution(mesh):
    fine = Mesh(mesh.devices.reshape(SIZES), CARDINAL)
    dp, ctx, tp = ("zh", "co"), ("zl", "y"), "x"
    tokens = P(dp, ctx, tp)
    return jax.shard_map(
        per_device,
        mesh=fine,
        in_specs=(tokens,) * 5 + (P(dp, None), P()),
        out_specs=(tokens,) * 3 + (P(dp + ctx, tp),),
        check_vma=False,
    )
```

```python
import functools

import jax
import jax.numpy as jnp
import numpy as np
from jax import lax
from jax.experimental import pallas as pl
from jax.experimental.pallas import tpu as pltpu
from jax.sharding import Mesh, PartitionSpec as P

DH = 128
HEADS = 8
HALF = 112
ROWS = 2 * HALF
LANES = HEADS * HALF
RANKS = 16
BLOCKS = 2 * RANKS
SEQ = ROWS * RANKS
DOCS = 6
MAX_DOC = 1194
SPAN = 2 * HALF
STEPS = -(-(MAX_DOC - 1 + HALF) // SPAN)
PAD = SPAN
SCALE = DH**-0.5
LOG2E = 1.4426950408889634
MASKED = -1e30
CARDINAL = ("zh", "co", "zl", "y", "x")
SIZES = (2, 2, 4, 4, 4)
BF = jnp.bfloat16
F32 = jnp.float32


def dot(a, b, ca, cb):
    return lax.dot_general(a, b, (((ca,), (cb,)), ((), ())), preferred_element_type=F32)


def fold(x, op):
    return op(x.reshape(x.shape[0] // 8, 8, x.shape[1]), axis=0)


class Place:
    def __init__(self, facts):
        self.facts = facts
        self.zl, self.y = facts[DOCS + RANKS], facts[DOCS + RANKS + 1]

    def pair(self, rank):
        return self.facts[DOCS + rank]

    def rows(self, zl, y, half):
        pair = self.pair(zl * 4 + y)
        block = pair if half == 0 else BLOCKS - 1 - pair
        return pl.ds(pl.multiple_of(PAD + block * HALF, 16), HALF)

    def gather(self, refs, buf):
        buf[0:PAD, :] = jnp.zeros((PAD, DH), BF)
        for s, ref in enumerate(refs):
            for a in range(4):
                zl, y = lax.rem(self.zl + 4 - a, 4), lax.rem(self.y + 4 - s, 4)
                for half in range(2):
                    rows = slice(half * HALF, (half + 1) * HALF)
                    buf[self.rows(zl, y, half), :] = ref[a, rows, :]

    def scatter(self, acc, refs, scale):
        for s, ref in enumerate(refs):
            for a in range(4):
                zl, y = lax.rem(self.zl + a, 4), lax.rem(self.y + s, 4)
                for half in range(2):
                    rows = slice(half * HALF, (half + 1) * HALF)
                    ref[a, rows, :] = (acc[self.rows(zl, y, half), :] * scale).astype(BF)


class Window:
    def __init__(self, place, half):
        pair = place.pair(place.zl * 4 + place.y)
        block = jnp.where(half == 0, pair, BLOCKS - 1 - pair)
        lane = lax.broadcasted_iota(jnp.int32, (1, LANES), 1)
        within = lane
        for h in range(1, HEADS):
            within = jnp.where(lane >= h * HALF, lane - h * HALF, within)
        first = block * HALF
        self.first = first
        self.pos = within + first
        self.low = jnp.zeros_like(self.pos)
        low0 = jnp.int32(0)
        self.last_low = jnp.int32(0)
        end = jnp.int32(0)
        for d in range(DOCS - 1):
            end = end + place.facts[d]
            self.low = jnp.where(self.pos >= end, end, self.low)
            low0 = jnp.where(first >= end, end, low0)
            self.last_low = jnp.where(first + HALF - 1 >= end, end, self.last_low)
        stop = first + HALF
        self.count = lax.div(stop - low0 + (SPAN - 1), SPAN)
        self.start = stop - self.count * SPAN

    def keys(self, t):
        return pl.ds(pl.multiple_of(PAD + self.start + t * SPAN, 16), SPAN)

    def kept(self, t):
        return pl.ds(pl.multiple_of(t * SPAN, SPAN), SPAN)

    def scores(self, t, kbuf, qs):
        return dot(kbuf[self.keys(t), :], qs[...], 1, 1) * (SCALE * LOG2E)

    def masked(self, t, s):
        key = lax.broadcasted_iota(jnp.int32, (SPAN, LANES), 0) + (self.start + t * SPAN)
        return jnp.where((key >= self.low) & (key <= self.pos), s, MASKED)

    def all_allowed(self, t):
        first_key = self.start + t * SPAN
        return (first_key >= self.last_low) & (first_key + SPAN <= self.first + 1)


def heads_apart(ref, half, stack):
    row0 = pl.multiple_of(half * HALF, 16)
    for h in range(HEADS):
        stack[h * HALF : (h + 1) * HALF, :] = ref[pl.ds(row0, HALF), h * DH : (h + 1) * DH]


def forward_kernel(
    facts, q_ref, do_ref, k0, k1, k2, k3, stats, out0, out1, out2, out3,
    kbuf, dvacc, s_scr, qs, dos,
):
    place = Place(facts)
    place.gather((k0, k1, k2, k3), kbuf)
    dvacc[...] = jnp.zeros_like(dvacc)

    def one_block(half, carry):
        heads_apart(q_ref, half, qs)
        heads_apart(do_ref, half, dos)
        window = Window(place, half)

        def score(t, mass):
            def some(masked):
                s = window.scores(t, kbuf, qs)
                s = window.masked(t, s) if masked else s
                s_scr[window.kept(t), :] = s
                return mass + fold(jnp.exp2(s), jnp.sum)

            return lax.cond(window.all_allowed(t), lambda: some(False), lambda: some(True))

        mass = lax.fori_loop(0, window.count, score, jnp.zeros((8, LANES), F32))
        log_sum = jnp.log2(jnp.sum(mass, axis=0, keepdims=True))

        def spread(t, carry):
            p = jnp.exp2(s_scr[window.kept(t), :] - log_sum).astype(BF)
            dvacc[window.keys(t), :] += dot(p, dos[...], 1, 0)
            return carry

        lax.fori_loop(0, window.count, spread, 0)
        stats[half] = log_sum
        return carry

    lax.fori_loop(0, 2, one_block, 0)
    place.scatter(dvacc, (out0, out1, out2, out3), 1.0)


def backward_kernel(
    facts, q_ref, do_ref, k0, k1, k2, k3, v0, v1, v2, v3, stats,
    dq_ref, out0, out1, out2, out3,
    kbuf, vbuf, dkacc, p_scr, dp_scr, qs, dos,
):
    place = Place(facts)
    place.gather((k0, k1, k2, k3), kbuf)
    place.gather((v0, v1, v2, v3), vbuf)
    dkacc[...] = jnp.zeros_like(dkacc)

    def one_block(half, carry):
        heads_apart(q_ref, half, qs)
        heads_apart(do_ref, half, dos)
        window = Window(place, half)
        log_sum = stats[half]

        def weigh(t, moment):
            def some(masked):
                s = window.scores(t, kbuf, qs)
                s = window.masked(t, s) if masked else s
                p = jnp.exp2(s - log_sum)
                dp = dot(vbuf[window.keys(t), :], dos[...], 1, 1)
                p_scr[window.kept(t), :] = p
                dp_scr[window.kept(t), :] = dp
                return moment + fold(p * dp, jnp.sum)

            return lax.cond(window.all_allowed(t), lambda: some(False), lambda: some(True))

        moment = lax.fori_loop(0, window.count, weigh, jnp.zeros((8, LANES), F32))
        delta = jnp.sum(moment, axis=0, keepdims=True)

        def spread(t, dqt):
            g = (p_scr[window.kept(t), :] * (dp_scr[window.kept(t), :] - delta)).astype(BF)
            at = window.keys(t)
            dkacc[at, :] += dot(g, qs[...], 1, 0)
            return dqt + dot(kbuf[at, :], g, 0, 0)

        dqt = lax.fori_loop(0, window.count, spread, jnp.zeros((DH, LANES), F32))
        dq = (dqt * SCALE).T.astype(BF)
        row0 = pl.multiple_of(half * HALF, 16)
        for h in range(HEADS):
            dq_ref[pl.ds(row0, HALF), h * DH : (h + 1) * DH] = dq[h * HALF : (h + 1) * HALF, :]
        return carry

    lax.fori_loop(0, 2, one_block, 0)
    place.scatter(dkacc, (out0, out1, out2, out3), SCALE)


SHARES = (jax.ShapeDtypeStruct((4, ROWS, DH), BF),) * 4


def forward(facts, q, do, ks):
    vmem = pl.BlockSpec(memory_space=pltpu.VMEM)
    return pl.pallas_call(
        forward_kernel,
        out_shape=(jax.ShapeDtypeStruct((2, 1, LANES), F32),) + SHARES,
        in_specs=[pl.BlockSpec(memory_space=pltpu.SMEM)] + [vmem] * 6,
        out_specs=(vmem,) * 5,
        scratch_shapes=[
            pltpu.VMEM((PAD + SEQ, DH), BF),
            pltpu.VMEM((PAD + SEQ, DH), F32),
            pltpu.VMEM((STEPS * SPAN, LANES), F32),
            pltpu.VMEM((LANES, DH), BF),
            pltpu.VMEM((LANES, DH), BF),
        ],
        compiler_params=pltpu.CompilerParams(vmem_limit_bytes=32 * 2**20),
        cost_estimate=pl.CostEstimate(flops=3 * 10**9, bytes_accessed=4 * 10**6, transcendentals=2 * 10**6),
    )(facts, q, do, *ks)


def backward(facts, q, do, ks, vs, stats):
    vmem = pl.BlockSpec(memory_space=pltpu.VMEM)
    return pl.pallas_call(
        backward_kernel,
        out_shape=(jax.ShapeDtypeStruct((ROWS, HEADS * DH), BF),) + SHARES,
        in_specs=[pl.BlockSpec(memory_space=pltpu.SMEM)] + [vmem] * 11,
        out_specs=(vmem,) * 5,
        scratch_shapes=[
            pltpu.VMEM((PAD + SEQ, DH), BF),
            pltpu.VMEM((PAD + SEQ, DH), BF),
            pltpu.VMEM((PAD + SEQ, DH), F32),
            pltpu.VMEM((STEPS * SPAN, LANES), F32),
            pltpu.VMEM((STEPS * SPAN, LANES), F32),
            pltpu.VMEM((LANES, DH), BF),
            pltpu.VMEM((LANES, DH), BF),
        ],
        compiler_params=pltpu.CompilerParams(vmem_limit_bytes=32 * 2**20),
        cost_estimate=pl.CostEstimate(
            flops=5 * 10**9, bytes_accessed=5 * 10**6, transcendentals=2 * 10**6
        ),
    )(facts, q, do, *ks, *vs, stats)


def ring(shift):
    return [(i, (i + shift) % 4) for i in range(4)]


def add_up(*xs):
    return functools.reduce(lambda a, b: a + b, [x.astype(F32) for x in xs])


def copy_kernel(*refs):
    for source, target in zip(refs[: len(refs) // 2], refs[len(refs) // 2 :]):
        target[...] = source[...]


def near(*arrays):
    vmem = pl.BlockSpec(memory_space=pltpu.VMEM)
    return pl.pallas_call(
        copy_kernel,
        out_shape=tuple(jax.ShapeDtypeStruct(a.shape, a.dtype) for a in arrays),
        in_specs=[vmem] * len(arrays),
        out_specs=(vmem,) * len(arrays),
        compiler_params=pltpu.CompilerParams(vmem_limit_bytes=16 * 2**20),
    )(*arrays)


def columns_kernel(c0, c1, c2, c3, keys, values):
    for a, ref in enumerate((c0, c1, c2, c3)):
        keys[a] = ref[:, 0:DH]
        values[a] = ref[:, DH : 2 * DH]


def columns_of(pieces):
    vmem = pl.BlockSpec(memory_space=pltpu.VMEM)
    return pl.pallas_call(
        columns_kernel,
        out_shape=SHARES[:2],
        in_specs=[vmem] * 4,
        out_specs=(vmem,) * 2,
        compiler_params=pltpu.CompilerParams(vmem_limit_bytes=16 * 2**20),
    )(*pieces)


def finish_kernel(facts, *refs):
    key_parts, value_parts, (key_out, value_out, mine, sent) = refs[:4], refs[4:8], refs[8:]

    def rounded(parts):
        return functools.reduce(lambda a, b: a + b, [p[...].astype(F32) for p in parts]).astype(BF)

    key, value = rounded(key_parts), rounded(value_parts)
    key_out[...] = key
    value_out[...] = value
    key, value = key.astype(F32), value.astype(F32)
    left = lax.broadcasted_iota(jnp.int32, key.shape, 1) < DH // 2
    low = jnp.where(left, key, pltpu.roll(value, DH // 2, 1)).astype(BF)
    high = jnp.where(left, pltpu.roll(key, DH // 2, 1), value).astype(BF)
    even = lax.rem(facts[DOCS + RANKS], 2) == 0

    @pl.when(even)
    def _():
        mine[...] = low
        sent[...] = high

    @pl.when(jnp.logical_not(even))
    def _():
        mine[...] = high
        sent[...] = low


def finish(facts, key_parts, value_parts):
    vmem = pl.BlockSpec(memory_space=pltpu.VMEM)
    return pl.pallas_call(
        finish_kernel,
        out_shape=(jax.ShapeDtypeStruct((ROWS, DH), BF),) * 4,
        in_specs=[pl.BlockSpec(memory_space=pltpu.SMEM)] + [vmem] * 8,
        out_specs=(vmem,) * 4,
        compiler_params=pltpu.CompilerParams(vmem_limit_bytes=8 * 2**20),
    )(facts, *key_parts, *value_parts)


def product_kernel(
    facts, hid0, hid1, hid2, hid3, row0, row1, row2, row3, out0, out1, out2, out3, acc
):
    my_zl, my_y, my_x, core, zh = (facts[DOCS + RANKS + i] for i in range(5))
    for j, row in enumerate((row0, row1, row2, row3)):
        group = lax.rem(my_x + 4 - j, 4)

        @pl.when(group // 2 == core)
        def _():
            for c in range(4):
                columns = slice(c * 512, (c + 1) * 512)
                total = None
                for i, hidden in enumerate((hid0, hid1, hid2, hid3)):
                    part = dot(row[i * ROWS : (i + 1) * ROWS, :], hidden[:, columns], 0, 0)
                    total = part if total is None else total + part
                acc[...] = total
                side = lax.rem(lax.rem(group, 2) + my_zl // 2, 2)
                for s, out in enumerate((out0, out1, out2, out3)):
                    y = lax.rem(my_y + s, 4)
                    for kind in range(2):
                        at = pl.ds(pl.multiple_of(kind * 64 + y * 16, 16), 16)
                        out[lax.rem(kind + zh, 2), side, :, columns] = acc[at, :].astype(BF)


def weight_product(facts, *operands):
    vmem = pl.BlockSpec(memory_space=pltpu.VMEM)
    return pl.pallas_call(
        product_kernel,
        out_shape=(jax.ShapeDtypeStruct((2, 2, 16, 2048), BF),) * 4,
        in_specs=[pl.BlockSpec(memory_space=pltpu.SMEM)] + [vmem] * 8,
        out_specs=(vmem,) * 4,
        scratch_shapes=[pltpu.VMEM((DH, 512), F32)],
        compiler_params=pltpu.CompilerParams(vmem_limit_bytes=24 * 2**20),
        cost_estimate=pl.CostEstimate(flops=10**9, bytes_accessed=4 * 10**6, transcendentals=0),
    )(facts, *operands)


def after(value, *others):
    return lax.optimization_barrier((value, others))[0]


def per_device(hidden_in, queries, keys_in, values_in, out_grad, doc_lengths, pair_perm):
    zl, y, x = (lax.axis_index(a) for a in ("zl", "y", "x"))
    zh, core = lax.axis_index("zh"), lax.axis_index("co")
    swap = [(0, 1), (1, 0)]
    neighbour = [(0, 1), (1, 0), (2, 3), (3, 2)]
    facts = jnp.concatenate([doc_lengths[0], pair_perm, jnp.stack([zl, y, x, core, zh]).astype(jnp.int32)])

    def moved(value, axis, shift):
        return lax.ppermute(value, axis, ring(shift))

    own = jnp.concatenate([keys_in[0], values_in[0]], axis=1)
    pieces = [own] + [moved(own, "zl", a) for a in (1, 2, 3)]
    rows_in = near(queries[0], out_grad[0])
    hidden = hidden_in[0]
    hidden = (hidden, lax.ppermute(hidden, "co", swap))
    pieces, rows_in, hidden = lax.optimization_barrier((pieces, rows_in, hidden))
    ks, vs = columns_of(pieces)
    ks = [ks] + [moved(ks, "y", s) for s in (1, 2, 3)]
    vs = after(vs, ks[1])
    vs = [vs] + [moved(vs if s != 2 else after(vs, *ks[2:]), "y", s) for s in (1, 2, 3)]

    def received(shares):
        return [shares[0]] + [moved(shares[s], "y", s) for s in (1, 2, 3)]

    def over_zl(got):
        parts = [add_up(*[g[a] for g in got]) for a in range(4)]
        return [parts[0]] + [moved(parts[a].astype(BF), "zl", a) for a in (1, 2, 3)]

    stats, *dvs = forward(facts, *rows_in, ks)
    dvs = received(dvs)
    beside = lax.ppermute(after(hidden[0], stats), "zl", neighbour)
    dq, *dks = backward(facts, *rows_in, ks, vs, stats)
    dks = received(after(dks, dvs))
    key_grads, value_grads, mine, sent = finish(facts, over_zl(dks), over_zl(dvs))

    beside = after(beside, *dks)
    hidden = (hidden[0], beside, hidden[1], lax.ppermute(beside, "co", swap))
    rows = jnp.stack([mine, lax.ppermute(sent, "zl", neighbour)])
    cross = [
        (x0 + 4 * c, x0 + 4 * (1 - c)) for c in range(2) for x0 in range(4) if x0 // 2 == 1 - c
    ]
    rows = jnp.stack([rows, lax.ppermute(rows, ("co", "x"), cross)]).reshape(4 * ROWS, DH)

    def along(j):
        return [
            (x0 + 4 * c, (x0 + j) % 4 + 4 * c) for c in range(2) for x0 in range(4) if x0 // 2 == c
        ]

    rows = [rows] + [lax.ppermute(rows, ("co", "x"), along(j)) for j in (1, 2, 3)]
    shares = received(weight_product(facts, *hidden, *rows))
    total = add_up(*shares)
    other_zl = [(0, 2), (2, 0), (1, 3), (3, 1)]
    both = [(a + 4 * c, b + 4 * (1 - c)) for a, b in other_zl for c in range(2)]
    grad_weight = add_up(
        total[0, 0],
        lax.ppermute(total[0, 1].astype(BF), "zl", other_zl),
        lax.ppermute(total[1, 0].astype(BF), "zh", swap),
        lax.ppermute(total[1, 1].astype(BF), ("zh", "zl"), both),
    )
    return dq[None], key_grads[None], value_grads[None], grad_weight


def solution(mesh):
    fine = Mesh(mesh.devices.reshape(SIZES), CARDINAL)
    dp, ctx, tp = ("zh", "co"), ("zl", "y"), "x"
    tokens = P(dp, ctx, tp)
    return jax.shard_map(
        per_device,
        mesh=fine,
        in_specs=(tokens,) * 5 + (P(dp, None), P()),
        out_specs=(tokens,) * 3 + (P(dp + ctx, tp),),
        check_vma=False,
    )
```

```python
import functools

import jax
import jax.numpy as jnp
import numpy as np
from jax import lax
from jax.experimental import pallas as pl
from jax.experimental.pallas import tpu as pltpu
from jax.sharding import Mesh, PartitionSpec as P

DH = 128
HEADS = 8
HALF = 112
ROWS = 2 * HALF
LANES = HEADS * HALF
RANKS = 16
BLOCKS = 2 * RANKS
SEQ = ROWS * RANKS
DOCS = 6
MAX_DOC = 1194
SPAN = 2 * HALF
STEPS = -(-(MAX_DOC - 1 + HALF) // SPAN)
PAD = SPAN
SCALE = DH**-0.5
LOG2E = 1.4426950408889634
MASKED = -1e30
CARDINAL = ("zh", "co", "zl", "y", "x")
SIZES = (2, 2, 4, 4, 4)
BF = jnp.bfloat16
F32 = jnp.float32


def dot(a, b, ca, cb):
    return lax.dot_general(a, b, (((ca,), (cb,)), ((), ())), preferred_element_type=F32)


def fold(x, op):
    return op(x.reshape(x.shape[0] // 8, 8, x.shape[1]), axis=0)


class Place:
    def __init__(self, facts):
        self.facts = facts
        self.zl, self.y = facts[DOCS + RANKS], facts[DOCS + RANKS + 1]

    def pair(self, rank):
        return self.facts[DOCS + rank]

    def rows(self, zl, y, half):
        pair = self.pair(zl * 4 + y)
        block = pair if half == 0 else BLOCKS - 1 - pair
        return pl.ds(pl.multiple_of(PAD + block * HALF, 16), HALF)

    def gather(self, refs, buf):
        buf[0:PAD, :] = jnp.zeros((PAD, DH), BF)
        for s, ref in enumerate(refs):
            for a in range(4):
                zl, y = lax.rem(self.zl + 4 - a, 4), lax.rem(self.y + 4 - s, 4)
                for half in range(2):
                    rows = slice(half * HALF, (half + 1) * HALF)
                    buf[self.rows(zl, y, half), :] = ref[a, rows, :]

    def scatter(self, acc, refs, scale):
        for s, ref in enumerate(refs):
            for a in range(4):
                zl, y = lax.rem(self.zl + a, 4), lax.rem(self.y + s, 4)
                for half in range(2):
                    rows = slice(half * HALF, (half + 1) * HALF)
                    ref[a, rows, :] = (acc[self.rows(zl, y, half), :] * scale).astype(BF)


class Window:
    def __init__(self, place, half):
        pair = place.pair(place.zl * 4 + place.y)
        block = jnp.where(half == 0, pair, BLOCKS - 1 - pair)
        lane = lax.broadcasted_iota(jnp.int32, (1, LANES), 1)
        within = lane
        for h in range(1, HEADS):
            within = jnp.where(lane >= h * HALF, lane - h * HALF, within)
        first = block * HALF
        self.first = first
        self.pos = within + first
        self.low = jnp.zeros_like(self.pos)
        low0 = jnp.int32(0)
        self.last_low = jnp.int32(0)
        end = jnp.int32(0)
        for d in range(DOCS - 1):
            end = end + place.facts[d]
            self.low = jnp.where(self.pos >= end, end, self.low)
            low0 = jnp.where(first >= end, end, low0)
            self.last_low = jnp.where(first + HALF - 1 >= end, end, self.last_low)
        stop = first + HALF
        self.count = lax.div(stop - low0 + (SPAN - 1), SPAN)
        self.start = stop - self.count * SPAN

    def keys(self, t):
        return pl.ds(pl.multiple_of(PAD + self.start + t * SPAN, 16), SPAN)

    def kept(self, t):
        return pl.ds(pl.multiple_of(t * SPAN, SPAN), SPAN)

    def scores(self, t, kbuf, qs):
        return dot(kbuf[self.keys(t), :], qs[...], 1, 1) * (SCALE * LOG2E)

    def masked(self, t, s):
        key = lax.broadcasted_iota(jnp.int32, (SPAN, LANES), 0) + (self.start + t * SPAN)
        return jnp.where((key >= self.low) & (key <= self.pos), s, MASKED)

    def all_allowed(self, t):
        first_key = self.start + t * SPAN
        return (first_key >= self.last_low) & (first_key + SPAN <= self.first + 1)


def heads_apart(ref, half, stack):
    row0 = pl.multiple_of(half * HALF, 16)
    for h in range(HEADS):
        stack[h * HALF : (h + 1) * HALF, :] = ref[pl.ds(row0, HALF), h * DH : (h + 1) * DH]


def forward_kernel(
    facts, q_ref, do_ref, k0, k1, k2, k3, stats, out0, out1, out2, out3,
    kbuf, dvacc, s_scr, qs, dos,
):
    place = Place(facts)
    place.gather((k0, k1, k2, k3), kbuf)
    dvacc[...] = jnp.zeros_like(dvacc)

    def one_block(half, carry):
        heads_apart(q_ref, half, qs)
        heads_apart(do_ref, half, dos)
        window = Window(place, half)

        def score(t, mass):
            def some(masked):
                s = window.scores(t, kbuf, qs)
                s = window.masked(t, s) if masked else s
                s_scr[window.kept(t), :] = s
                return mass + fold(jnp.exp2(s), jnp.sum)

            return lax.cond(window.all_allowed(t), lambda: some(False), lambda: some(True))

        mass = lax.fori_loop(0, window.count, score, jnp.zeros((8, LANES), F32))
        log_sum = jnp.log2(jnp.sum(mass, axis=0, keepdims=True))

        def spread(t, carry):
            p = jnp.exp2(s_scr[window.kept(t), :] - log_sum).astype(BF)
            dvacc[window.keys(t), :] += dot(p, dos[...], 1, 0)
            return carry

        lax.fori_loop(0, window.count, spread, 0)
        stats[half] = log_sum
        return carry

    lax.fori_loop(0, 2, one_block, 0)
    place.scatter(dvacc, (out0, out1, out2, out3), 1.0)


def backward_kernel(
    facts, q_ref, do_ref, k0, k1, k2, k3, v0, v1, v2, v3, stats,
    dq_ref, out0, out1, out2, out3,
    kbuf, vbuf, dkacc, p_scr, dp_scr, qs, dos,
):
    place = Place(facts)
    place.gather((k0, k1, k2, k3), kbuf)
    place.gather((v0, v1, v2, v3), vbuf)
    dkacc[...] = jnp.zeros_like(dkacc)

    def one_block(half, carry):
        heads_apart(q_ref, half, qs)
        heads_apart(do_ref, half, dos)
        window = Window(place, half)
        log_sum = stats[half]

        def weigh(t, moment):
            def some(masked):
                s = window.scores(t, kbuf, qs)
                s = window.masked(t, s) if masked else s
                p = jnp.exp2(s - log_sum)
                dp = dot(vbuf[window.keys(t), :], dos[...], 1, 1)
                p_scr[window.kept(t), :] = p
                dp_scr[window.kept(t), :] = dp
                return moment + fold(p * dp, jnp.sum)

            return lax.cond(window.all_allowed(t), lambda: some(False), lambda: some(True))

        moment = lax.fori_loop(0, window.count, weigh, jnp.zeros((8, LANES), F32))
        delta = jnp.sum(moment, axis=0, keepdims=True)

        def spread(t, dqt):
            g = (p_scr[window.kept(t), :] * (dp_scr[window.kept(t), :] - delta)).astype(BF)
            at = window.keys(t)
            dkacc[at, :] += dot(g, qs[...], 1, 0)
            return dqt + dot(kbuf[at, :], g, 0, 0)

        dqt = lax.fori_loop(0, window.count, spread, jnp.zeros((DH, LANES), F32))
        dq = (dqt * SCALE).T.astype(BF)
        row0 = pl.multiple_of(half * HALF, 16)
        for h in range(HEADS):
            dq_ref[pl.ds(row0, HALF), h * DH : (h + 1) * DH] = dq[h * HALF : (h + 1) * HALF, :]
        return carry

    lax.fori_loop(0, 2, one_block, 0)
    place.scatter(dkacc, (out0, out1, out2, out3), SCALE)


SHARES = (jax.ShapeDtypeStruct((4, ROWS, DH), BF),) * 4


def forward(facts, q, do, ks):
    vmem = pl.BlockSpec(memory_space=pltpu.VMEM)
    return pl.pallas_call(
        forward_kernel,
        out_shape=(jax.ShapeDtypeStruct((2, 1, LANES), F32),) + SHARES,
        in_specs=[pl.BlockSpec(memory_space=pltpu.SMEM)] + [vmem] * 6,
        out_specs=(vmem,) * 5,
        scratch_shapes=[
            pltpu.VMEM((PAD + SEQ, DH), BF),
            pltpu.VMEM((PAD + SEQ, DH), F32),
            pltpu.VMEM((STEPS * SPAN, LANES), F32),
            pltpu.VMEM((LANES, DH), BF),
            pltpu.VMEM((LANES, DH), BF),
        ],
        compiler_params=pltpu.CompilerParams(vmem_limit_bytes=32 * 2**20),
        cost_estimate=pl.CostEstimate(flops=3 * 10**9, bytes_accessed=4 * 10**6, transcendentals=2 * 10**6),
    )(facts, q, do, *ks)


def backward(facts, q, do, ks, vs, stats):
    vmem = pl.BlockSpec(memory_space=pltpu.VMEM)
    return pl.pallas_call(
        backward_kernel,
        out_shape=(jax.ShapeDtypeStruct((ROWS, HEADS * DH), BF),) + SHARES,
        in_specs=[pl.BlockSpec(memory_space=pltpu.SMEM)] + [vmem] * 11,
        out_specs=(vmem,) * 5,
        scratch_shapes=[
            pltpu.VMEM((PAD + SEQ, DH), BF),
            pltpu.VMEM((PAD + SEQ, DH), BF),
            pltpu.VMEM((PAD + SEQ, DH), F32),
            pltpu.VMEM((STEPS * SPAN, LANES), F32),
            pltpu.VMEM((STEPS * SPAN, LANES), F32),
            pltpu.VMEM((LANES, DH), BF),
            pltpu.VMEM((LANES, DH), BF),
        ],
        compiler_params=pltpu.CompilerParams(vmem_limit_bytes=32 * 2**20),
        cost_estimate=pl.CostEstimate(
            flops=5 * 10**9, bytes_accessed=5 * 10**6, transcendentals=2 * 10**6
        ),
    )(facts, q, do, *ks, *vs, stats)


def ring(shift):
    return [(i, (i + shift) % 4) for i in range(4)]


def add_up(*xs):
    return functools.reduce(lambda a, b: a + b, [x.astype(F32) for x in xs])


def copy_kernel(*refs):
    for source, target in zip(refs[: len(refs) // 2], refs[len(refs) // 2 :]):
        target[...] = source[...]


def near(*arrays):
    vmem = pl.BlockSpec(memory_space=pltpu.VMEM)
    return pl.pallas_call(
        copy_kernel,
        out_shape=tuple(jax.ShapeDtypeStruct(a.shape, a.dtype) for a in arrays),
        in_specs=[vmem] * len(arrays),
        out_specs=(vmem,) * len(arrays),
        compiler_params=pltpu.CompilerParams(vmem_limit_bytes=16 * 2**20),
    )(*arrays)


def stack_kernel(c0, c1, c2, c3, out):
    for a, ref in enumerate((c0, c1, c2, c3)):
        out[a] = ref[...]


def stacked(pieces):
    vmem = pl.BlockSpec(memory_space=pltpu.VMEM)
    return pl.pallas_call(
        stack_kernel,
        out_shape=SHARES[0],
        in_specs=[vmem] * 4,
        out_specs=vmem,
        compiler_params=pltpu.CompilerParams(vmem_limit_bytes=16 * 2**20),
    )(*pieces)


def finish_kernel(facts, *refs):
    key_parts, value_parts, (key_out, value_out, mine, sent) = refs[:4], refs[4:8], refs[8:]

    def rounded(parts):
        return functools.reduce(lambda a, b: a + b, [p[...].astype(F32) for p in parts]).astype(BF)

    key, value = rounded(key_parts), rounded(value_parts)
    key_out[...] = key
    value_out[...] = value
    key, value = key.astype(F32), value.astype(F32)
    left = lax.broadcasted_iota(jnp.int32, key.shape, 1) < DH // 2
    low = jnp.where(left, key, pltpu.roll(value, DH // 2, 1)).astype(BF)
    high = jnp.where(left, pltpu.roll(key, DH // 2, 1), value).astype(BF)
    even = lax.rem(facts[DOCS + RANKS], 2) == 0

    @pl.when(even)
    def _():
        mine[...] = low
        sent[...] = high

    @pl.when(jnp.logical_not(even))
    def _():
        mine[...] = high
        sent[...] = low


def finish(facts, key_parts, value_parts):
    vmem = pl.BlockSpec(memory_space=pltpu.VMEM)
    return pl.pallas_call(
        finish_kernel,
        out_shape=(jax.ShapeDtypeStruct((ROWS, DH), BF),) * 4,
        in_specs=[pl.BlockSpec(memory_space=pltpu.SMEM)] + [vmem] * 8,
        out_specs=(vmem,) * 4,
        compiler_params=pltpu.CompilerParams(vmem_limit_bytes=8 * 2**20),
    )(facts, *key_parts, *value_parts)


def product_kernel(
    facts, hid0, hid1, hid2, hid3, row0, row1, row2, row3, out0, out1, out2, out3, acc
):
    my_zl, my_y, my_x, core, zh = (facts[DOCS + RANKS + i] for i in range(5))
    for j, row in enumerate((row0, row1, row2, row3)):
        group = lax.rem(my_x + 4 - j, 4)

        @pl.when(group // 2 == core)
        def _():
            for c in range(4):
                columns = slice(c * 512, (c + 1) * 512)
                total = None
                for i, hidden in enumerate((hid0, hid1, hid2, hid3)):
                    part = dot(row[i * ROWS : (i + 1) * ROWS, :], hidden[:, columns], 0, 0)
                    total = part if total is None else total + part
                acc[...] = total
                side = lax.rem(lax.rem(group, 2) + my_zl // 2, 2)
                for s, out in enumerate((out0, out1, out2, out3)):
                    y = lax.rem(my_y + s, 4)
                    for kind in range(2):
                        at = pl.ds(pl.multiple_of(kind * 64 + y * 16, 16), 16)
                        out[lax.rem(kind + zh, 2), side, :, columns] = acc[at, :].astype(BF)


def weight_product(facts, *operands):
    vmem = pl.BlockSpec(memory_space=pltpu.VMEM)
    return pl.pallas_call(
        product_kernel,
        out_shape=(jax.ShapeDtypeStruct((2, 2, 16, 2048), BF),) * 4,
        in_specs=[pl.BlockSpec(memory_space=pltpu.SMEM)] + [vmem] * 8,
        out_specs=(vmem,) * 4,
        scratch_shapes=[pltpu.VMEM((DH, 512), F32)],
        compiler_params=pltpu.CompilerParams(vmem_limit_bytes=24 * 2**20),
        cost_estimate=pl.CostEstimate(flops=10**9, bytes_accessed=4 * 10**6, transcendentals=0),
    )(facts, *operands)


def after(value, *others):
    return lax.optimization_barrier((value, others))[0]


def per_device(hidden_in, queries, keys_in, values_in, out_grad, doc_lengths, pair_perm):
    zl, y, x = (lax.axis_index(a) for a in ("zl", "y", "x"))
    zh, core = lax.axis_index("zh"), lax.axis_index("co")
    swap = [(0, 1), (1, 0)]
    neighbour = [(0, 1), (1, 0), (2, 3), (3, 2)]
    facts = jnp.concatenate([doc_lengths[0], pair_perm, jnp.stack([zl, y, x, core, zh]).astype(jnp.int32)])

    def moved(value, axis, shift):
        return lax.ppermute(value, axis, ring(shift))

    ks, vs = (
        [own] + [moved(own, "zl", a) for a in (1, 2, 3)] for own in (keys_in[0], values_in[0])
    )
    rows_in = near(queries[0], out_grad[0])
    ks, vs, rows_in = lax.optimization_barrier((ks, vs, rows_in))
    ks = stacked(ks)
    ks = [ks] + [moved(ks, "y", s) for s in (1, 2, 3)]
    vs = after(stacked(vs), ks[1])
    vs = [vs] + [moved(vs if s != 2 else after(vs, *ks[2:]), "y", s) for s in (1, 2, 3)]

    def received(shares):
        return [shares[0]] + [moved(shares[s], "y", s) for s in (1, 2, 3)]

    def over_zl(got):
        parts = [add_up(*[g[a] for g in got]) for a in range(4)]
        return [parts[0]] + [moved(parts[a].astype(BF), "zl", a) for a in (1, 2, 3)]

    stats, *dvs = forward(facts, *rows_in, ks)
    dvs = received(dvs)
    hidden = hidden_in[0]
    beside = lax.ppermute(after(hidden, stats), "zl", neighbour)
    dq, *dks = backward(facts, *rows_in, ks, vs, stats)
    dks = received(after(dks, dvs[1]))
    key_grads, value_grads, mine, sent = finish(facts, over_zl(dks), over_zl(dvs))

    hidden = after((hidden, beside), *dks)
    hidden = (*hidden, *(lax.ppermute(h, "co", swap) for h in hidden))
    rows = jnp.stack([mine, lax.ppermute(sent, "zl", neighbour)])
    cross = [
        (x0 + 4 * c, x0 + 4 * (1 - c)) for c in range(2) for x0 in range(4) if x0 // 2 == 1 - c
    ]
    rows = jnp.stack([rows, lax.ppermute(rows, ("co", "x"), cross)]).reshape(4 * ROWS, DH)

    def along(j):
        return [
            (x0 + 4 * c, (x0 + j) % 4 + 4 * c) for c in range(2) for x0 in range(4) if x0 // 2 == c
        ]

    rows = [rows] + [lax.ppermute(rows, ("co", "x"), along(j)) for j in (1, 2, 3)]
    shares = received(weight_product(facts, *hidden, *rows))
    total = add_up(*shares)
    other_zl = [(0, 2), (2, 0), (1, 3), (3, 1)]
    both = [(a + 4 * c, b + 4 * (1 - c)) for a, b in other_zl for c in range(2)]
    grad_weight = add_up(
        total[0, 0],
        lax.ppermute(total[1, 0].astype(BF), "zh", swap),
        lax.ppermute(total[1, 1].astype(BF), ("zh", "zl"), both),
        lax.ppermute(total[0, 1].astype(BF), "zl", other_zl),
    )
    return dq[None], key_grads[None], value_grads[None], grad_weight


def solution(mesh):
    fine = Mesh(mesh.devices.reshape(SIZES), CARDINAL)
    dp, ctx, tp = ("zh", "co"), ("zl", "y"), "x"
    tokens = P(dp, ctx, tp)
    return jax.shard_map(
        per_device,
        mesh=fine,
        in_specs=(tokens,) * 5 + (P(dp, None), P()),
        out_specs=(tokens,) * 3 + (P(dp + ctx, tp),),
        check_vma=False,
    )
```

```python
import functools

import jax
import jax.numpy as jnp
import numpy as np
from jax import lax
from jax.experimental import pallas as pl
from jax.experimental.pallas import tpu as pltpu
from jax.sharding import Mesh, PartitionSpec as P

DH = 128
HEADS = 8
HALF = 112
ROWS = 2 * HALF
LANES = HEADS * HALF
RANKS = 16
BLOCKS = 2 * RANKS
SEQ = ROWS * RANKS
DOCS = 6
MAX_DOC = 1194
SPAN = 2 * HALF
STEPS = -(-(MAX_DOC - 1 + HALF) // SPAN)
PAD = SPAN
SCALE = DH**-0.5
LOG2E = 1.4426950408889634
MASKED = -1e30
CARDINAL = ("zh", "co", "zl", "y", "x")
SIZES = (2, 2, 4, 4, 4)
BF = jnp.bfloat16
F32 = jnp.float32


def dot(a, b, ca, cb):
    return lax.dot_general(a, b, (((ca,), (cb,)), ((), ())), preferred_element_type=F32)


def fold(x, op):
    return op(x.reshape(x.shape[0] // 8, 8, x.shape[1]), axis=0)


class Place:
    def __init__(self, facts):
        self.facts = facts
        self.zl, self.y = facts[DOCS + RANKS], facts[DOCS + RANKS + 1]

    def pair(self, rank):
        return self.facts[DOCS + rank]

    def rows(self, zl, y, half):
        pair = self.pair(zl * 4 + y)
        block = pair if half == 0 else BLOCKS - 1 - pair
        return pl.ds(pl.multiple_of(PAD + block * HALF, 16), HALF)

    def gather(self, refs, buf):
        buf[0:PAD, :] = jnp.zeros((PAD, DH), BF)
        for s, ref in enumerate(refs):
            for a in range(4):
                zl, y = lax.rem(self.zl + 4 - a, 4), lax.rem(self.y + 4 - s, 4)
                for half in range(2):
                    rows = slice(half * HALF, (half + 1) * HALF)
                    buf[self.rows(zl, y, half), :] = ref[a, rows, :]

    def scatter(self, acc, refs, scale):
        for s, ref in enumerate(refs):
            for a in range(4):
                zl, y = lax.rem(self.zl + a, 4), lax.rem(self.y + s, 4)
                for half in range(2):
                    rows = slice(half * HALF, (half + 1) * HALF)
                    ref[a, rows, :] = (acc[self.rows(zl, y, half), :] * scale).astype(BF)


class Window:
    def __init__(self, place, half):
        pair = place.pair(place.zl * 4 + place.y)
        block = jnp.where(half == 0, pair, BLOCKS - 1 - pair)
        lane = lax.broadcasted_iota(jnp.int32, (1, LANES), 1)
        within = lane
        for h in range(1, HEADS):
            within = jnp.where(lane >= h * HALF, lane - h * HALF, within)
        first = block * HALF
        self.first = first
        self.pos = within + first
        self.low = jnp.zeros_like(self.pos)
        low0 = jnp.int32(0)
        self.last_low = jnp.int32(0)
        end = jnp.int32(0)
        for d in range(DOCS - 1):
            end = end + place.facts[d]
            self.low = jnp.where(self.pos >= end, end, self.low)
            low0 = jnp.where(first >= end, end, low0)
            self.last_low = jnp.where(first + HALF - 1 >= end, end, self.last_low)
        stop = first + HALF
        self.count = lax.div(stop - low0 + (SPAN - 1), SPAN)
        self.start = stop - self.count * SPAN

    def keys(self, t):
        return pl.ds(pl.multiple_of(PAD + self.start + t * SPAN, 16), SPAN)

    def kept(self, t):
        return pl.ds(pl.multiple_of(t * SPAN, SPAN), SPAN)

    def scores(self, t, kbuf, qs):
        return dot(kbuf[self.keys(t), :], qs[...], 1, 1) * (SCALE * LOG2E)

    def masked(self, t, s):
        key = lax.broadcasted_iota(jnp.int32, (SPAN, LANES), 0) + (self.start + t * SPAN)
        return jnp.where((key >= self.low) & (key <= self.pos), s, MASKED)

    def all_allowed(self, t):
        first_key = self.start + t * SPAN
        return (first_key >= self.last_low) & (first_key + SPAN <= self.first + 1)


def heads_apart(ref, half, stack):
    row0 = pl.multiple_of(half * HALF, 16)
    for h in range(HEADS):
        stack[h * HALF : (h + 1) * HALF, :] = ref[pl.ds(row0, HALF), h * DH : (h + 1) * DH]


def forward_kernel(
    facts, q_ref, do_ref, k0, k1, k2, k3, stats, out0, out1, out2, out3,
    kbuf, dvacc, s_scr, qs, dos,
):
    place = Place(facts)
    place.gather((k0, k1, k2, k3), kbuf)
    dvacc[...] = jnp.zeros_like(dvacc)

    def one_block(half, carry):
        heads_apart(q_ref, half, qs)
        heads_apart(do_ref, half, dos)
        window = Window(place, half)

        def score(t, mass):
            def some(masked):
                s = window.scores(t, kbuf, qs)
                s = window.masked(t, s) if masked else s
                s_scr[window.kept(t), :] = s
                return mass + fold(jnp.exp2(s), jnp.sum)

            return lax.cond(window.all_allowed(t), lambda: some(False), lambda: some(True))

        mass = lax.fori_loop(0, window.count, score, jnp.zeros((8, LANES), F32))
        log_sum = jnp.log2(jnp.sum(mass, axis=0, keepdims=True))

        def spread(t, carry):
            p = jnp.exp2(s_scr[window.kept(t), :] - log_sum).astype(BF)
            dvacc[window.keys(t), :] += dot(p, dos[...], 1, 0)
            return carry

        lax.fori_loop(0, window.count, spread, 0)
        stats[half] = log_sum
        return carry

    lax.fori_loop(0, 2, one_block, 0)
    place.scatter(dvacc, (out0, out1, out2, out3), 1.0)


def backward_kernel(
    facts, q_ref, do_ref, k0, k1, k2, k3, v0, v1, v2, v3, stats,
    dq_ref, out0, out1, out2, out3,
    kbuf, vbuf, dkacc, p_scr, dp_scr, qs, dos,
):
    place = Place(facts)
    place.gather((k0, k1, k2, k3), kbuf)
    place.gather((v0, v1, v2, v3), vbuf)
    dkacc[...] = jnp.zeros_like(dkacc)

    def one_block(half, carry):
        heads_apart(q_ref, half, qs)
        heads_apart(do_ref, half, dos)
        window = Window(place, half)
        log_sum = stats[half]

        def weigh(t, moment):
            def some(masked):
                s = window.scores(t, kbuf, qs)
                s = window.masked(t, s) if masked else s
                p = jnp.exp2(s - log_sum)
                dp = dot(vbuf[window.keys(t), :], dos[...], 1, 1)
                p_scr[window.kept(t), :] = p
                dp_scr[window.kept(t), :] = dp
                return moment + fold(p * dp, jnp.sum)

            return lax.cond(window.all_allowed(t), lambda: some(False), lambda: some(True))

        moment = lax.fori_loop(0, window.count, weigh, jnp.zeros((8, LANES), F32))
        delta = jnp.sum(moment, axis=0, keepdims=True)

        def spread(t, dqt):
            g = (p_scr[window.kept(t), :] * (dp_scr[window.kept(t), :] - delta)).astype(BF)
            at = window.keys(t)
            dkacc[at, :] += dot(g, qs[...], 1, 0)
            return dqt + dot(kbuf[at, :], g, 0, 0)

        dqt = lax.fori_loop(0, window.count, spread, jnp.zeros((DH, LANES), F32))
        dq = (dqt * SCALE).T.astype(BF)
        row0 = pl.multiple_of(half * HALF, 16)
        for h in range(HEADS):
            dq_ref[pl.ds(row0, HALF), h * DH : (h + 1) * DH] = dq[h * HALF : (h + 1) * HALF, :]
        return carry

    lax.fori_loop(0, 2, one_block, 0)
    place.scatter(dkacc, (out0, out1, out2, out3), SCALE)


SHARES = (jax.ShapeDtypeStruct((4, ROWS, DH), BF),) * 4


def forward(facts, q, do, ks):
    vmem = pl.BlockSpec(memory_space=pltpu.VMEM)
    return pl.pallas_call(
        forward_kernel,
        out_shape=(jax.ShapeDtypeStruct((2, 1, LANES), F32),) + SHARES,
        in_specs=[pl.BlockSpec(memory_space=pltpu.SMEM)] + [vmem] * 6,
        out_specs=(vmem,) * 5,
        scratch_shapes=[
            pltpu.VMEM((PAD + SEQ, DH), BF),
            pltpu.VMEM((PAD + SEQ, DH), F32),
            pltpu.VMEM((STEPS * SPAN, LANES), F32),
            pltpu.VMEM((LANES, DH), BF),
            pltpu.VMEM((LANES, DH), BF),
        ],
        compiler_params=pltpu.CompilerParams(vmem_limit_bytes=32 * 2**20),
        cost_estimate=pl.CostEstimate(flops=3 * 10**9, bytes_accessed=4 * 10**6, transcendentals=2 * 10**6),
    )(facts, q, do, *ks)


def backward(facts, q, do, ks, vs, stats):
    vmem = pl.BlockSpec(memory_space=pltpu.VMEM)
    return pl.pallas_call(
        backward_kernel,
        out_shape=(jax.ShapeDtypeStruct((ROWS, HEADS * DH), BF),) + SHARES,
        in_specs=[pl.BlockSpec(memory_space=pltpu.SMEM)] + [vmem] * 11,
        out_specs=(vmem,) * 5,
        scratch_shapes=[
            pltpu.VMEM((PAD + SEQ, DH), BF),
            pltpu.VMEM((PAD + SEQ, DH), BF),
            pltpu.VMEM((PAD + SEQ, DH), F32),
            pltpu.VMEM((STEPS * SPAN, LANES), F32),
            pltpu.VMEM((STEPS * SPAN, LANES), F32),
            pltpu.VMEM((LANES, DH), BF),
            pltpu.VMEM((LANES, DH), BF),
        ],
        compiler_params=pltpu.CompilerParams(vmem_limit_bytes=32 * 2**20),
        cost_estimate=pl.CostEstimate(
            flops=5 * 10**9, bytes_accessed=5 * 10**6, transcendentals=2 * 10**6
        ),
    )(facts, q, do, *ks, *vs, stats)


def ring(shift):
    return [(i, (i + shift) % 4) for i in range(4)]


def add_up(*xs):
    return functools.reduce(lambda a, b: a + b, [x.astype(F32) for x in xs])


def copy_kernel(*refs):
    for source, target in zip(refs[: len(refs) // 2], refs[len(refs) // 2 :]):
        target[...] = source[...]


def near(*arrays):
    vmem = pl.BlockSpec(memory_space=pltpu.VMEM)
    return pl.pallas_call(
        copy_kernel,
        out_shape=tuple(jax.ShapeDtypeStruct(a.shape, a.dtype) for a in arrays),
        in_specs=[vmem] * len(arrays),
        out_specs=(vmem,) * len(arrays),
        compiler_params=pltpu.CompilerParams(vmem_limit_bytes=16 * 2**20),
    )(*arrays)


def stack_kernel(c0, c1, c2, c3, out):
    for a, ref in enumerate((c0, c1, c2, c3)):
        out[a] = ref[...]


def stacked(pieces):
    vmem = pl.BlockSpec(memory_space=pltpu.VMEM)
    return pl.pallas_call(
        stack_kernel,
        out_shape=SHARES[0],
        in_specs=[vmem] * 4,
        out_specs=vmem,
        compiler_params=pltpu.CompilerParams(vmem_limit_bytes=16 * 2**20),
    )(*pieces)


def finish_kernel(facts, *refs):
    key_parts, value_parts, (key_out, value_out, mine, sent) = refs[:4], refs[4:8], refs[8:]

    def rounded(parts):
        return functools.reduce(lambda a, b: a + b, [p[...].astype(F32) for p in parts]).astype(BF)

    key, value = rounded(key_parts), rounded(value_parts)
    key_out[...] = key
    value_out[...] = value
    key, value = key.astype(F32), value.astype(F32)
    left = lax.broadcasted_iota(jnp.int32, key.shape, 1) < DH // 2
    low = jnp.where(left, key, pltpu.roll(value, DH // 2, 1)).astype(BF)
    high = jnp.where(left, pltpu.roll(key, DH // 2, 1), value).astype(BF)
    even = lax.rem(facts[DOCS + RANKS], 2) == 0

    @pl.when(even)
    def _():
        mine[...] = low
        sent[...] = high

    @pl.when(jnp.logical_not(even))
    def _():
        mine[...] = high
        sent[...] = low


def finish(facts, key_parts, value_parts):
    vmem = pl.BlockSpec(memory_space=pltpu.VMEM)
    return pl.pallas_call(
        finish_kernel,
        out_shape=(jax.ShapeDtypeStruct((ROWS, DH), BF),) * 4,
        in_specs=[pl.BlockSpec(memory_space=pltpu.SMEM)] + [vmem] * 8,
        out_specs=(vmem,) * 4,
        compiler_params=pltpu.CompilerParams(vmem_limit_bytes=8 * 2**20),
    )(facts, *key_parts, *value_parts)


def product_kernel(
    facts, hid0, hid1, hid2, hid3, row0, row2, row1, row3, out0, out1, out2, out3, acc
):
    my_zl, my_y, my_x, core, zh = (facts[DOCS + RANKS + i] for i in range(5))
    for j, row in enumerate((row0, row1, row2, row3)):
        group = lax.rem(my_x + 4 - j, 4)

        @pl.when(group // 2 == core)
        def _():
            for c in range(4):
                columns = slice(c * 512, (c + 1) * 512)
                total = None
                for i, hidden in enumerate((hid0, hid1, hid2, hid3)):
                    part = dot(row[i * ROWS : (i + 1) * ROWS, :], hidden[:, columns], 0, 0)
                    total = part if total is None else total + part
                acc[...] = total
                side = lax.rem(lax.rem(group, 2) + my_zl // 2, 2)
                for s, out in enumerate((out0, out1, out2, out3)):
                    y = lax.rem(my_y + s, 4)
                    for kind in range(2):
                        at = pl.ds(pl.multiple_of(kind * 64 + y * 16, 16), 16)
                        out[lax.rem(kind + zh, 2), side, :, columns] = acc[at, :].astype(BF)


def weight_product(facts, *operands):
    vmem = pl.BlockSpec(memory_space=pltpu.VMEM)
    return pl.pallas_call(
        product_kernel,
        out_shape=(jax.ShapeDtypeStruct((2, 2, 16, 2048), BF),) * 4,
        in_specs=[pl.BlockSpec(memory_space=pltpu.SMEM)] + [vmem] * 8,
        out_specs=(vmem,) * 4,
        scratch_shapes=[pltpu.VMEM((DH, 512), F32)],
        compiler_params=pltpu.CompilerParams(vmem_limit_bytes=24 * 2**20),
        cost_estimate=pl.CostEstimate(flops=10**9, bytes_accessed=4 * 10**6, transcendentals=0),
    )(facts, *operands)


def after(value, *others):
    return lax.optimization_barrier((value, others))[0]


def per_device(hidden_in, queries, keys_in, values_in, out_grad, doc_lengths, pair_perm):
    zl, y, x = (lax.axis_index(a) for a in ("zl", "y", "x"))
    zh, core = lax.axis_index("zh"), lax.axis_index("co")
    swap = [(0, 1), (1, 0)]
    neighbour = [(0, 1), (1, 0), (2, 3), (3, 2)]
    facts = jnp.concatenate([doc_lengths[0], pair_perm, jnp.stack([zl, y, x, core, zh]).astype(jnp.int32)])

    def moved(value, axis, shift):
        return lax.ppermute(value, axis, ring(shift))

    ks, vs = (
        [own] + [moved(own, "zl", a) for a in (1, 2, 3)] for own in (keys_in[0], values_in[0])
    )
    rows_in = near(queries[0], out_grad[0])
    ks, vs, rows_in = lax.optimization_barrier((ks, vs, rows_in))
    ks = stacked(ks)
    ks = [ks] + [moved(ks, "y", s) for s in (1, 2, 3)]
    vs = after(stacked(vs), ks[1])
    vs = [vs] + [moved(vs if s != 2 else after(vs, *ks[2:]), "y", s) for s in (1, 2, 3)]

    def received(shares):
        return [shares[0]] + [moved(shares[s], "y", s) for s in (1, 3, 2)]

    def over_zl(got):
        parts = [add_up(*[g[a] for g in got]) for a in range(4)]
        return [parts[0]] + [moved(parts[a].astype(BF), "zl", a) for a in (1, 2, 3)]

    stats, *dvs = forward(facts, *rows_in, ks)
    dvs = received(dvs)
    hidden = hidden_in[0]
    beside = lax.ppermute(after(hidden, stats), "zl", neighbour)
    dq, *dks = backward(facts, *rows_in, ks, vs, stats)
    dks = received(after(dks, dvs[1]))
    key_grads, value_grads, mine, sent = finish(facts, over_zl(dks), over_zl(dvs))

    hidden = after((hidden, beside), *dks)
    hidden = (*hidden, *(lax.ppermute(h, "co", swap) for h in hidden))
    rows = jnp.stack([mine, lax.ppermute(sent, "zl", neighbour)])
    cross = [
        (x0 + 4 * c, x0 + 4 * (1 - c)) for c in range(2) for x0 in range(4) if x0 // 2 == 1 - c
    ]
    rows = jnp.stack([rows, lax.ppermute(rows, ("co", "x"), cross)]).reshape(4 * ROWS, DH)

    def along(j):
        return [
            (x0 + 4 * c, (x0 + j) % 4 + 4 * c) for c in range(2) for x0 in range(4) if x0 // 2 == c
        ]

    rows = [rows] + [lax.ppermute(rows, ("co", "x"), along(j)) for j in (1, 2, 3)]
    shares = received(weight_product(facts, *hidden, rows[0], rows[2], rows[1], rows[3]))
    total = add_up(*shares)
    other_zl = [(0, 2), (2, 0), (1, 3), (3, 1)]
    both = [(a + 4 * c, b + 4 * (1 - c)) for a, b in other_zl for c in range(2)]
    grad_weight = add_up(
        total[0, 0],
        lax.ppermute(total[0, 1].astype(BF), "zl", other_zl),
        lax.ppermute(total[1, 0].astype(BF), "zh", swap),
        lax.ppermute(total[1, 1].astype(BF), ("zh", "zl"), both),
    )
    return dq[None], key_grads[None], value_grads[None], grad_weight


def solution(mesh):
    fine = Mesh(mesh.devices.reshape(SIZES), CARDINAL)
    dp, ctx, tp = ("zh", "co"), ("zl", "y"), "x"
    tokens = P(dp, ctx, tp)
    return jax.shard_map(
        per_device,
        mesh=fine,
        in_specs=(tokens,) * 5 + (P(dp, None), P()),
        out_specs=(tokens,) * 3 + (P(dp + ctx, tp),),
        check_vma=False,
    )
```

```python
import functools

import jax
import jax.numpy as jnp
import numpy as np
from jax import lax
from jax.experimental import pallas as pl
from jax.experimental.pallas import tpu as pltpu
from jax.sharding import Mesh, PartitionSpec as P

DH = 128
HEADS = 8
HALF = 112
ROWS = 2 * HALF
LANES = HEADS * HALF
RANKS = 16
BLOCKS = 2 * RANKS
SEQ = ROWS * RANKS
DOCS = 6
MAX_DOC = 1194
SPAN = 2 * HALF
STEPS = -(-(MAX_DOC - 1 + HALF) // SPAN)
PAD = SPAN
SCALE = DH**-0.5
LOG2E = 1.4426950408889634
MASKED = -1e30
CARDINAL = ("zh", "co", "zl", "y", "x")
SIZES = (2, 2, 4, 4, 4)
BF = jnp.bfloat16
F32 = jnp.float32


def dot(a, b, ca, cb):
    return lax.dot_general(a, b, (((ca,), (cb,)), ((), ())), preferred_element_type=F32)


def fold(x, op):
    return op(x.reshape(x.shape[0] // 8, 8, x.shape[1]), axis=0)


class Place:
    def __init__(self, facts):
        self.facts = facts
        self.zl, self.y = facts[DOCS + RANKS], facts[DOCS + RANKS + 1]

    def pair(self, rank):
        return self.facts[DOCS + rank]

    def rows(self, zl, y, half):
        pair = self.pair(zl * 4 + y)
        block = pair if half == 0 else BLOCKS - 1 - pair
        return pl.ds(pl.multiple_of(PAD + block * HALF, 16), HALF)

    def gather(self, refs, buf):
        buf[0:PAD, :] = jnp.zeros((PAD, DH), BF)
        for s, ref in enumerate(refs):
            for a in range(4):
                zl, y = lax.rem(self.zl + 4 - a, 4), lax.rem(self.y + 4 - s, 4)
                for half in range(2):
                    rows = slice(half * HALF, (half + 1) * HALF)
                    buf[self.rows(zl, y, half), :] = ref[a, rows, :]

    def scatter(self, acc, refs, scale):
        for s, ref in enumerate(refs):
            for a in range(4):
                zl, y = lax.rem(self.zl + a, 4), lax.rem(self.y + s, 4)
                for half in range(2):
                    rows = slice(half * HALF, (half + 1) * HALF)
                    ref[a, rows, :] = (acc[self.rows(zl, y, half), :] * scale).astype(BF)


class Window:
    def __init__(self, place, half):
        pair = place.pair(place.zl * 4 + place.y)
        block = jnp.where(half == 0, pair, BLOCKS - 1 - pair)
        lane = lax.broadcasted_iota(jnp.int32, (1, LANES), 1)
        within = lane
        for h in range(1, HEADS):
            within = jnp.where(lane >= h * HALF, lane - h * HALF, within)
        first = block * HALF
        self.first = first
        self.pos = within + first
        self.low = jnp.zeros_like(self.pos)
        low0 = jnp.int32(0)
        self.last_low = jnp.int32(0)
        end = jnp.int32(0)
        for d in range(DOCS - 1):
            end = end + place.facts[d]
            self.low = jnp.where(self.pos >= end, end, self.low)
            low0 = jnp.where(first >= end, end, low0)
            self.last_low = jnp.where(first + HALF - 1 >= end, end, self.last_low)
        stop = first + HALF
        self.count = lax.div(stop - low0 + (SPAN - 1), SPAN)
        self.start = stop - self.count * SPAN

    def keys(self, t):
        return pl.ds(pl.multiple_of(PAD + self.start + t * SPAN, 16), SPAN)

    def kept(self, t):
        return pl.ds(pl.multiple_of(t * SPAN, SPAN), SPAN)

    def scores(self, t, kbuf, qs):
        return dot(kbuf[self.keys(t), :], qs[...], 1, 1) * (SCALE * LOG2E)

    def masked(self, t, s):
        key = lax.broadcasted_iota(jnp.int32, (SPAN, LANES), 0) + (self.start + t * SPAN)
        return jnp.where((key >= self.low) & (key <= self.pos), s, MASKED)

    def all_allowed(self, t):
        first_key = self.start + t * SPAN
        return (first_key >= self.last_low) & (first_key + SPAN <= self.first + 1)


def heads_apart(ref, half, stack):
    row0 = pl.multiple_of(half * HALF, 16)
    for h in range(HEADS):
        stack[h * HALF : (h + 1) * HALF, :] = ref[pl.ds(row0, HALF), h * DH : (h + 1) * DH]


def forward_kernel(
    facts, q_ref, do_ref, k0, k1, k2, k3, stats, out0, out1, out2, out3,
    kbuf, dvacc, s_scr, qs, dos,
):
    place = Place(facts)
    place.gather((k0, k1, k2, k3), kbuf)
    dvacc[...] = jnp.zeros_like(dvacc)

    def one_block(half, carry):
        heads_apart(q_ref, half, qs)
        heads_apart(do_ref, half, dos)
        window = Window(place, half)

        def score(t, mass):
            def some(masked):
                s = window.scores(t, kbuf, qs)
                s = window.masked(t, s) if masked else s
                s_scr[window.kept(t), :] = s
                return mass + fold(jnp.exp2(s), jnp.sum)

            return lax.cond(window.all_allowed(t), lambda: some(False), lambda: some(True))

        mass = lax.fori_loop(0, window.count, score, jnp.zeros((8, LANES), F32))
        log_sum = jnp.log2(jnp.sum(mass, axis=0, keepdims=True))

        def spread(t, carry):
            p = jnp.exp2(s_scr[window.kept(t), :] - log_sum).astype(BF)
            dvacc[window.keys(t), :] += dot(p, dos[...], 1, 0)
            return carry

        lax.fori_loop(0, window.count, spread, 0)
        stats[half] = log_sum
        return carry

    lax.fori_loop(0, 2, one_block, 0)
    place.scatter(dvacc, (out0, out1, out2, out3), 1.0)


def backward_kernel(
    facts, q_ref, do_ref, k0, k1, k2, k3, v0, v1, v2, v3, stats,
    dq_ref, out0, out1, out2, out3,
    kbuf, vbuf, dkacc, p_scr, dp_scr, qs, dos,
):
    place = Place(facts)
    place.gather((k0, k1, k2, k3), kbuf)
    place.gather((v0, v1, v2, v3), vbuf)
    dkacc[...] = jnp.zeros_like(dkacc)

    def one_block(half, carry):
        heads_apart(q_ref, half, qs)
        heads_apart(do_ref, half, dos)
        window = Window(place, half)
        log_sum = stats[half]

        def weigh(t, moment):
            def some(masked):
                s = window.scores(t, kbuf, qs)
                s = window.masked(t, s) if masked else s
                p = jnp.exp2(s - log_sum)
                dp = dot(vbuf[window.keys(t), :], dos[...], 1, 1)
                p_scr[window.kept(t), :] = p
                dp_scr[window.kept(t), :] = dp
                return moment + fold(p * dp, jnp.sum)

            return lax.cond(window.all_allowed(t), lambda: some(False), lambda: some(True))

        moment = lax.fori_loop(0, window.count, weigh, jnp.zeros((8, LANES), F32))
        delta = jnp.sum(moment, axis=0, keepdims=True)

        def spread(t, dqt):
            g = (p_scr[window.kept(t), :] * (dp_scr[window.kept(t), :] - delta)).astype(BF)
            at = window.keys(t)
            dkacc[at, :] += dot(g, qs[...], 1, 0)
            return dqt + dot(kbuf[at, :], g, 0, 0)

        dqt = lax.fori_loop(0, window.count, spread, jnp.zeros((DH, LANES), F32))
        dq = (dqt * SCALE).T.astype(BF)
        row0 = pl.multiple_of(half * HALF, 16)
        for h in range(HEADS):
            dq_ref[pl.ds(row0, HALF), h * DH : (h + 1) * DH] = dq[h * HALF : (h + 1) * HALF, :]
        return carry

    lax.fori_loop(0, 2, one_block, 0)
    place.scatter(dkacc, (out0, out1, out2, out3), SCALE)


SHARES = (jax.ShapeDtypeStruct((4, ROWS, DH), BF),) * 4


def forward(facts, q, do, ks):
    vmem = pl.BlockSpec(memory_space=pltpu.VMEM)
    return pl.pallas_call(
        forward_kernel,
        out_shape=(jax.ShapeDtypeStruct((2, 1, LANES), F32),) + SHARES,
        in_specs=[pl.BlockSpec(memory_space=pltpu.SMEM)] + [vmem] * 6,
        out_specs=(vmem,) * 5,
        scratch_shapes=[
            pltpu.VMEM((PAD + SEQ, DH), BF),
            pltpu.VMEM((PAD + SEQ, DH), F32),
            pltpu.VMEM((STEPS * SPAN, LANES), F32),
            pltpu.VMEM((LANES, DH), BF),
            pltpu.VMEM((LANES, DH), BF),
        ],
        compiler_params=pltpu.CompilerParams(vmem_limit_bytes=32 * 2**20),
        cost_estimate=pl.CostEstimate(flops=3 * 10**9, bytes_accessed=4 * 10**6, transcendentals=2 * 10**6),
    )(facts, q, do, *ks)


def backward(facts, q, do, ks, vs, stats):
    vmem = pl.BlockSpec(memory_space=pltpu.VMEM)
    return pl.pallas_call(
        backward_kernel,
        out_shape=(jax.ShapeDtypeStruct((ROWS, HEADS * DH), BF),) + SHARES,
        in_specs=[pl.BlockSpec(memory_space=pltpu.SMEM)] + [vmem] * 11,
        out_specs=(vmem,) * 5,
        scratch_shapes=[
            pltpu.VMEM((PAD + SEQ, DH), BF),
            pltpu.VMEM((PAD + SEQ, DH), BF),
            pltpu.VMEM((PAD + SEQ, DH), F32),
            pltpu.VMEM((STEPS * SPAN, LANES), F32),
            pltpu.VMEM((STEPS * SPAN, LANES), F32),
            pltpu.VMEM((LANES, DH), BF),
            pltpu.VMEM((LANES, DH), BF),
        ],
        compiler_params=pltpu.CompilerParams(vmem_limit_bytes=32 * 2**20),
        cost_estimate=pl.CostEstimate(
            flops=5 * 10**9, bytes_accessed=5 * 10**6, transcendentals=2 * 10**6
        ),
    )(facts, q, do, *ks, *vs, stats)


def ring(shift):
    return [(i, (i + shift) % 4) for i in range(4)]


def add_up(*xs):
    return functools.reduce(lambda a, b: a + b, [x.astype(F32) for x in xs])


def copy_kernel(*refs):
    for source, target in zip(refs[: len(refs) // 2], refs[len(refs) // 2 :]):
        target[...] = source[...]


def near(*arrays):
    vmem = pl.BlockSpec(memory_space=pltpu.VMEM)
    return pl.pallas_call(
        copy_kernel,
        out_shape=tuple(jax.ShapeDtypeStruct(a.shape, a.dtype) for a in arrays),
        in_specs=[vmem] * len(arrays),
        out_specs=(vmem,) * len(arrays),
        compiler_params=pltpu.CompilerParams(vmem_limit_bytes=16 * 2**20),
    )(*arrays)


def stack_kernel(c0, c1, c2, c3, out):
    for a, ref in enumerate((c0, c1, c2, c3)):
        out[a] = ref[...]


def stacked(pieces):
    vmem = pl.BlockSpec(memory_space=pltpu.VMEM)
    return pl.pallas_call(
        stack_kernel,
        out_shape=SHARES[0],
        in_specs=[vmem] * 4,
        out_specs=vmem,
        compiler_params=pltpu.CompilerParams(vmem_limit_bytes=16 * 2**20),
    )(*pieces)


def finish_kernel(facts, *refs):
    key_parts, value_parts, (key_out, value_out, mine, sent) = refs[:4], refs[4:8], refs[8:]

    def rounded(parts):
        return functools.reduce(lambda a, b: a + b, [p[...].astype(F32) for p in parts]).astype(BF)

    key, value = rounded(key_parts), rounded(value_parts)
    key_out[...] = key
    value_out[...] = value
    key, value = key.astype(F32), value.astype(F32)
    left = lax.broadcasted_iota(jnp.int32, key.shape, 1) < DH // 2
    low = jnp.where(left, key, pltpu.roll(value, DH // 2, 1)).astype(BF)
    high = jnp.where(left, pltpu.roll(key, DH // 2, 1), value).astype(BF)
    even = lax.rem(facts[DOCS + RANKS], 2) == 0

    @pl.when(even)
    def _():
        mine[...] = low
        sent[...] = high

    @pl.when(jnp.logical_not(even))
    def _():
        mine[...] = high
        sent[...] = low


def finish(facts, key_parts, value_parts):
    vmem = pl.BlockSpec(memory_space=pltpu.VMEM)
    return pl.pallas_call(
        finish_kernel,
        out_shape=(jax.ShapeDtypeStruct((ROWS, DH), BF),) * 4,
        in_specs=[pl.BlockSpec(memory_space=pltpu.SMEM)] + [vmem] * 8,
        out_specs=(vmem,) * 4,
        compiler_params=pltpu.CompilerParams(vmem_limit_bytes=8 * 2**20),
    )(facts, *key_parts, *value_parts)


def product_kernel(
    facts, hid0, hid1, hid2, hid3, row0, row2, row1, row3, out0, out1, out2, out3, acc
):
    my_zl, my_y, my_x, core, zh = (facts[DOCS + RANKS + i] for i in range(5))
    for j, row in enumerate((row0, row1, row2, row3)):
        group = lax.rem(my_x + 4 - j, 4)

        @pl.when(group // 2 == core)
        def _():
            for c in range(4):
                columns = slice(c * 512, (c + 1) * 512)
                total = None
                for i, hidden in enumerate((hid0, hid1, hid2, hid3)):
                    part = dot(row[i * ROWS : (i + 1) * ROWS, :], hidden[:, columns], 0, 0)
                    total = part if total is None else total + part
                acc[...] = total
                side = lax.rem(lax.rem(group, 2) + my_zl // 2, 2)
                for s, out in enumerate((out0, out1, out2, out3)):
                    y = lax.rem(my_y + s, 4)
                    for kind in range(2):
                        at = pl.ds(pl.multiple_of(kind * 64 + y * 16, 16), 16)
                        out[lax.rem(kind + zh, 2), side, :, columns] = acc[at, :].astype(BF)


def weight_product(facts, *operands):
    vmem = pl.BlockSpec(memory_space=pltpu.VMEM)
    return pl.pallas_call(
        product_kernel,
        out_shape=(jax.ShapeDtypeStruct((2, 2, 16, 2048), BF),) * 4,
        in_specs=[pl.BlockSpec(memory_space=pltpu.SMEM)] + [vmem] * 8,
        out_specs=(vmem,) * 4,
        scratch_shapes=[pltpu.VMEM((DH, 512), F32)],
        compiler_params=pltpu.CompilerParams(vmem_limit_bytes=24 * 2**20),
        cost_estimate=pl.CostEstimate(flops=10**9, bytes_accessed=4 * 10**6, transcendentals=0),
    )(facts, *operands)


def after(value, *others):
    return lax.optimization_barrier((value, others))[0]


def per_device(hidden_in, queries, keys_in, values_in, out_grad, doc_lengths, pair_perm):
    zl, y, x = (lax.axis_index(a) for a in ("zl", "y", "x"))
    zh, core = lax.axis_index("zh"), lax.axis_index("co")
    swap = [(0, 1), (1, 0)]
    neighbour = [(0, 1), (1, 0), (2, 3), (3, 2)]
    facts = jnp.concatenate([doc_lengths[0], pair_perm, jnp.stack([zl, y, x, core, zh]).astype(jnp.int32)])

    def moved(value, axis, shift):
        return lax.ppermute(value, axis, ring(shift))

    ks, vs = (
        [own] + [moved(own, "zl", a) for a in (1, 2, 3)] for own in (keys_in[0], values_in[0])
    )
    rows_in = near(queries[0], out_grad[0])
    ks, vs, rows_in = lax.optimization_barrier((ks, vs, rows_in))
    ks = stacked(ks)
    ks = [ks] + [moved(ks, "y", s) for s in (1, 2, 3)]
    vs = after(stacked(vs), ks[1])
    vs = [vs] + [moved(vs if s != 2 else after(vs, *ks[2:]), "y", s) for s in (1, 2, 3)]

    def received(shares):
        return [shares[0]] + [moved(shares[s], "y", s) for s in (1, 3, 2)]

    def over_zl(got):
        parts = [add_up(*[g[a] for g in got]) for a in range(4)]
        return [parts[0]] + [moved(parts[a].astype(BF), "zl", a) for a in (1, 2, 3)]

    stats, *dvs = forward(facts, *rows_in, ks)
    dvs = received(dvs)
    hidden = hidden_in[0]
    beside = lax.ppermute(after(hidden, stats), "zl", neighbour)
    dq, *dks = backward(facts, *rows_in, ks, vs, stats)
    dks = received(after(dks, dvs[1]))
    key_grads, value_grads, mine, sent = finish(facts, over_zl(dks), over_zl(dvs))

    hidden = after((hidden, beside), *dks)
    hidden = (*hidden, *(lax.ppermute(h, "co", swap) for h in hidden))
    rows = jnp.stack([mine, lax.ppermute(sent, "zl", neighbour)])
    cross = [
        (x0 + 4 * c, x0 + 4 * (1 - c)) for c in range(2) for x0 in range(4) if x0 // 2 == 1 - c
    ]
    rows = jnp.stack([rows, lax.ppermute(rows, ("co", "x"), cross)]).reshape(4 * ROWS, DH)

    def along(j):
        return [
            (x0 + 4 * c, (x0 + j) % 4 + 4 * c) for c in range(2) for x0 in range(4) if x0 // 2 == c
        ]

    rows = [rows] + [lax.ppermute(rows, ("co", "x"), along(j)) for j in (1, 2, 3)]
    shares = received(weight_product(facts, *hidden, rows[0], rows[2], rows[1], rows[3]))
    total = add_up(*shares)
    other_zl = [(0, 2), (2, 0), (1, 3), (3, 1)]
    both = [(a + 4 * c, b + 4 * (1 - c)) for a, b in other_zl for c in range(2)]
    grad_weight = add_up(
        total[0, 0],
        lax.ppermute(total[1, 0].astype(BF), "zh", swap),
        lax.ppermute(total[1, 1].astype(BF), ("zh", "zl"), both),
        lax.ppermute(total[0, 1].astype(BF), "zl", other_zl),
    )
    return dq[None], key_grads[None], value_grads[None], grad_weight


def solution(mesh):
    fine = Mesh(mesh.devices.reshape(SIZES), CARDINAL)
    dp, ctx, tp = ("zh", "co"), ("zl", "y"), "x"
    tokens = P(dp, ctx, tp)
    return jax.shard_map(
        per_device,
        mesh=fine,
        in_specs=(tokens,) * 5 + (P(dp, None), P()),
        out_specs=(tokens,) * 3 + (P(dp + ctx, tp),),
        check_vma=False,
    )
```

```python
import functools

import jax
import jax.numpy as jnp
import numpy as np
from jax import lax
from jax.experimental import pallas as pl
from jax.experimental.pallas import tpu as pltpu
from jax.sharding import Mesh, PartitionSpec as P

DH = 128
HEADS = 8
HALF = 112
ROWS = 2 * HALF
LANES = HEADS * HALF
RANKS = 16
BLOCKS = 2 * RANKS
SEQ = ROWS * RANKS
DOCS = 6
MAX_DOC = 1194
SPAN = 2 * HALF
STEPS = -(-(MAX_DOC - 1 + HALF) // SPAN)
PAD = SPAN
SCALE = DH**-0.5
LOG2E = 1.4426950408889634
MASKED = -1e30
CARDINAL = ("zh", "co", "zl", "y", "x")
SIZES = (2, 2, 4, 4, 4)
BF = jnp.bfloat16
F32 = jnp.float32


def dot(a, b, ca, cb):
    return lax.dot_general(a, b, (((ca,), (cb,)), ((), ())), preferred_element_type=F32)


def fold(x, op):
    return op(x.reshape(x.shape[0] // 8, 8, x.shape[1]), axis=0)


class Place:
    def __init__(self, facts):
        self.facts = facts
        self.zl, self.y = facts[DOCS + RANKS], facts[DOCS + RANKS + 1]

    def pair(self, rank):
        return self.facts[DOCS + rank]

    def rows(self, zl, y, half):
        pair = self.pair(zl * 4 + y)
        block = pair if half == 0 else BLOCKS - 1 - pair
        return pl.ds(pl.multiple_of(PAD + block * HALF, 16), HALF)

    def gather(self, refs, buf):
        buf[0:PAD, :] = jnp.zeros((PAD, DH), BF)
        for s, ref in enumerate(refs):
            for a in range(4):
                zl, y = lax.rem(self.zl + 4 - a, 4), lax.rem(self.y + 4 - s, 4)
                for half in range(2):
                    rows = slice(half * HALF, (half + 1) * HALF)
                    buf[self.rows(zl, y, half), :] = ref[a, rows, :]

    def scatter(self, acc, refs, scale):
        for s, ref in enumerate(refs):
            for a in range(4):
                zl, y = lax.rem(self.zl + a, 4), lax.rem(self.y + s, 4)
                for half in range(2):
                    rows = slice(half * HALF, (half + 1) * HALF)
                    ref[a, rows, :] = (acc[self.rows(zl, y, half), :] * scale).astype(BF)


class Window:
    def __init__(self, place, half):
        pair = place.pair(place.zl * 4 + place.y)
        block = jnp.where(half == 0, pair, BLOCKS - 1 - pair)
        lane = lax.broadcasted_iota(jnp.int32, (1, LANES), 1)
        within = lane
        for h in range(1, HEADS):
            within = jnp.where(lane >= h * HALF, lane - h * HALF, within)
        first = block * HALF
        self.first = first
        self.pos = within + first
        self.low = jnp.zeros_like(self.pos)
        low0 = jnp.int32(0)
        self.last_low = jnp.int32(0)
        end = jnp.int32(0)
        for d in range(DOCS - 1):
            end = end + place.facts[d]
            self.low = jnp.where(self.pos >= end, end, self.low)
            low0 = jnp.where(first >= end, end, low0)
            self.last_low = jnp.where(first + HALF - 1 >= end, end, self.last_low)
        stop = first + HALF
        self.count = lax.div(stop - low0 + (SPAN - 1), SPAN)
        self.start = stop - self.count * SPAN

    def keys(self, t):
        return pl.ds(pl.multiple_of(PAD + self.start + t * SPAN, 16), SPAN)

    def kept(self, t):
        return pl.ds(pl.multiple_of(t * SPAN, SPAN), SPAN)

    def scores(self, t, kbuf, qs):
        return dot(kbuf[self.keys(t), :], qs[...], 1, 1) * (SCALE * LOG2E)

    def masked(self, t, s):
        key = lax.broadcasted_iota(jnp.int32, (SPAN, LANES), 0) + (self.start + t * SPAN)
        return jnp.where((key >= self.low) & (key <= self.pos), s, MASKED)

    def all_allowed(self, t):
        first_key = self.start + t * SPAN
        return (first_key >= self.last_low) & (first_key + SPAN <= self.first + 1)


def heads_apart(ref, half, stack):
    row0 = pl.multiple_of(half * HALF, 16)
    for h in range(HEADS):
        stack[h * HALF : (h + 1) * HALF, :] = ref[pl.ds(row0, HALF), h * DH : (h + 1) * DH]


def forward_kernel(
    facts, q_ref, do_ref, k0, k1, k2, k3, stats, out0, out1, out2, out3,
    kbuf, dvacc, s_scr, qs, dos,
):
    place = Place(facts)
    place.gather((k0, k1, k2, k3), kbuf)
    dvacc[...] = jnp.zeros_like(dvacc)

    def one_block(half, carry):
        heads_apart(q_ref, half, qs)
        heads_apart(do_ref, half, dos)
        window = Window(place, half)

        def score(t, mass):
            def some(masked):
                s = window.scores(t, kbuf, qs)
                s = window.masked(t, s) if masked else s
                s_scr[window.kept(t), :] = s
                return mass + fold(jnp.exp2(s), jnp.sum)

            return lax.cond(window.all_allowed(t), lambda: some(False), lambda: some(True))

        mass = lax.fori_loop(0, window.count, score, jnp.zeros((8, LANES), F32))
        log_sum = jnp.log2(jnp.sum(mass, axis=0, keepdims=True))

        def spread(t, carry):
            p = jnp.exp2(s_scr[window.kept(t), :] - log_sum).astype(BF)
            dvacc[window.keys(t), :] += dot(p, dos[...], 1, 0)
            return carry

        lax.fori_loop(0, window.count, spread, 0)
        stats[half] = log_sum
        return carry

    lax.fori_loop(0, 2, one_block, 0)
    place.scatter(dvacc, (out0, out1, out2, out3), 1.0)


def backward_kernel(
    facts, q_ref, do_ref, k0, k1, k2, k3, v0, v1, v2, v3, stats,
    dq_ref, out0, out1, out2, out3,
    kbuf, vbuf, dkacc, p_scr, dp_scr, qs, dos,
):
    place = Place(facts)
    place.gather((k0, k1, k2, k3), kbuf)
    place.gather((v0, v1, v2, v3), vbuf)
    dkacc[...] = jnp.zeros_like(dkacc)

    def one_block(half, carry):
        heads_apart(q_ref, half, qs)
        heads_apart(do_ref, half, dos)
        window = Window(place, half)
        log_sum = stats[half]

        def weigh(t, moment):
            def some(masked):
                s = window.scores(t, kbuf, qs)
                s = window.masked(t, s) if masked else s
                p = jnp.exp2(s - log_sum)
                dp = dot(vbuf[window.keys(t), :], dos[...], 1, 1)
                p_scr[window.kept(t), :] = p
                dp_scr[window.kept(t), :] = dp
                return moment + fold(p * dp, jnp.sum)

            return lax.cond(window.all_allowed(t), lambda: some(False), lambda: some(True))

        moment = lax.fori_loop(0, window.count, weigh, jnp.zeros((8, LANES), F32))
        delta = jnp.sum(moment, axis=0, keepdims=True)

        def spread(t, dqt):
            g = (p_scr[window.kept(t), :] * (dp_scr[window.kept(t), :] - delta)).astype(BF)
            at = window.keys(t)
            dkacc[at, :] += dot(g, qs[...], 1, 0)
            return dqt + dot(kbuf[at, :], g, 0, 0)

        dqt = lax.fori_loop(0, window.count, spread, jnp.zeros((DH, LANES), F32))
        dq = (dqt * SCALE).T.astype(BF)
        row0 = pl.multiple_of(half * HALF, 16)
        for h in range(HEADS):
            dq_ref[pl.ds(row0, HALF), h * DH : (h + 1) * DH] = dq[h * HALF : (h + 1) * HALF, :]
        return carry

    lax.fori_loop(0, 2, one_block, 0)
    place.scatter(dkacc, (out0, out1, out2, out3), SCALE)


SHARES = (jax.ShapeDtypeStruct((4, ROWS, DH), BF),) * 4


def forward(facts, q, do, ks):
    vmem = pl.BlockSpec(memory_space=pltpu.VMEM)
    return pl.pallas_call(
        forward_kernel,
        out_shape=(jax.ShapeDtypeStruct((2, 1, LANES), F32),) + SHARES,
        in_specs=[pl.BlockSpec(memory_space=pltpu.SMEM)] + [vmem] * 6,
        out_specs=(vmem,) * 5,
        scratch_shapes=[
            pltpu.VMEM((PAD + SEQ, DH), BF),
            pltpu.VMEM((PAD + SEQ, DH), F32),
            pltpu.VMEM((STEPS * SPAN, LANES), F32),
            pltpu.VMEM((LANES, DH), BF),
            pltpu.VMEM((LANES, DH), BF),
        ],
        compiler_params=pltpu.CompilerParams(vmem_limit_bytes=32 * 2**20),
        cost_estimate=pl.CostEstimate(flops=3 * 10**9, bytes_accessed=4 * 10**6, transcendentals=2 * 10**6),
    )(facts, q, do, *ks)


def backward(facts, q, do, ks, vs, stats):
    vmem = pl.BlockSpec(memory_space=pltpu.VMEM)
    return pl.pallas_call(
        backward_kernel,
        out_shape=(jax.ShapeDtypeStruct((ROWS, HEADS * DH), BF),) + SHARES,
        in_specs=[pl.BlockSpec(memory_space=pltpu.SMEM)] + [vmem] * 11,
        out_specs=(vmem,) * 5,
        scratch_shapes=[
            pltpu.VMEM((PAD + SEQ, DH), BF),
            pltpu.VMEM((PAD + SEQ, DH), BF),
            pltpu.VMEM((PAD + SEQ, DH), F32),
            pltpu.VMEM((STEPS * SPAN, LANES), F32),
            pltpu.VMEM((STEPS * SPAN, LANES), F32),
            pltpu.VMEM((LANES, DH), BF),
            pltpu.VMEM((LANES, DH), BF),
        ],
        compiler_params=pltpu.CompilerParams(vmem_limit_bytes=32 * 2**20),
        cost_estimate=pl.CostEstimate(
            flops=5 * 10**9, bytes_accessed=5 * 10**6, transcendentals=2 * 10**6
        ),
    )(facts, q, do, *ks, *vs, stats)


def ring(shift):
    return [(i, (i + shift) % 4) for i in range(4)]


def add_up(*xs):
    return functools.reduce(lambda a, b: a + b, [x.astype(F32) for x in xs])


def copy_kernel(*refs):
    for source, target in zip(refs[: len(refs) // 2], refs[len(refs) // 2 :]):
        target[...] = source[...]


def near(*arrays):
    vmem = pl.BlockSpec(memory_space=pltpu.VMEM)
    return pl.pallas_call(
        copy_kernel,
        out_shape=tuple(jax.ShapeDtypeStruct(a.shape, a.dtype) for a in arrays),
        in_specs=[vmem] * len(arrays),
        out_specs=(vmem,) * len(arrays),
        compiler_params=pltpu.CompilerParams(vmem_limit_bytes=16 * 2**20),
    )(*arrays)


def stack_kernel(c0, c2, c1, c3, out):
    for a, ref in enumerate((c0, c1, c2, c3)):
        out[a] = ref[...]


def stacked(pieces):
    vmem = pl.BlockSpec(memory_space=pltpu.VMEM)
    return pl.pallas_call(
        stack_kernel,
        out_shape=SHARES[0],
        in_specs=[vmem] * 4,
        out_specs=vmem,
        compiler_params=pltpu.CompilerParams(vmem_limit_bytes=16 * 2**20),
    )(pieces[0], pieces[2], pieces[1], pieces[3])


def finish_kernel(facts, *refs):
    key_parts, value_parts, (key_out, value_out, mine, sent) = refs[:4], refs[4:8], refs[8:]

    def rounded(parts):
        return functools.reduce(lambda a, b: a + b, [p[...].astype(F32) for p in parts]).astype(BF)

    key, value = rounded(key_parts), rounded(value_parts)
    key_out[...] = key
    value_out[...] = value
    key, value = key.astype(F32), value.astype(F32)
    left = lax.broadcasted_iota(jnp.int32, key.shape, 1) < DH // 2
    low = jnp.where(left, key, pltpu.roll(value, DH // 2, 1)).astype(BF)
    high = jnp.where(left, pltpu.roll(key, DH // 2, 1), value).astype(BF)
    even = lax.rem(facts[DOCS + RANKS], 2) == 0

    @pl.when(even)
    def _():
        mine[...] = low
        sent[...] = high

    @pl.when(jnp.logical_not(even))
    def _():
        mine[...] = high
        sent[...] = low


def finish(facts, key_parts, value_parts):
    vmem = pl.BlockSpec(memory_space=pltpu.VMEM)
    return pl.pallas_call(
        finish_kernel,
        out_shape=(jax.ShapeDtypeStruct((ROWS, DH), BF),) * 4,
        in_specs=[pl.BlockSpec(memory_space=pltpu.SMEM)] + [vmem] * 8,
        out_specs=(vmem,) * 4,
        compiler_params=pltpu.CompilerParams(vmem_limit_bytes=8 * 2**20),
    )(facts, *key_parts, *value_parts)


def product_kernel(
    facts, hid0, hid1, hid2, hid3, row0, row2, row1, row3, out0, out1, out2, out3, acc
):
    my_zl, my_y, my_x, core, zh = (facts[DOCS + RANKS + i] for i in range(5))
    for j, row in enumerate((row0, row1, row2, row3)):
        group = lax.rem(my_x + 4 - j, 4)

        @pl.when(group // 2 == core)
        def _():
            for c in range(4):
                columns = slice(c * 512, (c + 1) * 512)
                total = None
                for i, hidden in enumerate((hid0, hid1, hid2, hid3)):
                    part = dot(row[i * ROWS : (i + 1) * ROWS, :], hidden[:, columns], 0, 0)
                    total = part if total is None else total + part
                acc[...] = total
                side = lax.rem(lax.rem(group, 2) + my_zl // 2, 2)
                for s, out in enumerate((out0, out1, out2, out3)):
                    y = lax.rem(my_y + s, 4)
                    for kind in range(2):
                        at = pl.ds(pl.multiple_of(kind * 64 + y * 16, 16), 16)
                        out[lax.rem(kind + zh, 2), side, :, columns] = acc[at, :].astype(BF)


def weight_product(facts, *operands):
    vmem = pl.BlockSpec(memory_space=pltpu.VMEM)
    return pl.pallas_call(
        product_kernel,
        out_shape=(jax.ShapeDtypeStruct((2, 2, 16, 2048), BF),) * 4,
        in_specs=[pl.BlockSpec(memory_space=pltpu.SMEM)] + [vmem] * 8,
        out_specs=(vmem,) * 4,
        scratch_shapes=[pltpu.VMEM((DH, 512), F32)],
        compiler_params=pltpu.CompilerParams(vmem_limit_bytes=24 * 2**20),
        cost_estimate=pl.CostEstimate(flops=10**9, bytes_accessed=4 * 10**6, transcendentals=0),
    )(facts, *operands)


def after(value, *others):
    return lax.optimization_barrier((value, others))[0]


def per_device(hidden_in, queries, keys_in, values_in, out_grad, doc_lengths, pair_perm):
    zl, y, x = (lax.axis_index(a) for a in ("zl", "y", "x"))
    zh, core = lax.axis_index("zh"), lax.axis_index("co")
    swap = [(0, 1), (1, 0)]
    neighbour = [(0, 1), (1, 0), (2, 3), (3, 2)]
    facts = jnp.concatenate([doc_lengths[0], pair_perm, jnp.stack([zl, y, x, core, zh]).astype(jnp.int32)])

    def moved(value, axis, shift):
        return lax.ppermute(value, axis, ring(shift))

    ks, vs = (
        [own] + [moved(own, "zl", a) for a in (1, 2, 3)] for own in (keys_in[0], values_in[0])
    )
    rows_in = near(queries[0], out_grad[0])
    ks, vs, rows_in = lax.optimization_barrier((ks, vs, rows_in))
    ks = stacked(ks)
    ks = [ks] + [moved(ks, "y", s) for s in (1, 2, 3)]
    vs = after(stacked(vs), ks[1])
    vs = [vs] + [moved(vs if s != 2 else after(vs, *ks[2:]), "y", s) for s in (1, 2, 3)]

    def received(shares):
        return [shares[0]] + [moved(shares[s], "y", s) for s in (1, 3, 2)]

    def over_zl(got):
        parts = [add_up(*[g[a] for g in got]) for a in range(4)]
        return [parts[0]] + [moved(parts[a].astype(BF), "zl", a) for a in (2, 1, 3)]

    stats, *dvs = forward(facts, *rows_in, ks)
    dvs = received(dvs)
    hidden = hidden_in[0]
    beside = lax.ppermute(after(hidden, stats), "zl", neighbour)
    dq, *dks = backward(facts, *rows_in, ks, vs, stats)
    dks = received(after(dks, dvs[1]))
    key_grads, value_grads, mine, sent = finish(facts, over_zl(dks), over_zl(dvs))

    hidden = after((hidden, beside), *dks)
    hidden = (*hidden, *(lax.ppermute(h, "co", swap) for h in hidden))
    rows = jnp.stack([mine, lax.ppermute(sent, "zl", neighbour)])
    cross = [
        (x0 + 4 * c, x0 + 4 * (1 - c)) for c in range(2) for x0 in range(4) if x0 // 2 == 1 - c
    ]
    rows = jnp.stack([rows, lax.ppermute(rows, ("co", "x"), cross)]).reshape(4 * ROWS, DH)

    def along(j):
        return [
            (x0 + 4 * c, (x0 + j) % 4 + 4 * c) for c in range(2) for x0 in range(4) if x0 // 2 == c
        ]

    rows = [rows] + [lax.ppermute(rows, ("co", "x"), along(j)) for j in (1, 2, 3)]
    shares = received(weight_product(facts, *hidden, rows[0], rows[2], rows[1], rows[3]))
    total = add_up(*shares)
    other_zl = [(0, 2), (2, 0), (1, 3), (3, 1)]
    both = [(a + 4 * c, b + 4 * (1 - c)) for a, b in other_zl for c in range(2)]
    grad_weight = add_up(
        total[0, 0],
        lax.ppermute(total[1, 0].astype(BF), "zh", swap),
        lax.ppermute(total[1, 1].astype(BF), ("zh", "zl"), both),
        lax.ppermute(total[0, 1].astype(BF), "zl", other_zl),
    )
    return dq[None], key_grads[None], value_grads[None], grad_weight


def solution(mesh):
    fine = Mesh(mesh.devices.reshape(SIZES), CARDINAL)
    dp, ctx, tp = ("zh", "co"), ("zl", "y"), "x"
    tokens = P(dp, ctx, tp)
    return jax.shard_map(
        per_device,
        mesh=fine,
        in_specs=(tokens,) * 5 + (P(dp, None), P()),
        out_specs=(tokens,) * 3 + (P(dp + ctx, tp),),
        check_vma=False,
    )
```
